32 devices in a mesh: dp: 4 (over z), mp: 8 (over y, x, core).
Axes of the slice: x: 2, y: 2, z: 4, core: 2. Of those that a mesh axis runs over, the one named last changes fastest.
Arguments:
- inputs: bfloat16 [4096, 2048], P(('dp', 'mp')), may hold values from -6 to 6
- segments: int32 [4, 1024], P('dp'), may hold values from 0 to 2, as said below
- cotangent: bfloat16 [4096, 2048], P(('dp', 'mp')), may hold values from -7.2 to 7.2
- triple_weight: float32 [3, 2048, 2048], P(None, 'dp', 'mp'), may hold values from -0.09375 to 0.09375
- output_weight: float32 [2048, 2048], P('mp', 'dp'), may hold values from -1 to 1
- gate_weight: float32 [2, 2048, 5632], P(None, 'dp', 'mp'), may hold values from -0.125 to 0.125
- down_weight: float32 [5632, 2048], P('mp', 'dp'), may hold values from -0.078125 to 0.078125
- vector_params: float32 [7, 2048], replicated, may hold values from -1.5 to 3.75
- triple_moment: float32 [3, 2048, 2048], P(None, 'dp', 'mp'), may hold values from -9.1552734e-05 to 9.1552734e-05
- output_moment: float32 [2048, 2048], P('mp', 'dp'), may hold values from -2.2888184e-05 to 2.2888184e-05
- gate_moment: float32 [2, 2048, 5632], P(None, 'dp', 'mp'), may hold values from -9.1552734e-05 to 9.1552734e-05
- down_moment: float32 [5632, 2048], P('mp', 'dp'), may hold values from -9.1552734e-05 to 9.1552734e-05
- vector_moment: float32 [7, 2048], replicated, may hold values from -0.00024414062 to 0.00024414062
- triple_square: float32 [3, 2048, 2048], P(None, 'dp', 'mp'), may hold values from 1.0312375e-09 to 4.0860355e-09
- output_square: float32 [2048, 2048], P('mp', 'dp'), may hold values from 6.420913e-11 to 2.5294505e-10
- gate_square: float32 [2, 2048, 5632], P(None, 'dp', 'mp'), may hold values from 1.0312375e-09 to 4.0860355e-09
- down_square: float32 [5632, 2048], P('mp', 'dp'), may hold values from 1.0312375e-09 to 4.0860355e-09
- vector_square: float32 [7, 2048], replicated, may hold values from 9.144936e-09 to 3.6968892e-08
Outputs:
- block_output: bfloat16 [4096, 2048], P(('dp', 'mp'))
- input_grad: float32 [4096, 2048], P(('dp', 'mp'))
- grad_norm: float32 [], replicated
- triple_updated: float32 [3, 2048, 2048], P(None, 'dp', 'mp')
- output_updated: float32 [2048, 2048], P('mp', 'dp')
- gate_updated: float32 [2, 2048, 5632], P(None, 'dp', 'mp')
- down_updated: float32 [5632, 2048], P('mp', 'dp')
- vector_updated: float32 [7, 2048], replicated
- triple_first: float32 [3, 2048, 2048], P(None, 'dp', 'mp')
- output_first: float32 [2048, 2048], P('mp', 'dp')
- gate_first: float32 [2, 2048, 5632], P(None, 'dp', 'mp')
- down_first: float32 [5632, 2048], P('mp', 'dp')
- vector_first: float32 [7, 2048], replicated
- triple_second: float32 [3, 2048, 2048], P(None, 'dp', 'mp')
- output_second: float32 [2048, 2048], P('mp', 'dp')
- gate_second: float32 [2, 2048, 5632], P(None, 'dp', 'mp')
- down_second: float32 [5632, 2048], P('mp', 'dp')
- vector_second: float32 [7, 2048], replicated
- query_bias_grad: float32 [2048], replicated
The draws below stay inside these ranges and needn't reach their ends.
Inputs may be any that keep to these rules, and one draw needn't show every extreme that they name: `segments`: each row holds three documents numbered 0, 1, 2 in order; documents 0 and 2 are each shorter than 128 tokens.
All inputs are finite; a program needn't handle non-finite values.
Results may differ from the reference program's by a relative error of at most 0.028.
Values may be sent and summed in bfloat16 or wider, within the bound.
No kernel may reach another device: no remote copies, remote signals or barrier semaphores. Data moves between devices by JAX's collectives and lax.ppermute only.
A program may use at most 192 MiB of HBM per device.

```python
import math
import jax
import jax.numpy as jnp
from jax import lax

MODEL_WIDTH = 2048
HEAD_COUNT = 32
FF = 5632
HEAD_SIZE = 64
ROTARY = 16
DEVICE_TOKENS = 128
STEP = 5
PACKED_ROWS = 4
ROW_LENGTH = 1024
TOKEN_TOTAL = 4096
PARAMS = 51394560


def draw_segments(key, part):
    key = jax.random.fold_in(key, 11)
    key_front, key_backward = jax.random.split(key)
    front_end = jax.random.randint(key_front, (PACKED_ROWS, 1), 1, DEVICE_TOKENS)
    backward_begin = jax.random.randint(key_backward, (PACKED_ROWS, 1), ROW_LENGTH - DEVICE_TOKENS + 1, ROW_LENGTH)
    loop_counter = jnp.arange(ROW_LENGTH, dtype=jnp.int32)[None, :]
    return (loop_counter >= front_end).astype(jnp.int32) + (loop_counter >= backward_begin).astype(jnp.int32)


def draw_vector_params(key, part):
    key = jax.random.fold_in(key, 23)
    key_jitter, key_offset, key_bias = jax.random.split(key, 3)
    ramp = jnp.arange(MODEL_WIDTH, dtype=jnp.float32) / (MODEL_WIDTH - 1)
    jitter = jnp.exp(jax.random.uniform(key_jitter, (2, MODEL_WIDTH), jnp.float32, -0.2, 0.2))
    gains = (0.8 + 1.6 * ramp)[None, :] * jitter
    offsets = jnp.clip(0.2 * jax.random.normal(key_offset, (2, MODEL_WIDTH), jnp.float32), -1.0, 1.0)
    biases = jnp.clip(0.3 * jax.random.normal(key_bias, (3, MODEL_WIDTH), jnp.float32), -1.5, 1.5)
    return jnp.concatenate([gains[0:1], offsets[0:1], gains[1:2], offsets[1:2], biases], axis=0)


def draw_cotangent(key, part):
    key = jax.random.fold_in(key, 37)
    where_positions = (jnp.arange(TOKEN_TOTAL, dtype=jnp.int32) % ROW_LENGTH).astype(jnp.float32) / ROW_LENGTH
    rise = 0.6 + 1.2 * where_positions
    noise = jnp.clip(jax.random.normal(key, (TOKEN_TOTAL, MODEL_WIDTH), jnp.float32), -4.0, 4.0)
    return (rise[:, None] * noise).astype(jnp.bfloat16)


def levels(stream_key, dims, shards, smallest, high):
    def one(dim, blocks):
        draws = jax.random.uniform(jax.random.fold_in(jax.random.fold_in(stream_key, 6), dim), (blocks,), jnp.float32, smallest / len(shards), high / len(shards))
        return jnp.repeat(jnp.exp(draws), dims[dim] // blocks).reshape((-1,) + (1,) * (len(dims) - dim - 1))

    gain = one(*shards[0])
    for cut in shards[1:]:
        gain = gain * one(*cut)
    return gain


def normal_values(key, dims, scale, most, pieces=(), kind=jnp.bfloat16):
    array = jax.random.normal(key, dims, jnp.float32) * scale
    if len(pieces) > 0:
        array = levels(key, dims, pieces, -0.22, 0.18) * array
    return jnp.clip(array, min=-most, max=most).astype(kind)


def setup_inputs(seed: int = 0) -> dict:
    key_list = jax.random.split(jax.random.key(seed), 19)
    inputs = normal_values(key_list[0], (TOKEN_TOTAL, MODEL_WIDTH), 1.0, 6.0, ((0, 32),))
    segments = draw_segments(jax.random.fold_in(key_list[18], 71), 0)
    cotangent = draw_cotangent(jax.random.fold_in(key_list[18], 71), 0)
    triple_weight = normal_values(key_list[3], (3, MODEL_WIDTH, MODEL_WIDTH), (2 * MODEL_WIDTH) ** -0.5, 0.09375, ((1, 4), (2, 8)), jnp.float32)
    output_weight = normal_values(key_list[4], (MODEL_WIDTH, MODEL_WIDTH), (MODEL_WIDTH // 64) ** -0.5, 1.0, ((0, 8), (1, 4)), jnp.float32)
    gate_weight = normal_values(key_list[5], (2, MODEL_WIDTH, FF), MODEL_WIDTH ** -0.5, 0.125, ((1, 4), (2, 8)), jnp.float32)
    down_weight = normal_values(key_list[6], (FF, MODEL_WIDTH), FF ** -0.5, 0.078125, ((0, 8), (1, 4)), jnp.float32)
    vector_params = draw_vector_params(jax.random.fold_in(key_list[18], 71), 0)
    triple_moment = normal_values(key_list[8], (3, MODEL_WIDTH, MODEL_WIDTH), (0.11 * PARAMS ** -0.5), 9.1552734375e-05, ((1, 4), (2, 8)), jnp.float32)
    output_moment = normal_values(key_list[9], (MODEL_WIDTH, MODEL_WIDTH), (0.028 * PARAMS ** -0.5), 2.288818359375e-05, ((0, 8), (1, 4)), jnp.float32)
    gate_moment = normal_values(key_list[10], (2, MODEL_WIDTH, FF), (0.11 * PARAMS ** -0.5), 9.1552734375e-05, ((1, 4), (2, 8)), jnp.float32)
    down_moment = normal_values(key_list[11], (FF, MODEL_WIDTH), (0.11 * PARAMS ** -0.5), 9.1552734375e-05, ((0, 8), (1, 4)), jnp.float32)
    vector_moment = normal_values(key_list[12], (7, MODEL_WIDTH), (0.33 * PARAMS ** -0.5), 0.00024414062, (), jnp.float32)
    triple_square = jnp.clip(jnp.exp(math.log(4.086035509942576e-09) - 1.3768156 * jax.random.uniform(key_list[13], (3, MODEL_WIDTH, MODEL_WIDTH), jnp.float32) ** levels(key_list[13], (3, MODEL_WIDTH, MODEL_WIDTH), ((1, 4), (2, 8)), -0.2, 0.2)), 1.0312375398058293e-09, 4.086035509942576e-09)
    output_square = jnp.clip(jnp.exp(math.log(2.5294505379136467e-10) - 1.3710269 * jax.random.uniform(key_list[14], (MODEL_WIDTH, MODEL_WIDTH), jnp.float32) ** levels(key_list[14], (MODEL_WIDTH, MODEL_WIDTH), ((0, 8), (1, 4)), -0.2, 0.2)), 6.420913106763848e-11, 2.5294505379136467e-10)
    gate_square = jnp.clip(jnp.exp(math.log(4.086035509942576e-09) - 1.3768156 * jax.random.uniform(key_list[15], (2, MODEL_WIDTH, FF), jnp.float32) ** levels(key_list[15], (2, MODEL_WIDTH, FF), ((1, 4), (2, 8)), -0.2, 0.2)), 1.0312375398058293e-09, 4.086035509942576e-09)
    down_square = jnp.clip(jnp.exp(math.log(4.086035509942576e-09) - 1.3768156 * jax.random.uniform(key_list[16], (FF, MODEL_WIDTH), jnp.float32) ** levels(key_list[16], (FF, MODEL_WIDTH), ((0, 8), (1, 4)), -0.2, 0.2)), 1.0312375398058293e-09, 4.086035509942576e-09)
    vector_square = jnp.clip(jnp.exp(jax.random.uniform(key_list[17], (7, MODEL_WIDTH), jnp.float32, math.log(9.144936363725265e-09), math.log(3.696889194770847e-08))), 9.144936363725265e-09, 3.696889194770847e-08)
    return dict(inputs=inputs, segments=segments, cotangent=cotangent, triple_weight=triple_weight, output_weight=output_weight, gate_weight=gate_weight, down_weight=down_weight, vector_params=vector_params, triple_moment=triple_moment, output_moment=output_moment, gate_moment=gate_moment, down_moment=down_moment, vector_moment=vector_moment, triple_square=triple_square, output_square=output_square, gate_square=gate_square, down_square=down_square, vector_square=vector_square)


norm_eps = 1e-05
rotary_base = 10000.0
clip_limit = 1.0
first_decay = 0.9
second_decay = 0.95
adam_eps = 1e-08
matrix_rate = 0.03
output_rate = 0.2
vector_rate = 0.5
weight_decay = 0.1
masked_score = -1e+30
highest = lax.Precision.HIGHEST

@jax.custom_vjp
def low(v):
    return lax.optimization_barrier(v.astype(jnp.bfloat16)).astype(jnp.float32)

@jax.custom_vjp
def low_back(v):
    return v

def low_keep(v):
    return (low(v), None)

def low_pass(kept, grad):
    return (grad,)

def back_keep(v):
    return (v, None)

def back_low(kept, grad):
    return (low(grad),)
low.defvjp(low_keep, low_pass)
low_back.defvjp(back_keep, back_low)

def layer_norm(values, gain_row, offset_row):
    center = values - lax.optimization_barrier(jnp.mean(values, axis=-1, keepdims=True))
    spread = lax.optimization_barrier(jnp.mean(center * center, axis=-1, keepdims=True))
    return center * lax.rsqrt(spread + norm_eps) * gain_row + offset_row

def positions_of(row_segments):
    length = row_segments.shape[0]
    loop_counter = jnp.arange(length, dtype=jnp.int32)
    earlier = jnp.concatenate([jnp.full((1,), -1, jnp.int32), row_segments[:-1]])
    starts = jnp.where(row_segments != earlier, loop_counter, jnp.zeros_like(loop_counter))
    return loop_counter - lax.cummax(starts, axis=0)

def rotary_tables(positions, rotary):
    half_width = rotary // 2
    frequency = rotary_base ** (-2.0 * jnp.arange(half_width, dtype=jnp.float32) / rotary)
    angles = positions.astype(jnp.float32)[:, None] * frequency[None, :]
    return (jnp.cos(angles), jnp.sin(angles))

def rotate(values, cosine_table, sine_table, rotary):
    half_width = rotary // 2
    first_part = values[..., :half_width]
    second_part = values[..., half_width:rotary]
    cosine_wide = cosine_table[:, None, :]
    sine_wide = sine_table[:, None, :]
    return jnp.concatenate([first_part * cosine_wide - second_part * sine_wide, second_part * cosine_wide + first_part * sine_wide, values[..., rotary:]], axis=-1)

def attention(queries, keys_all, values_all, row_segments):
    rows_per_block = min(512, ROW_LENGTH)
    block_number = ROW_LENGTH // rows_per_block
    loop_counter = jnp.arange(ROW_LENGTH, dtype=jnp.int32)
    score_scale = HEAD_SIZE ** (-0.5)

    def one_block(block):
        query_block, segment_block, step_block = block
        scores = jnp.einsum('qhd,khd->hqk', query_block, keys_all, precision=highest) * score_scale
        scores = low_back(scores)
        allowed = (segment_block[:, None] == row_segments[None, :]) & (loop_counter[None, :] <= step_block[:, None])
        soft = jax.nn.softmax(jnp.where(allowed[None], scores, masked_score), axis=-1)
        return jnp.einsum('hqk,khd->qhd', low(soft), values_all, precision=highest)
    mixed_rows = lax.map(jax.checkpoint(one_block), (queries.reshape(block_number, rows_per_block, HEAD_COUNT, HEAD_SIZE), row_segments.reshape(block_number, rows_per_block), loop_counter.reshape(block_number, rows_per_block)))
    return mixed_rows.reshape(ROW_LENGTH, MODEL_WIDTH)

def layer_rows(source_rows, triple_low, output_low, gate_low, down_low, params, segments):

    def single_row(row):
        row_source, row_segments = row
        normed_one = low(layer_norm(row_source, params[0], params[1]))
        projected_rows = jnp.einsum('sd,pde->pse', normed_one, triple_low, precision=highest) + params[4:7][:, None, :]
        projected_rows = low_back(projected_rows)
        reshaped_array = projected_rows.reshape(3, ROW_LENGTH, HEAD_COUNT, HEAD_SIZE)
        cosine_table, sine_table = rotary_tables(positions_of(row_segments), ROTARY)
        queries = low(rotate(reshaped_array[0], cosine_table, sine_table, ROTARY))
        keys_all = low(rotate(reshaped_array[1], cosine_table, sine_table, ROTARY))
        values_all = low(reshaped_array[2])
        mixed_rows = low_back(low(attention(queries, keys_all, values_all, row_segments)))
        hidden = row_source + low_back(jnp.dot(mixed_rows, output_low, precision=highest))
        normed_two = low(layer_norm(hidden, params[2], params[3]))
        gate_up = low_back(jnp.einsum('sd,pdf->psf', normed_two, gate_low, precision=highest))
        activated = low(jax.nn.silu(gate_up[0]) * gate_up[1])
        return hidden + low_back(jnp.dot(activated, down_low, precision=highest))
    final_result = lax.map(single_row, (source_rows.reshape(PACKED_ROWS, ROW_LENGTH, MODEL_WIDTH), segments))
    return final_result.reshape(PACKED_ROWS * ROW_LENGTH, MODEL_WIDTH)

def adam_step(master, moment, square, grad, factor, rate, decay):
    clipped = grad * factor
    first_new = first_decay * moment + (1.0 - first_decay) * clipped
    second_new = second_decay * square + (1.0 - second_decay) * clipped * clipped
    first_hat = first_new / (1.0 - first_decay ** STEP)
    second_hat = second_new / (1.0 - second_decay ** STEP)
    updated = master - rate * (first_hat / (jnp.sqrt(second_hat) + adam_eps) + decay * master)
    return (updated, first_new, second_new)

def reference(inputs, segments, cotangent, triple_weight, output_weight, gate_weight, down_weight, vector_params, triple_moment, output_moment, gate_moment, down_moment, vector_moment, triple_square, output_square, gate_square, down_square, vector_square):

    def forward(source_rows, triple_master, output_master, gate_master, down_master, params):
        return layer_rows(source_rows, low(triple_master), low(output_master), low(gate_master), low(down_master), params, segments)
    primal, pullback = jax.vjp(forward, inputs.astype(jnp.float32), triple_weight, output_weight, gate_weight, down_weight, vector_params)
    input_grad, triple_grad, output_grad, gate_grad, down_grad, vector_grad = pullback(cotangent.astype(jnp.float32))
    grads = (triple_grad, output_grad, gate_grad, down_grad, vector_grad)
    total = jnp.float32(0.0)
    for single in grads:
        total = total + jnp.sum(single * single)
    grad_norm = jnp.sqrt(total)
    factor = jnp.minimum(1.0, clip_limit / (grad_norm + 1e-06))
    masters = (triple_weight, output_weight, gate_weight, down_weight, vector_params)
    moments = (triple_moment, output_moment, gate_moment, down_moment, vector_moment)
    squares = (triple_square, output_square, gate_square, down_square, vector_square)
    rate_table = (matrix_rate, output_rate, matrix_rate, matrix_rate, vector_rate)
    results = []
    for number in range(5):
        decay = weight_decay if number < 4 else 0.0
        results.append(adam_step(masters[number], moments[number], squares[number], grads[number], factor, rate_table[number], decay))
    return (primal.astype(jnp.bfloat16), input_grad, grad_norm, results[0][0], results[1][0], results[2][0], results[3][0], results[4][0], results[0][1], results[1][1], results[2][1], results[3][1], results[4][1], results[0][2], results[1][2], results[2][2], results[3][2], results[4][2], vector_grad[4])
```

```python
import functools

import jax
import jax.numpy as jnp
from jax import lax
from jax.experimental import pallas as pl
from jax.experimental.pallas import tpu as pltpu
from jax.sharding import PartitionSpec as P

HEAD_SIZE = 64
ROTARY = 16
STEP = 5


norm_eps = 1e-05
rotary_base = 10000.0
clip_limit = 1.0
first_decay = 0.9
second_decay = 0.95
adam_eps = 1e-08
matrix_rate = 0.03
output_rate = 0.2
vector_rate = 0.5
weight_decay = 0.1
masked_score = -1e30


def normalize(values, gain_row, offset_row):
    center = values - jnp.mean(values, axis=-1, keepdims=True)
    spread = jnp.mean(center * center, axis=-1, keepdims=True)
    return center * lax.rsqrt(spread + norm_eps) * gain_row + offset_row


def positions_of(row_segments):
    length = row_segments.shape[0]
    loop_counter = jnp.arange(length, dtype=jnp.int32)
    earlier = jnp.concatenate([jnp.full((1,), -1, jnp.int32), row_segments[:-1]])
    starts = jnp.where(row_segments != earlier, loop_counter, jnp.zeros_like(loop_counter))
    return loop_counter - lax.cummax(starts, axis=0)


def rotary_tables(positions, rotary):
    half_width = rotary // 2
    frequency = rotary_base ** (-2.0 * jnp.arange(half_width, dtype=jnp.float32) / rotary)
    angles = positions.astype(jnp.float32)[:, None] * frequency[None, :]
    return (jnp.cos(angles), jnp.sin(angles))


def rotate(values, cosine_table, sine_table, rotary):
    half_width = rotary // 2
    first_part = values[..., :half_width]
    second_part = values[..., half_width:rotary]
    cosine_wide = cosine_table[:, None, :]
    sine_wide = sine_table[:, None, :]
    return jnp.concatenate(
        [
            first_part * cosine_wide - second_part * sine_wide,
            second_part * cosine_wide + first_part * sine_wide,
            values[..., rotary:],
        ],
        axis=-1,
    )


def adam_step(master, moment, square, grad, factor, rate, decay):
    clipped = grad * factor
    first_new = first_decay * moment + (1.0 - first_decay) * clipped
    second_new = second_decay * square + (1.0 - second_decay) * clipped * clipped
    first_hat = first_new / (1.0 - first_decay**STEP)
    second_hat = second_new / (1.0 - second_decay**STEP)
    updated = master - rate * (first_hat / (jnp.sqrt(second_hat) + adam_eps) + decay * master)
    return (updated, first_new, second_new)


def attend_kernel(rows, heads, q_ref, k_ref, v_ref, seg_col_ref, seg_row_ref, out_ref, lse_ref):
    length = q_ref.shape[0]
    for start in range(0, length, rows):
        stop = start + rows
        allowed = (seg_col_ref[start:stop, :] == seg_row_ref[:, :stop]) & (
            lax.broadcasted_iota(jnp.int32, (rows, stop), 1)
            <= lax.broadcasted_iota(jnp.int32, (rows, stop), 0) + start
        )
        outs, logs = [], []
        for head in range(heads):
            lanes = slice(head * HEAD_SIZE, (head + 1) * HEAD_SIZE)
            scores = lax.dot_general(
                q_ref[start:stop, lanes], k_ref[:stop, lanes], (((1,), (1,)), ((), ())),
                preferred_element_type=jnp.float32,
            )
            masked = jnp.where(allowed, scores, masked_score)
            largest = jnp.max(masked, axis=-1, keepdims=True)
            powers = jnp.exp(masked - largest)
            totals = jnp.sum(powers, axis=-1, keepdims=True)
            soft_low = (powers * (1.0 / totals)).astype(jnp.bfloat16)
            outs.append(jnp.dot(soft_low, v_ref[:stop, lanes], preferred_element_type=jnp.float32))
            logs.append(largest + jnp.log(totals))
        out_ref[start:stop, :] = jnp.concatenate(outs, axis=1).astype(jnp.bfloat16)
        lse_ref[start:stop, :] = jnp.concatenate(logs, axis=1)


def attend(queries, keys, values, row_segments):
    length, width = queries.shape
    heads = width // HEAD_SIZE
    rows = min(256, length)
    return pl.pallas_call(
        functools.partial(attend_kernel, rows, heads),
        out_shape=(
            jax.ShapeDtypeStruct((length, width), jnp.bfloat16),
            jax.ShapeDtypeStruct((length, heads), jnp.float32),
        ),
        compiler_params=pltpu.CompilerParams(vmem_limit_bytes=48 << 20),
        cost_estimate=pl.CostEstimate(
            flops=4 * length * length * width, bytes_accessed=8 * length * width,
            transcendentals=length * length * heads,
        ),
        name="attend",
    )(queries, keys, values, row_segments[:, None], row_segments[None, :])


def attend_back_kernel(rows, heads, q_ref, k_ref, v_ref, g_ref, lse_ref, seg_col_ref, seg_row_ref,
                       dq_ref, dk_ref, dv_ref):
    length = q_ref.shape[0]
    for start in reversed(range(0, length, rows)):
        stop = start + rows
        allowed = (seg_col_ref[:stop, :] == seg_row_ref[:, start:stop]) & (
            lax.broadcasted_iota(jnp.int32, (stop, rows), 0)
            <= lax.broadcasted_iota(jnp.int32, (stop, rows), 1) + start
        )
        query_grads, key_grads, value_grads = [], [], []
        for head in range(heads):
            lanes = slice(head * HEAD_SIZE, (head + 1) * HEAD_SIZE)
            q, g = q_ref[start:stop, lanes], g_ref[start:stop, lanes]
            k, v = k_ref[:stop, lanes], v_ref[:stop, lanes]
            across = (((1,), (1,)), ((), ()))
            scores = lax.dot_general(k, q, across, preferred_element_type=jnp.float32)
            soft = jnp.exp(
                jnp.where(allowed, scores - lse_ref[head:head + 1, start:stop], masked_score)
            )
            soft_grad = lax.dot_general(v, g, across, preferred_element_type=jnp.float32)
            inner = jnp.sum(soft * soft_grad, axis=0, keepdims=True)
            score_grad = (soft * (soft_grad - inner)).astype(jnp.bfloat16)
            soft_low = soft.astype(jnp.bfloat16)
            value_grads.append(jnp.dot(soft_low, g, preferred_element_type=jnp.float32))
            key_grads.append(jnp.dot(score_grad, q, preferred_element_type=jnp.float32))
            query_grads.append(lax.dot_general(
                score_grad, k, (((0,), (0,)), ((), ())), preferred_element_type=jnp.float32
            ))
        dq_ref[start:stop, :] = jnp.concatenate(query_grads, axis=1)
        key_grad = jnp.concatenate(key_grads, axis=1)
        value_grad = jnp.concatenate(value_grads, axis=1)
        if stop == length:
            dk_ref[...] = key_grad
            dv_ref[...] = value_grad
        else:
            dk_ref[:stop, :] += key_grad
            dv_ref[:stop, :] += value_grad


def attend_back(queries, keys, values, mixed_grad, logsum, row_segments):
    length, width = queries.shape
    heads = width // HEAD_SIZE
    rows = min(256, length)
    wide = jax.ShapeDtypeStruct((length, width), jnp.float32)
    return pl.pallas_call(
        functools.partial(attend_back_kernel, rows, heads),
        out_shape=(wide, wide, wide),
        compiler_params=pltpu.CompilerParams(vmem_limit_bytes=48 << 20),
        cost_estimate=pl.CostEstimate(
            flops=10 * length * length * width, bytes_accessed=20 * length * width,
            transcendentals=length * length * heads,
        ),
        name="attend_back",
    )(queries, keys, values, mixed_grad, logsum.T, row_segments[:, None], row_segments[None, :])


def tie(value, *others):
    return lax.optimization_barrier((value, others))[0]


def turns(count, step):
    return [(i, (i + step) % count) for i in range(count)]


def block_at(array, index, dim, count):
    size = array.shape[dim] // count
    return lax.dynamic_slice_in_dim(array, lax.rem(index + count, count) * size, size, dim)


def ring_gather(shard, axis, dim):
    count, place = lax.axis_size(axis), lax.axis_index(axis)
    shape = list(shard.shape)
    size = shape[dim]
    shape[dim] = size * count
    whole = lax.dynamic_update_slice_in_dim(jnp.zeros(shape, shard.dtype), shard, place * size, dim)
    hops = []
    for step in range(1, count):
        shard = lax.ppermute(shard, axis, [(i, (i + 1) % count) for i in range(count)])
        hops.append(shard)
        whole = lax.dynamic_update_slice_in_dim(whole, shard, lax.rem(place + count - step, count) * size, dim)
    return whole, hops


def line_gather(shard, axis, dim):
    count, place = lax.axis_size(axis), lax.axis_index(axis)
    shape = list(shard.shape)
    size = shape[dim]
    shape[dim] = size * count
    right, left = shard, shard
    from_left, from_right, hops = {}, {}, []
    for step in range(1, count):
        right = lax.ppermute(right, axis, [(i, i + 1) for i in range(step - 1, count - 1)])
        left = lax.ppermute(left, axis, [(i, i - 1) for i in range(1, count - step + 1)])
        from_left[step] = right
        from_right[count - step] = left
        hops.append((right, left))
    whole = lax.dynamic_update_slice_in_dim(jnp.zeros(shape, shard.dtype), shard, place * size, dim)
    for step in range(1, count):
        whole = lax.dynamic_update_slice_in_dim(
            whole, from_left[step] + from_right[step], lax.rem(place + count - step, count) * size, dim
        )
    return whole, hops


def line_sum(array, axis, dim):
    count, place = lax.axis_size(axis), lax.axis_index(axis)
    right = block_at(array, place - 1, dim, count)
    left = block_at(array, place + 1, dim, count)
    hops = []
    for step in range(1, count):
        right = lax.ppermute(right, axis, [(i, i + 1) for i in range(step)])
        left = lax.ppermute(left, axis, [(i, i - 1) for i in range(count - step, count)])
        hops.append((right, left))
        if step < count - 1:
            right = right + block_at(array, place - 1 - step, dim, count)
            left = left + block_at(array, place + 1 + step, dim, count)
    own = block_at(array, place, dim, count).astype(jnp.float32)
    return own + right.astype(jnp.float32) + left.astype(jnp.float32), hops


def sum_everywhere(values, axes):
    for axis in axes:
        count, place = lax.axis_size(axis), lax.axis_index(axis)
        arrived = jnp.stack(
            [values]
            + [
                lax.ppermute(values, axis, [(i, (i + s) % count) for i in range(count)])
                for s in range(1, count)
            ]
        )
        values = 0.0
        for j in range(count):
            values = values + lax.dynamic_index_in_dim(
                arrived, lax.rem(place + count - j, count), 0, keepdims=False
            )
    return values


def swap(value, bit, axis):
    return lax.ppermute(value, axis, [(i, i ^ bit) for i in range(lax.axis_size(axis))])


def gather_rows(local, axis, second=(), third=(), ordered=True):
    if lax.axis_size(axis) != 8:
        return lax.all_gather(tie(local, second, third), axis, axis=0, tiled=True)
    place = lax.axis_index(axis)
    rows, width = local.shape
    half = width // 2
    near, far = swap(local, 2, axis), swap(local, 4, axis)
    corner = jnp.concatenate(
        [
            swap(tie(near[:, :half], second), 4, axis),
            swap(tie(far[:, half:], second), 2, axis),
        ],
        axis=1,
    )
    found = {0: local, 2: near, 4: far, 6: corner}
    for bits in (0, 2, 4, 6):
        sent = tie(found[bits], third) if bits == 6 else found[bits]
        found[bits + 1] = swap(sent, 1, axis)
    if not ordered:
        return jnp.concatenate([found[bits] for bits in range(8)], axis=0)
    whole = jnp.zeros((8, rows, width), local.dtype)
    for bits in (0, 2, 4, 1, 3, 5, 6, 7):
        whole = lax.dynamic_update_index_in_dim(whole, found[bits], jnp.bitwise_xor(place, bits), 0)
    return whole.reshape(8 * rows, width)


def sum_rows(partial, axis, second=(), third=(), ordered=True):
    bf16, f32 = jnp.bfloat16, jnp.float32
    partial = partial.astype(bf16)
    if lax.axis_size(axis) != 8:
        partial = tie(partial, second, third)
        return lax.psum_scatter(partial, axis, scatter_dimension=0, tiled=True).astype(f32)
    place = lax.axis_index(axis)
    width = partial.shape[1]
    half = width // 2
    blocks = partial.reshape(8, partial.shape[0] // 8, width)

    def block(bits):
        if not ordered:
            return blocks[bits]
        return lax.dynamic_index_in_dim(blocks, jnp.bitwise_xor(place, bits), 0, keepdims=False)

    chips = (6, 2, 4, 0)
    others = swap(jnp.stack([block(bits + 1) for bits in chips]), 1, axis)
    pair = {
        bits: (block(bits).astype(f32) + others[k].astype(f32)).astype(bf16)
        for k, bits in enumerate(chips)
    }
    near = swap(tie(jnp.stack([pair[2][:, :half], pair[6][:, :half]]), second), 2, axis).astype(f32)
    far = swap(tie(jnp.stack([pair[4][:, half:], pair[6][:, half:]]), second), 4, axis).astype(f32)
    last_far = swap(tie((pair[4][:, :half].astype(f32) + near[1]).astype(bf16), third), 4, axis)
    last_near = swap(tie((pair[2][:, half:].astype(f32) + far[1]).astype(bf16), third), 2, axis)
    return jnp.concatenate(
        [
            pair[0][:, :half].astype(f32) + near[0] + last_far.astype(f32),
            pair[0][:, half:].astype(f32) + far[0] + last_near.astype(f32),
        ],
        axis=1,
    )


def per_device(
    inputs,
    segments,
    cotangent,
    triple_weight,
    output_weight,
    gate_weight,
    down_weight,
    vector_params,
    triple_moment,
    output_moment,
    gate_moment,
    down_moment,
    vector_moment,
    triple_square,
    output_square,
    gate_square,
    down_square,
    vector_square,
):
    bf16, f32 = jnp.bfloat16, jnp.float32
    rank = lax.axis_index("mp")
    width = inputs.shape[1]
    head_width = triple_weight.shape[2]
    local_heads = head_width // HEAD_SIZE
    hidden_width = down_weight.shape[0]
    cut = max(128, hidden_width // 2 // 128 * 128)
    row_segments = segments[0]
    seq_length = row_segments.shape[0]
    score_scale = HEAD_SIZE ** (-0.5)

    heads_shard = jnp.concatenate([triple_weight.astype(bf16), output_weight.astype(bf16).T[None]], axis=0)
    heads_full, heads_hops = ring_gather(heads_shard, "dp", 1)
    feed_shards = [
        jnp.concatenate(
            [gate_weight[:, :, low:high].astype(bf16), down_weight[low:high].astype(bf16).T[None]], axis=0
        )
        for low, high in ((0, cut), (cut, hidden_width))
    ]
    first_feed, first_hops = line_gather(tie(feed_shards[0], heads_hops[-1]), "dp", 1)
    second_feed, second_hops = line_gather(tie(feed_shards[1], first_hops[0]), "dp", 1)

    cosine_table, sine_table = rotary_tables(positions_of(row_segments), ROTARY)
    bias_rows = lax.dynamic_slice_in_dim(vector_params[4:7], rank * head_width, head_width, 1)
    source_rows = inputs.astype(f32)

    normed_one = gather_rows(
        normalize(source_rows, vector_params[0], vector_params[1]).astype(bf16), "mp", second=heads_hops[0]
    )
    cotangent_full = gather_rows(tie(cotangent, heads_hops[0]), "mp", second=heads_hops[1], ordered=False)
    projected_rows = (
        jnp.einsum("sd,pde->pse", normed_one, heads_full[:3], preferred_element_type=f32)
        + bias_rows[:, None, :]
    )
    split_rows = projected_rows.reshape(3, seq_length, local_heads, HEAD_SIZE)
    scaled = rotate(split_rows[0], cosine_table, sine_table, ROTARY).astype(bf16) * bf16(score_scale)
    queries = scaled.reshape(seq_length, head_width)
    keys = rotate(split_rows[1], cosine_table, sine_table, ROTARY).astype(bf16).reshape(seq_length, head_width)
    values = projected_rows[2].astype(bf16)
    mixed_rows, logsum = attend(queries, keys, values, row_segments)
    mixed_rows = tie(mixed_rows, cotangent_full, first_hops[0])
    hidden_part = sum_rows(
        jnp.einsum("se,de->sd", mixed_rows, heads_full[3], preferred_element_type=f32), "mp"
    )
    hidden = source_rows + hidden_part
    normed_two = gather_rows(
        normalize(hidden, vector_params[2], vector_params[3]).astype(bf16),
        "mp",
        second=first_hops[1],
        third=second_hops[0],
        ordered=False,
    )

    feed_out = 0.0
    normed_two_part = 0.0
    feed_totals, back_hops = [], []
    entry = normed_two
    for part in (first_feed, second_feed):
        gate_up = jnp.einsum("sd,pdf->psf", entry, part[:2], preferred_element_type=f32)
        sigmoid_gate = jax.nn.sigmoid(gate_up[0])
        silu_gate = gate_up[0] * sigmoid_gate
        activated = (silu_gate * gate_up[1]).astype(bf16)
        activated_grad = jnp.dot(cotangent_full, part[2], preferred_element_type=f32)
        slope = sigmoid_gate * (1.0 + gate_up[0] * (1.0 - sigmoid_gate))
        gate_up_grad = jnp.stack(
            [activated_grad * gate_up[1] * slope, activated_grad * silu_gate]
        ).astype(bf16)
        gate_grad = jnp.einsum("sd,psf->pdf", normed_two, gate_up_grad, preferred_element_type=f32)
        down_grad = jnp.einsum("sd,sf->df", cotangent_full, activated, preferred_element_type=f32)
        grads = jnp.concatenate([gate_grad.astype(bf16), down_grad.astype(bf16)[None]], axis=0)
        feed_out = feed_out + jnp.einsum("sf,df->sd", activated, part[2], preferred_element_type=f32)
        normed_two_part = normed_two_part + jnp.einsum(
            "psf,pdf->sd", gate_up_grad, part[:2], preferred_element_type=f32
        )
        total, hops = line_sum(grads, "dp", 1)
        feed_totals.append(total)
        back_hops.append(hops)
        entry = tie(normed_two, hops[-2])
    normed_two_grad = sum_rows(normed_two_part, "mp", third=back_hops[0][-1], ordered=False)
    normed_two_grad = tie(normed_two_grad, back_hops[1][0])

    _, second_back = jax.vjp(normalize, hidden, vector_params[2], vector_params[3])
    hidden_extra, gain_two_grad, offset_two_grad = second_back(normed_two_grad)
    hidden_grad = cotangent.astype(f32) + hidden_extra
    attention_full = gather_rows(hidden_grad.astype(bf16), "mp", third=back_hops[1][1])
    mixed_grad = jnp.dot(attention_full, heads_full[3], preferred_element_type=f32).astype(bf16)
    output_grad = jnp.einsum("sd,se->de", attention_full, mixed_rows, preferred_element_type=f32)
    query_grad, key_grad, value_grad = attend_back(queries, keys, values, mixed_grad, logsum, row_segments)
    query_grad = query_grad * score_scale

    def unrotate(values):
        heads = values.reshape(seq_length, local_heads, HEAD_SIZE)
        return rotate(heads, cosine_table, -sine_table, ROTARY).reshape(seq_length, head_width)

    raw_grad = jnp.stack([unrotate(query_grad), unrotate(key_grad), value_grad]).astype(bf16)
    bias_grad = jnp.sum(raw_grad.astype(f32), axis=1)
    triple_grad = jnp.einsum("sd,pse->pde", normed_one, raw_grad, preferred_element_type=f32)
    grads = jnp.concatenate([triple_grad.astype(bf16), output_grad.astype(bf16)[None]], axis=0)
    heads_total, last_hops = line_sum(grads, "dp", 1)
    normed_one_grad = sum_rows(
        jnp.einsum("pse,pde->sd", raw_grad, heads_full[:3], preferred_element_type=f32),
        "mp",
        second=back_hops[1][-1],
        third=last_hops[0],
    )
    _, first_back = jax.vjp(normalize, source_rows, vector_params[0], vector_params[1])
    input_extra, gain_one_grad, offset_one_grad = first_back(normed_one_grad)
    input_grad = hidden_grad + input_extra
    feed_rows = sum_rows(tie(feed_out, normed_one_grad), "mp", second=last_hops[1], ordered=False)
    block_output = (hidden + feed_rows).astype(bf16)

    bias_full = lax.dynamic_update_slice_in_dim(
        jnp.zeros((3, width), f32), bias_grad, rank * head_width, 1
    )
    gate_total = jnp.concatenate([total[:2] for total in feed_totals], axis=2)
    down_total = jnp.concatenate([total[2].T for total in feed_totals], axis=0)
    reduced = (heads_total[:3], heads_total[3].T, gate_total, down_total)
    local_squares = jnp.float32(0.0)
    for single in reduced:
        local_squares = local_squares + jnp.sum(single * single)
    vector_part = jnp.concatenate(
        [
            gain_one_grad[None],
            offset_one_grad[None],
            gain_two_grad[None],
            offset_two_grad[None],
            bias_full,
            jnp.broadcast_to(local_squares, (1, width)),
        ],
        axis=0,
    )
    summed = sum_everywhere(vector_part, ("dp", "mp"))
    vector_total, square_total = summed[:7], summed[7, 0]
    grad_norm = jnp.sqrt(square_total + jnp.sum(vector_total * vector_total))
    factor = jnp.minimum(1.0, clip_limit / (grad_norm + 1e-06))
    grads = reduced + (vector_total,)
    masters = (triple_weight, output_weight, gate_weight, down_weight, vector_params)
    moments = (triple_moment, output_moment, gate_moment, down_moment, vector_moment)
    squares = (triple_square, output_square, gate_square, down_square, vector_square)
    rate_table = (matrix_rate, output_rate, matrix_rate, matrix_rate, vector_rate)
    results = []
    for number in range(5):
        decay = weight_decay if number < 4 else 0.0
        results.append(
            adam_step(
                masters[number],
                moments[number],
                squares[number],
                grads[number],
                factor,
                rate_table[number],
                decay,
            )
        )
    return (
        (block_output, input_grad, grad_norm)
        + tuple(result[0] for result in results)
        + tuple(result[1] for result in results)
        + tuple(result[2] for result in results)
        + (vector_total[4],)
    )


def solution(mesh):
    in_specs = (
        P(("dp", "mp"), None),
        P("dp", None),
        P(("dp", "mp"), None),
        P(None, "dp", "mp"),
        P("mp", "dp"),
        P(None, "dp", "mp"),
        P("mp", "dp"),
        P(),
        P(None, "dp", "mp"),
        P("mp", "dp"),
        P(None, "dp", "mp"),
        P("mp", "dp"),
        P(),
        P(None, "dp", "mp"),
        P("mp", "dp"),
        P(None, "dp", "mp"),
        P("mp", "dp"),
        P(),
    )
    out_specs = (
        P(("dp", "mp"), None),
        P(("dp", "mp"), None),
        P(),
        P(None, "dp", "mp"),
        P("mp", "dp"),
        P(None, "dp", "mp"),
        P("mp", "dp"),
        P(),
        P(None, "dp", "mp"),
        P("mp", "dp"),
        P(None, "dp", "mp"),
        P("mp", "dp"),
        P(),
        P(None, "dp", "mp"),
        P("mp", "dp"),
        P(None, "dp", "mp"),
        P("mp", "dp"),
        P(),
        P(),
    )
    return jax.shard_map(
        per_device, mesh=mesh, in_specs=in_specs, out_specs=out_specs, check_vma=False
    )
```

```python
import functools

import jax
import jax.numpy as jnp
from jax import lax
from jax.experimental import pallas as pl
from jax.experimental.pallas import tpu as pltpu
from jax.sharding import PartitionSpec as P

HEAD_SIZE = 64
ROTARY = 16
STEP = 5


norm_eps = 1e-05
rotary_base = 10000.0
clip_limit = 1.0
first_decay = 0.9
second_decay = 0.95
adam_eps = 1e-08
matrix_rate = 0.03
output_rate = 0.2
vector_rate = 0.5
weight_decay = 0.1
masked_score = -1e30


def normalize(values, gain_row, offset_row):
    center = values - jnp.mean(values, axis=-1, keepdims=True)
    spread = jnp.mean(center * center, axis=-1, keepdims=True)
    return center * lax.rsqrt(spread + norm_eps) * gain_row + offset_row


def positions_of(row_segments):
    length = row_segments.shape[0]
    loop_counter = jnp.arange(length, dtype=jnp.int32)
    earlier = jnp.concatenate([jnp.full((1,), -1, jnp.int32), row_segments[:-1]])
    starts = jnp.where(row_segments != earlier, loop_counter, jnp.zeros_like(loop_counter))
    return loop_counter - lax.cummax(starts, axis=0)


def rotary_tables(positions, rotary):
    half_width = rotary // 2
    frequency = rotary_base ** (-2.0 * jnp.arange(half_width, dtype=jnp.float32) / rotary)
    angles = positions.astype(jnp.float32)[:, None] * frequency[None, :]
    return (jnp.cos(angles), jnp.sin(angles))


def adam_step(master, moment, square, grad, factor, rate, decay):
    clipped = grad * factor
    first_new = first_decay * moment + (1.0 - first_decay) * clipped
    second_new = second_decay * square + (1.0 - second_decay) * clipped * clipped
    first_hat = first_new / (1.0 - first_decay**STEP)
    second_hat = second_new / (1.0 - second_decay**STEP)
    updated = master - rate * (first_hat / (jnp.sqrt(second_hat) + adam_eps) + decay * master)
    return (updated, first_new, second_new)


def spot(rank, number, count, size):
    bits = jnp.bitwise_xor(rank, number)
    place = jnp.bitwise_and(bits, 1) * (count // 2) + jnp.right_shift(bits, 1)
    return pl.multiple_of(place * size, size)


def attend_kernel(rows, heads, scale, count, rank_ref, raw_ref, bias_ref, plain_ref, ahead_ref, behind_ref, seg_col_ref, seg_row_ref,
                  before_ref, out_ref, q_ref, k_ref, v_ref, lse_ref):
    length, width = q_ref.shape
    size = length // count
    rank = rank_ref[0, 0]
    for number in range(count):
        here = slice(number * size, (number + 1) * size)
        there = pl.ds(spot(rank, number, count, size), size)
        plain, ahead, behind = plain_ref[here, :], ahead_ref[here, :], behind_ref[here, :]
        for part, low_ref in enumerate((q_ref, k_ref)):
            lanes = slice(part * width, (part + 1) * width)
            value = raw_ref[there, lanes] + bias_ref[:, lanes]
            turned = (
                value * plain
                + pltpu.roll(value, width - ROTARY // 2, 1) * ahead
                + pltpu.roll(value, ROTARY // 2, 1) * behind
            ).astype(jnp.bfloat16)
            low_ref[here, :] = turned * jnp.bfloat16(scale) if part == 0 else turned
        lanes = slice(2 * width, 3 * width)
        v_ref[here, :] = (raw_ref[there, lanes] + bias_ref[:, lanes]).astype(jnp.bfloat16)
    for start in range(0, length, rows):
        stop = start + rows
        allowed = (seg_col_ref[start:stop, :] == seg_row_ref[:, :stop]) & (
            lax.broadcasted_iota(jnp.int32, (rows, stop), 1)
            <= lax.broadcasted_iota(jnp.int32, (rows, stop), 0) + start
        )
        outs, logs = [], []
        for head in range(heads):
            lanes = slice(head * HEAD_SIZE, (head + 1) * HEAD_SIZE)
            scores = lax.dot_general(
                q_ref[start:stop, lanes], k_ref[:stop, lanes], (((1,), (1,)), ((), ())),
                preferred_element_type=jnp.float32,
            )
            masked = jnp.where(allowed, scores, masked_score)
            largest = jnp.max(masked, axis=-1, keepdims=True)
            powers = jnp.exp(masked - largest)
            totals = jnp.sum(powers, axis=-1, keepdims=True)
            soft_low = (powers * (1.0 / totals)).astype(jnp.bfloat16)
            outs.append(jnp.dot(soft_low, v_ref[:stop, lanes], preferred_element_type=jnp.float32))
            logs.append(largest + jnp.log(totals))
        mixed = jnp.concatenate(outs, axis=1).astype(jnp.bfloat16)
        for low in range(0, rows, size):
            out_ref[pl.ds(spot(rank, (start + low) // size, count, size), size), :] = mixed[low : low + size]
        lse_ref[start:stop, :] = jnp.concatenate(logs, axis=1)


def attend(rank, count, raw, bias, tables, row_segments, before):
    length, width = raw.shape[0], raw.shape[1] // 3
    heads = width // HEAD_SIZE
    rows = min(256, length)
    low = jax.ShapeDtypeStruct((length, width), jnp.bfloat16)
    return pl.pallas_call(
        functools.partial(attend_kernel, rows, heads, HEAD_SIZE ** (-0.5), count),
        in_specs=[pl.BlockSpec(memory_space=pltpu.SMEM)] + [pl.BlockSpec(memory_space=pltpu.VMEM)] * 7
        + [pl.BlockSpec(memory_space=pl.ANY)],
        out_shape=(low, low, low, low, jax.ShapeDtypeStruct((length, heads), jnp.float32)),
        compiler_params=pltpu.CompilerParams(vmem_limit_bytes=48 << 20),
        cost_estimate=pl.CostEstimate(
            flops=4 * length * length * width, bytes_accessed=20 * length * width,
            transcendentals=length * length * heads,
        ),
        name="attend",
    )(rank.reshape(1, 1), raw, bias, *tables, row_segments[:, None], row_segments[None, :], before)


def attend_back_kernel(rows, heads, scale, count, rank_ref, q_ref, k_ref, v_ref, grad_ref, lse_ref, plain_ref, ahead_ref, behind_ref,
                       seg_col_ref, seg_row_ref, raw_ref, bias_ref, g_ref, dk_ref, dv_ref):
    length, width = q_ref.shape
    size = length // count
    rank = rank_ref[0, 0]
    for number in range(count):
        there = pl.ds(spot(rank, number, count, size), size)
        g_ref[number * size : (number + 1) * size, :] = grad_ref[there, :]

    def put(start, stop, part, value):
        here = slice(start, stop)
        if part < 2:
            value = (
                value * plain_ref[here, :]
                - pltpu.roll(value, width - ROTARY // 2, 1) * ahead_ref[here, :]
                - pltpu.roll(value, ROTARY // 2, 1) * behind_ref[here, :]
            )
        low = value.astype(jnp.bfloat16)
        lanes = slice(part * width, (part + 1) * width)
        for number in range(start // size, stop // size):
            there = pl.ds(spot(rank, number, count, size), size)
            raw_ref[there, lanes] = low[number * size - start : (number + 1) * size - start]
        bias_ref[:, lanes] += jnp.sum(low.astype(jnp.float32), axis=0, keepdims=True)

    bias_ref[...] = jnp.zeros_like(bias_ref)
    for start in reversed(range(0, length, rows)):
        stop = start + rows
        allowed = (seg_col_ref[:stop, :] == seg_row_ref[:, start:stop]) & (
            lax.broadcasted_iota(jnp.int32, (stop, rows), 0)
            <= lax.broadcasted_iota(jnp.int32, (stop, rows), 1) + start
        )
        query_grads, key_grads, value_grads = [], [], []
        for head in range(heads):
            lanes = slice(head * HEAD_SIZE, (head + 1) * HEAD_SIZE)
            q, g = q_ref[start:stop, lanes], g_ref[start:stop, lanes]
            k, v = k_ref[:stop, lanes], v_ref[:stop, lanes]
            across = (((1,), (1,)), ((), ()))
            scores = lax.dot_general(k, q, across, preferred_element_type=jnp.float32)
            soft = jnp.exp(
                jnp.where(allowed, scores - lse_ref[head:head + 1, start:stop], masked_score)
            )
            soft_grad = lax.dot_general(v, g, across, preferred_element_type=jnp.float32)
            inner = jnp.sum(soft * soft_grad, axis=0, keepdims=True)
            score_grad = (soft * (soft_grad - inner)).astype(jnp.bfloat16)
            soft_low = soft.astype(jnp.bfloat16)
            value_grads.append(jnp.dot(soft_low, g, preferred_element_type=jnp.float32))
            key_grads.append(jnp.dot(score_grad, q, preferred_element_type=jnp.float32))
            query_grads.append(lax.dot_general(
                score_grad, k, (((0,), (0,)), ((), ())), preferred_element_type=jnp.float32
            ))
        put(start, stop, 0, jnp.concatenate(query_grads, axis=1) * scale)
        key_grad = jnp.concatenate(key_grads, axis=1)
        value_grad = jnp.concatenate(value_grads, axis=1)
        if stop == length:
            dk_ref[...] = key_grad
            dv_ref[...] = value_grad
        else:
            dk_ref[:stop, :] += key_grad
            dv_ref[:stop, :] += value_grad
        put(start, stop, 1, dk_ref[start:stop, :])
        put(start, stop, 2, dv_ref[start:stop, :])


def attend_back(rank, count, queries, keys, values, mixed_grad, logsum, tables, row_segments):
    length, width = queries.shape
    heads = width // HEAD_SIZE
    rows = min(256, length)
    return pl.pallas_call(
        functools.partial(attend_back_kernel, rows, heads, HEAD_SIZE ** (-0.5), count),
        in_specs=[pl.BlockSpec(memory_space=pltpu.SMEM)] + [pl.BlockSpec(memory_space=pltpu.VMEM)] * 10,
        out_shape=(
            jax.ShapeDtypeStruct((length, 3 * width), jnp.bfloat16),
            jax.ShapeDtypeStruct((1, 3 * width), jnp.float32),
        ),
        scratch_shapes=[pltpu.VMEM((length, width), jnp.bfloat16)] + [pltpu.VMEM((length, width), jnp.float32)] * 2,
        compiler_params=pltpu.CompilerParams(vmem_limit_bytes=48 << 20),
        cost_estimate=pl.CostEstimate(
            flops=10 * length * length * width, bytes_accessed=30 * length * width,
            transcendentals=length * length * heads,
        ),
        name="attend_back",
    )(
        rank.reshape(1, 1), queries, keys, values, mixed_grad, logsum.T, *tables,
        row_segments[:, None], row_segments[None, :],
    )


def adam_kernel(rate, decay, factor_ref, master_ref, moment_ref, square_ref, grad_ref,
                updated_ref, first_ref, second_ref):
    updated_ref[...], first_ref[...], second_ref[...] = adam_step(
        master_ref[...], moment_ref[...], square_ref[...], grad_ref[...].astype(jnp.float32),
        factor_ref[0, 0], rate, decay,
    )


def adam(master, moment, square, grad, factor, rate, decay):
    shape = master.shape
    flat = [array.reshape(-1, shape[-1]) for array in (master, moment, square, grad)]
    rows, width = flat[0].shape
    block = rows
    while block * width > 196608 and block % 16 == 0:
        block //= 2
    spec = pl.BlockSpec((block, width), lambda i: (i, 0))
    like = jax.ShapeDtypeStruct((rows, width), jnp.float32)
    results = pl.pallas_call(
        functools.partial(adam_kernel, rate, decay),
        grid=(rows // block,),
        in_specs=[pl.BlockSpec(memory_space=pltpu.SMEM)] + [spec] * 4,
        out_specs=[spec] * 3,
        out_shape=[like] * 3,
        compiler_params=pltpu.CompilerParams(vmem_limit_bytes=60 << 20),
        cost_estimate=pl.CostEstimate(flops=20 * rows * width, bytes_accessed=26 * rows * width, transcendentals=0),
        name="adam",
    )(factor.reshape(1, 1), *flat)
    return tuple(result.reshape(shape) for result in results)


def feed_kernel(rows_ref, cotangent_ref, weight_ref, activated_ref, grad_ref, back_ref, out_ref):
    line, _, slab = weight_ref.shape
    half = activated_ref.shape[0]
    across = (((1,), (1,)), ((), ()))
    gate_up, activated_grad = 0.0, 0.0
    for z in range(line):
        columns = slice(z * slab, (z + 1) * slab)
        gate_up += lax.dot_general(
            weight_ref[z, : 2 * half, :], rows_ref[:, columns], across, preferred_element_type=jnp.float32
        )
        activated_grad += lax.dot_general(
            weight_ref[z, 2 * half :, :], cotangent_ref[:, columns], across, preferred_element_type=jnp.float32
        )
    gate, up = gate_up[:half], gate_up[half:]
    sigmoid_gate = jax.nn.sigmoid(gate)
    silu_gate = gate * sigmoid_gate
    activated = (silu_gate * up).astype(jnp.bfloat16)
    slope = sigmoid_gate * (1.0 + gate * (1.0 - sigmoid_gate))
    gate_grad = (activated_grad * up * slope).astype(jnp.bfloat16)
    up_grad = (activated_grad * silu_gate).astype(jnp.bfloat16)
    activated_ref[...] = activated
    grad_ref[:half, :] = gate_grad
    grad_ref[half:, :] = up_grad
    down = (((0,), (0,)), ((), ()))
    for z in range(line):
        columns = slice(z * slab, (z + 1) * slab)
        back = lax.dot_general(
            grad_ref[...], weight_ref[z, : 2 * half, :], down, preferred_element_type=jnp.float32
        )
        back_ref[:, columns] = back.astype(jnp.bfloat16)
        out = lax.dot_general(
            activated, weight_ref[z, 2 * half :, :], down, preferred_element_type=jnp.float32
        )
        out_ref[:, columns] = out.astype(jnp.bfloat16)


def feed(rows, cotangent_rows, weights):
    length, width = rows.shape
    line, units, slab = weights.shape
    half = units // 3
    tile = min(512, length)
    by_rows = pl.BlockSpec((tile, width), lambda i: (i, 0))
    low = jnp.bfloat16
    return pl.pallas_call(
        feed_kernel,
        grid=(length // tile,),
        in_specs=[by_rows, by_rows, pl.BlockSpec(weights.shape, lambda i: (0, 0, 0))],
        out_specs=[
            pl.BlockSpec((half, tile), lambda i: (0, i)),
            pl.BlockSpec((2 * half, tile), lambda i: (0, i)),
            by_rows,
            by_rows,
        ],
        out_shape=[
            jax.ShapeDtypeStruct((half, length), low),
            jax.ShapeDtypeStruct((2 * half, length), low),
            jax.ShapeDtypeStruct((length, width), low),
            jax.ShapeDtypeStruct((length, width), low),
        ],
        compiler_params=pltpu.CompilerParams(vmem_limit_bytes=56 << 20),
        cost_estimate=pl.CostEstimate(
            flops=12 * length * width * half, bytes_accessed=10 * length * width, transcendentals=length * half,
        ),
        name="feed",
    )(rows, cotangent_rows, weights)


def tie(value, *others):
    return lax.optimization_barrier((value, others))[0]


def turns(count, step):
    return [(i, (i + step) % count) for i in range(count)]


def hold(value, *others):
    def kernel(*refs):
        pass

    others = [array.reshape((-1,) + array.shape[-2:])[0, :8, :128] for array in others]
    anywhere = pl.BlockSpec(memory_space=pl.ANY)
    return pl.pallas_call(
        kernel,
        out_shape=jax.ShapeDtypeStruct(value.shape, value.dtype),
        in_specs=[anywhere] * (1 + len(others)),
        out_specs=anywhere,
        input_output_aliases={0: 0},
        name="hold",
    )(value, *others)


def island(function, *operands):
    index = lax.axis_index("dp") * lax.axis_size("mp") + lax.axis_index("mp")
    shapes = jax.eval_shape(function, *operands)

    def never(*operands):
        return jax.tree.map(lambda shape: jnp.zeros(shape.shape, shape.dtype), shapes)

    return lax.cond(index >= 0, function, never, *operands)


def exchange(blocks, axis):
    return lax.all_to_all(blocks, axis, split_axis=0, concat_axis=0)


def cut_columns(array, count):
    return jnp.stack(jnp.split(array, count, axis=1))


def sum_everywhere(values, axes):
    for axis, count, bits in axes:
        place = lax.rem(lax.axis_index(axis) // bits, count)
        arrived = [values] + [swap(values, bits * k, axis) for k in range(1, count)]
        total = 0.0
        for j in range(count):
            total = total + sum(jnp.where(place == j ^ k, arrived[k], 0.0) for k in range(count))
        values = total
    return values


def swap(value, bits, axis):
    return lax.ppermute(value, axis, [(i, i ^ bits) for i in range(lax.axis_size(axis))])


def gather_rows(local, axis, second=()):
    count = lax.axis_size(axis)
    dim = local.ndim - 2
    if count != 8:
        whole = lax.all_gather(tie(local, second), axis, axis=0)
        place = lax.axis_index(axis)
        sides = [
            [
                lax.dynamic_index_in_dim(whole, jnp.bitwise_xor(place, 2 * k + core), 0, keepdims=False)
                for k in range(count // 2)
            ]
            for core in range(2)
        ]
        return [jnp.concatenate(side, axis=dim) for side in sides]
    rows = local.shape[dim] // 2
    near, far = swap(local, 2, axis), swap(local, 4, axis)
    corner_low = swap(tie(lax.slice_in_dim(near, 0, rows, axis=dim), second), 4, axis)
    corner_high = swap(tie(lax.slice_in_dim(far, rows, 2 * rows, axis=dim), second), 2, axis)
    mine = jnp.concatenate([local, near, far, corner_low, corner_high], axis=dim)
    return [mine, swap(mine, 1, axis)]


def sum_rows(mine, others, axis):
    bf16, f32 = jnp.bfloat16, jnp.float32
    count = lax.axis_size(axis)
    chips = count // 2
    arrived = swap(others.astype(bf16), 1, axis)
    pair = (mine.astype(f32) + arrived.astype(f32)).astype(bf16)
    pair = pair.reshape(pair.shape[:-2] + (chips, -1, pair.shape[-1]))
    rows = pair.shape[-2]
    if count != 8:
        total = pair[..., 0, :, :].astype(f32)
        for k in range(1, chips):
            total = total + swap(pair[..., k, :, :], 2 * k, axis).astype(f32)
        return total, arrived
    half = rows // 2
    low, high = pair[..., :half, :], pair[..., half:, :]
    near = swap(jnp.stack([low[..., 1, :, :], low[..., 3, :, :]]), 2, axis)
    far = swap(jnp.stack([high[..., 2, :, :], high[..., 3, :, :]]), 4, axis)
    last_far = swap((low[..., 2, :, :].astype(f32) + near[1].astype(f32)).astype(bf16), 4, axis)
    last_near = swap((high[..., 1, :, :].astype(f32) + far[1].astype(f32)).astype(bf16), 2, axis)
    low = low[..., 0, :, :].astype(f32) + near[0].astype(f32) + last_far.astype(f32)
    high = high[..., 0, :, :].astype(f32) + far[0].astype(f32) + last_near.astype(f32)
    return jnp.concatenate([low, high], axis=-2), (near, far)


def per_device(
    inputs,
    segments,
    cotangent,
    triple_weight,
    output_weight,
    gate_weight,
    down_weight,
    vector_params,
    triple_moment,
    output_moment,
    gate_moment,
    down_moment,
    vector_moment,
    triple_square,
    output_square,
    gate_square,
    down_square,
    vector_square,
):
    bf16, f32 = jnp.bfloat16, jnp.float32
    line, count = lax.axis_size("dp"), lax.axis_size("mp")
    rank = lax.axis_index("mp")
    tokens, width = inputs.shape
    head_width = triple_weight.shape[2]
    slab = triple_weight.shape[1]
    half = down_weight.shape[0] // 2
    row_segments = segments[0]
    seq_length = row_segments.shape[0]
    side = seq_length // 2

    heads_low = jnp.concatenate(
        [triple_weight[p].astype(bf16) for p in range(3)] + [output_weight.astype(bf16).T], axis=1
    )
    heads_full = lax.all_gather(heads_low, "dp", axis=0, tiled=True)
    triple_full, output_full = heads_full[:, : 3 * head_width], heads_full[:, 3 * head_width :]
    cotangent_swapped = swap(cotangent, 1, "dp")

    def first_rows(inputs, params):
        normed = normalize(inputs.astype(f32), params[0], params[1]).astype(bf16)
        return jnp.concatenate(gather_rows(normed, "mp"), axis=0)

    normed_one = island(first_rows, inputs, vector_params)

    gate_low = gate_weight.astype(bf16).swapaxes(1, 2).reshape(2, 2, half, slab)
    down_low = down_weight.astype(bf16).reshape(2, half, slab)
    feed_halves = [jnp.concatenate([gate_low[0, h], gate_low[1, h], down_low[h]], axis=0) for h in range(2)]
    feed_sent = hold(jnp.stack(feed_halves * (line // 2)), heads_full)
    feed_weights = exchange(feed_sent, "dp")
    cotangent_sides = gather_rows(jnp.stack([cotangent_swapped, cotangent]), "mp")
    cotangent_rows = jnp.concatenate([piece.reshape(-1, width) for piece in cotangent_sides], axis=0)

    cosine_table, sine_table = rotary_tables(positions_of(row_segments), ROTARY)
    still = jnp.zeros((seq_length, HEAD_SIZE - ROTARY), f32)
    zeros = jnp.zeros_like(sine_table)
    tables = [
        jnp.tile(jnp.concatenate(parts, axis=1), (1, head_width // HEAD_SIZE))
        for parts in (
            (cosine_table, cosine_table, still + 1.0),
            (-sine_table, zeros, still),
            (zeros, sine_table, still),
        )
    ]
    bias_rows = lax.dynamic_slice_in_dim(vector_params[4:7], rank * head_width, head_width, 1)
    across = (((1,), (1,)), ((), ()))
    down = (((0,), (0,)), ((), ()))
    projected_rows = jnp.dot(normed_one, triple_full, preferred_element_type=f32)
    mixed_rows, queries, keys, values, logsum = attend(
        rank, count, projected_rows, bias_rows.reshape(1, 3 * head_width), tables, row_segments, feed_sent[0, :8, :128]
    )

    def second_rows(mixed_rows, output_full, inputs, params):
        parts = [
            lax.dot_general(part, output_full, across, preferred_element_type=f32)
            for part in (mixed_rows[:side], mixed_rows[side:])
        ]
        hidden = inputs.astype(f32) + sum_rows(*parts, "mp")[0]
        normed = normalize(hidden, params[2], params[3]).astype(bf16)
        swapped = swap(normed, 1, "dp")
        own = gather_rows(normed, "mp")
        other = gather_rows(swapped, "mp")
        return hidden, jnp.concatenate([other[0], own[0], other[1], own[1]], axis=0)

    hidden, rows = island(second_rows, mixed_rows, output_full, inputs, vector_params)

    activated, gate_up_grad, normed_parts, feed_parts = feed(rows, cotangent_rows, feed_weights)
    down_grad = jnp.dot(activated, cotangent_rows, preferred_element_type=f32).astype(bf16)
    down_sent = cut_columns(down_grad, line)
    down_parts = exchange(down_sent, "dp")

    def normed_grads(normed_parts, gate_up_grad, rows):
        parts = normed_parts.reshape(4, side, width)
        normed_other, stage = sum_rows(parts[0], parts[2], "mp")
        normed_back = swap(normed_other.astype(bf16), 1, "dp")
        normed_own, _ = sum_rows(parts[1], tie(parts[3], stage), "mp")
        gate_grad = jnp.dot(gate_up_grad, rows, preferred_element_type=f32).astype(bf16)
        return normed_own + normed_back.astype(f32), cut_columns(gate_grad, line)

    normed_two_grad, gate_blocks = island(normed_grads, hold(normed_parts, down_sent), gate_up_grad, rows)
    gate_sent = hold(gate_blocks, down_parts)
    gate_parts = exchange(gate_sent, "dp")

    def attention_rows(normed_two_grad, hidden, cotangent, params):
        _, second_back = jax.vjp(normalize, hidden, params[2], params[3])
        hidden_extra, gain_grad, offset_grad = second_back(normed_two_grad)
        hidden_grad = cotangent.astype(f32) + hidden_extra
        sides = gather_rows(hidden_grad.astype(bf16), "mp")
        return hidden_grad, gain_grad, offset_grad, jnp.concatenate(sides, axis=0)

    hidden_grad, gain_two_grad, offset_two_grad, attention_full = island(
        attention_rows, hold(normed_two_grad, gate_sent), hidden, cotangent, vector_params
    )
    mixed_grad = jnp.dot(attention_full, output_full, preferred_element_type=f32).astype(bf16)
    raw_grad, bias_grad = attend_back(
        rank, count, queries, keys, values, mixed_grad, logsum, tables, row_segments
    )
    triple_grad = lax.dot_general(normed_one, raw_grad, down, preferred_element_type=f32).astype(bf16)
    output_grad = lax.dot_general(attention_full, mixed_rows, down, preferred_element_type=f32).astype(bf16)
    heads_grad = jnp.concatenate([triple_grad, output_grad], axis=1)
    heads_grad = hold(heads_grad, gate_parts)
    heads_total = lax.psum_scatter(heads_grad, "dp", scatter_dimension=0, tiled=True).astype(f32)

    stages = (("dp", line, 1), ("mp", count // 2, 2), ("mp", 2, 1))

    def last_sums(raw_grad, triple_full, feed_parts, inputs, hidden, hidden_grad, params):
        parts = [
            lax.dot_general(part, triple_full, across, preferred_element_type=f32)
            for part in (raw_grad[:side], raw_grad[side:])
        ]
        normed_one_grad, stage = sum_rows(*parts, "mp")
        _, first_back = jax.vjp(normalize, inputs.astype(f32), params[0], params[1])
        input_extra, gain_grad, offset_grad = first_back(normed_one_grad)
        parts = feed_parts.reshape(2, 2, side, width)
        feed_sums, _ = sum_rows(parts[0], parts[1], "mp")
        feed_back = swap(feed_sums[0].astype(bf16), 1, "dp").astype(f32)
        block_output = (hidden + feed_sums[1] + feed_back).astype(bf16)
        return hidden_grad + input_extra, gain_grad, offset_grad, block_output

    input_grad, gain_one_grad, offset_one_grad, block_output = island(
        last_sums, hold(raw_grad, heads_grad), triple_full, feed_parts, inputs, hidden, hidden_grad, vector_params
    )

    def both_halves(parts):
        halves = jnp.sum(parts.reshape((-1, 2) + parts.shape[1:]).astype(f32), axis=0)
        return halves.reshape(-1, slab)

    reduced = (
        jnp.stack([heads_total[:, p * head_width : (p + 1) * head_width] for p in range(3)]),
        heads_total[:, 3 * head_width :].T,
        jnp.concatenate([both_halves(gate_parts[:, :half]), both_halves(gate_parts[:, half:])], axis=0),
        both_halves(down_parts),
    )
    reduced = lax.optimization_barrier(reduced)
    local_squares = sum(jnp.sum(single * single) for single in reduced)
    bias_full = lax.dynamic_update_slice_in_dim(
        jnp.zeros((3, width), f32), bias_grad.reshape(3, head_width), rank * head_width, 1
    )
    norm_part = jnp.stack([gain_one_grad, offset_one_grad, gain_two_grad, offset_two_grad])
    vector_part = jnp.concatenate([norm_part, bias_full, jnp.broadcast_to(local_squares, (1, width))], axis=0)
    summed = sum_everywhere(vector_part, stages)
    vector_total = summed[:7]
    square_total = summed[7, 0] + jnp.sum(vector_total * vector_total)
    grad_norm = jnp.sqrt(square_total)
    factor = jnp.minimum(1.0, clip_limit / (grad_norm + 1e-06))
    gate_results = adam(
        *(array.swapaxes(1, 2) for array in (gate_weight, gate_moment, gate_square)),
        reduced[2],
        factor,
        matrix_rate,
        weight_decay,
    )
    results = [
        adam(triple_weight, triple_moment, triple_square, reduced[0], factor, matrix_rate, weight_decay),
        adam(output_weight, output_moment, output_square, reduced[1], factor, output_rate, weight_decay),
        tuple(array.swapaxes(1, 2) for array in gate_results),
        adam(down_weight, down_moment, down_square, reduced[3], factor, matrix_rate, weight_decay),
        adam_step(vector_params, vector_moment, vector_square, vector_total, factor, vector_rate, 0.0),
    ]
    return (
        (block_output, input_grad, grad_norm)
        + tuple(result[0] for result in results)
        + tuple(result[1] for result in results)
        + tuple(result[2] for result in results)
        + (vector_total[4],)
    )


def solution(mesh):
    in_specs = (
        P(("dp", "mp"), None),
        P("dp", None),
        P(("dp", "mp"), None),
        P(None, "dp", "mp"),
        P("mp", "dp"),
        P(None, "dp", "mp"),
        P("mp", "dp"),
        P(),
        P(None, "dp", "mp"),
        P("mp", "dp"),
        P(None, "dp", "mp"),
        P("mp", "dp"),
        P(),
        P(None, "dp", "mp"),
        P("mp", "dp"),
        P(None, "dp", "mp"),
        P("mp", "dp"),
        P(),
    )
    out_specs = (
        P(("dp", "mp"), None),
        P(("dp", "mp"), None),
        P(),
        P(None, "dp", "mp"),
        P("mp", "dp"),
        P(None, "dp", "mp"),
        P("mp", "dp"),
        P(),
        P(None, "dp", "mp"),
        P("mp", "dp"),
        P(None, "dp", "mp"),
        P("mp", "dp"),
        P(),
        P(None, "dp", "mp"),
        P("mp", "dp"),
        P(None, "dp", "mp"),
        P("mp", "dp"),
        P(),
        P(),
    )
    return jax.shard_map(
        per_device, mesh=mesh, in_specs=in_specs, out_specs=out_specs, check_vma=False
    )
```

```python
import functools

import jax
import jax.numpy as jnp
from jax import lax
from jax.experimental import pallas as pl
from jax.experimental.pallas import tpu as pltpu
from jax.sharding import PartitionSpec as P

HEAD_SIZE = 64
ROTARY = 16
STEP = 5


norm_eps = 1e-05
rotary_base = 10000.0
clip_limit = 1.0
first_decay = 0.9
second_decay = 0.95
adam_eps = 1e-08
matrix_rate = 0.03
output_rate = 0.2
vector_rate = 0.5
weight_decay = 0.1
masked_score = -1e30


def normalize(values, gain_row, offset_row):
    center = values - jnp.mean(values, axis=-1, keepdims=True)
    spread = jnp.mean(center * center, axis=-1, keepdims=True)
    return center * lax.rsqrt(spread + norm_eps) * gain_row + offset_row


def positions_of(row_segments):
    length = row_segments.shape[0]
    loop_counter = jnp.arange(length, dtype=jnp.int32)
    earlier = jnp.concatenate([jnp.full((1,), -1, jnp.int32), row_segments[:-1]])
    starts = jnp.where(row_segments != earlier, loop_counter, jnp.zeros_like(loop_counter))
    return loop_counter - lax.cummax(starts, axis=0)


def rotary_tables(positions, rotary):
    half_width = rotary // 2
    frequency = rotary_base ** (-2.0 * jnp.arange(half_width, dtype=jnp.float32) / rotary)
    angles = positions.astype(jnp.float32)[:, None] * frequency[None, :]
    return (jnp.cos(angles), jnp.sin(angles))


def adam_step(master, moment, square, grad, factor, rate, decay):
    clipped = grad * factor
    first_new = first_decay * moment + (1.0 - first_decay) * clipped
    second_new = second_decay * square + (1.0 - second_decay) * clipped * clipped
    first_hat = first_new / (1.0 - first_decay**STEP)
    second_hat = second_new / (1.0 - second_decay**STEP)
    updated = master - rate * (first_hat / (jnp.sqrt(second_hat) + adam_eps) + decay * master)
    return (updated, first_new, second_new)


def rotary_lanes(row_segments, width):
    cosine_table, sine_table = rotary_tables(positions_of(row_segments), ROTARY)
    half = ROTARY // 2
    lanes = jnp.arange(width) % HEAD_SIZE
    own = (lanes % half)[None, :] == jnp.arange(half)[:, None]
    turning = lanes < ROTARY
    plain = jnp.where(own & turning, 1.0, 0.0)
    ahead = jnp.where(own & (lanes < half), -1.0, 0.0)
    behind = jnp.where(own & turning & (lanes >= half), 1.0, 0.0)
    nothing = jnp.zeros_like(plain)
    rest = jnp.where(turning, 0.0, 1.0)[None, :]
    spread = jnp.concatenate(
        [
            jnp.concatenate([plain, nothing, nothing], axis=1),
            jnp.concatenate([nothing, ahead, behind], axis=1),
            jnp.concatenate([rest, jnp.zeros((1, 2 * width))], axis=1),
        ],
        axis=0,
    )
    factors = jnp.concatenate([cosine_table, sine_table, jnp.ones_like(cosine_table[:, :1])], axis=1)
    return jnp.dot(factors, spread, precision=lax.Precision.HIGHEST, preferred_element_type=jnp.float32)


def spot(rank, number, count, size):
    bits = jnp.bitwise_xor(rank, number)
    place = jnp.bitwise_and(bits, 1) * (count // 2) + jnp.right_shift(bits, 1)
    return pl.multiple_of(place * size, size)


def attend_kernel(rows, heads, scale, count, rank_ref, normed_ref, weight_ref, bias_ref, tables_ref, seg_col_ref, seg_row_ref,
                  before_ref, out_ref, q_ref, k_ref, v_ref, lse_ref, raw_ref):
    length, width = q_ref.shape
    size = length // count
    rank = rank_ref[0, 0]
    for start in range(0, length, rows):
        raw_ref[start : start + rows, :] = lax.dot_general(
            normed_ref[start : start + rows, :],
            weight_ref[...],
            (((1,), (1,)), ((), ())),
            preferred_element_type=jnp.float32,
        )
    for number in range(count):
        here = slice(number * size, (number + 1) * size)
        there = pl.ds(spot(rank, number, count, size), size)
        plain, ahead, behind = [tables_ref[here, k * width : (k + 1) * width] for k in range(3)]
        for part, low_ref in enumerate((q_ref, k_ref)):
            lanes = slice(part * width, (part + 1) * width)
            value = raw_ref[there, lanes] + bias_ref[:, lanes]
            turned = (
                value * plain
                + pltpu.roll(value, width - ROTARY // 2, 1) * ahead
                + pltpu.roll(value, ROTARY // 2, 1) * behind
            ).astype(jnp.bfloat16)
            low_ref[here, :] = turned * jnp.bfloat16(scale) if part == 0 else turned
        lanes = slice(2 * width, 3 * width)
        v_ref[here, :] = (raw_ref[there, lanes] + bias_ref[:, lanes]).astype(jnp.bfloat16)
    for start in range(0, length, rows):
        stop = start + rows
        allowed = (seg_col_ref[start:stop, :] == seg_row_ref[:, :stop]) & (
            lax.broadcasted_iota(jnp.int32, (rows, stop), 1)
            <= lax.broadcasted_iota(jnp.int32, (rows, stop), 0) + start
        )
        outs, logs = [], []
        for head in range(heads):
            lanes = slice(head * HEAD_SIZE, (head + 1) * HEAD_SIZE)
            scores = lax.dot_general(
                q_ref[start:stop, lanes], k_ref[:stop, lanes], (((1,), (1,)), ((), ())),
                preferred_element_type=jnp.float32,
            )
            masked = jnp.where(allowed, scores, masked_score)
            largest = jnp.max(masked, axis=-1, keepdims=True)
            powers = jnp.exp(masked - largest)
            totals = jnp.sum(powers, axis=-1, keepdims=True)
            soft_low = (powers * (1.0 / totals)).astype(jnp.bfloat16)
            outs.append(jnp.dot(soft_low, v_ref[:stop, lanes], preferred_element_type=jnp.float32))
            logs.append(largest + jnp.log(totals))
        mixed = jnp.concatenate(outs, axis=1).astype(jnp.bfloat16)
        for low in range(0, rows, size):
            out_ref[pl.ds(spot(rank, (start + low) // size, count, size), size), :] = mixed[low : low + size]
        lse_ref[start:stop, :] = jnp.concatenate(logs, axis=1)


def attend(rank, count, normed, weights, bias, tables, row_segments, before):
    length, features = normed.shape
    width = weights.shape[0] // 4
    heads = width // HEAD_SIZE
    rows = min(256, length)
    low = jax.ShapeDtypeStruct((length, width), jnp.bfloat16)

    def whole(shape):
        return pl.BlockSpec(shape, lambda i: (0,) * len(shape))

    return pl.pallas_call(
        functools.partial(attend_kernel, rows, heads, HEAD_SIZE ** (-0.5), count),
        grid=(1,),
        in_specs=[
            pl.BlockSpec(memory_space=pltpu.SMEM),
            whole((length, features)),
            whole((3 * width, features)),
            whole((1, 3 * width)),
        ]
        + [whole((length, 3 * width)), whole((length, 1)), whole((1, length)), pl.BlockSpec(memory_space=pl.ANY)],
        out_specs=[whole((length, width))] * 4 + [whole((length, heads))],
        scratch_shapes=[pltpu.VMEM((length, 3 * width), jnp.float32)],
        out_shape=(low, low, low, low, jax.ShapeDtypeStruct((length, heads), jnp.float32)),
        compiler_params=pltpu.CompilerParams(vmem_limit_bytes=60 << 20),
        cost_estimate=pl.CostEstimate(
            flops=4 * length * length * width + 6 * length * width * features, bytes_accessed=20 * length * width,
            transcendentals=length * length * heads,
        ),
        name="attend",
    )(rank.reshape(1, 1), normed, weights, bias, tables, row_segments[:, None], row_segments[None, :], before)


def attend_back_kernel(rows, heads, scale, count, rank_ref, q_ref, k_ref, v_ref, grad_ref, lse_ref, tables_ref,
                       seg_col_ref, seg_row_ref, raw_ref, bias_ref, g_ref, dk_ref, dv_ref):
    length, width = q_ref.shape
    size = length // count
    rank = rank_ref[0, 0]
    for number in range(count):
        there = pl.ds(spot(rank, number, count, size), size)
        g_ref[number * size : (number + 1) * size, :] = grad_ref[there, :]

    def put(start, stop, part, value):
        here = slice(start, stop)
        if part < 2:
            value = (
                value * tables_ref[here, :width]
                - pltpu.roll(value, width - ROTARY // 2, 1) * tables_ref[here, width : 2 * width]
                - pltpu.roll(value, ROTARY // 2, 1) * tables_ref[here, 2 * width :]
            )
        low = value.astype(jnp.bfloat16)
        lanes = slice(part * width, (part + 1) * width)
        for number in range(start // size, stop // size):
            there = pl.ds(spot(rank, number, count, size), size)
            raw_ref[there, lanes] = low[number * size - start : (number + 1) * size - start]
        bias_ref[:, lanes] += jnp.sum(low.astype(jnp.float32), axis=0, keepdims=True)

    bias_ref[...] = jnp.zeros_like(bias_ref)
    for start in reversed(range(0, length, rows)):
        stop = start + rows
        allowed = (seg_col_ref[:stop, :] == seg_row_ref[:, start:stop]) & (
            lax.broadcasted_iota(jnp.int32, (stop, rows), 0)
            <= lax.broadcasted_iota(jnp.int32, (stop, rows), 1) + start
        )
        query_grads, key_grads, value_grads = [], [], []
        for head in range(heads):
            lanes = slice(head * HEAD_SIZE, (head + 1) * HEAD_SIZE)
            q, g = q_ref[start:stop, lanes], g_ref[start:stop, lanes]
            k, v = k_ref[:stop, lanes], v_ref[:stop, lanes]
            across = (((1,), (1,)), ((), ()))
            scores = lax.dot_general(k, q, across, preferred_element_type=jnp.float32)
            soft = jnp.exp(
                jnp.where(allowed, scores - lse_ref[head:head + 1, start:stop], masked_score)
            )
            soft_grad = lax.dot_general(v, g, across, preferred_element_type=jnp.float32)
            inner = jnp.sum(soft * soft_grad, axis=0, keepdims=True)
            score_grad = (soft * (soft_grad - inner)).astype(jnp.bfloat16)
            soft_low = soft.astype(jnp.bfloat16)
            value_grads.append(jnp.dot(soft_low, g, preferred_element_type=jnp.float32))
            key_grads.append(jnp.dot(score_grad, q, preferred_element_type=jnp.float32))
            query_grads.append(lax.dot_general(
                score_grad, k, (((0,), (0,)), ((), ())), preferred_element_type=jnp.float32
            ))
        put(start, stop, 0, jnp.concatenate(query_grads, axis=1) * scale)
        key_grad = jnp.concatenate(key_grads, axis=1)
        value_grad = jnp.concatenate(value_grads, axis=1)
        if stop == length:
            dk_ref[...] = key_grad
            dv_ref[...] = value_grad
        else:
            dk_ref[:stop, :] += key_grad
            dv_ref[:stop, :] += value_grad
        put(start, stop, 1, dk_ref[start:stop, :])
        put(start, stop, 2, dv_ref[start:stop, :])


def attend_back(rank, count, queries, keys, values, mixed_grad, logsum, tables, row_segments):
    length, width = queries.shape
    heads = width // HEAD_SIZE
    rows = min(256, length)
    return pl.pallas_call(
        functools.partial(attend_back_kernel, rows, heads, HEAD_SIZE ** (-0.5), count),
        in_specs=[pl.BlockSpec(memory_space=pltpu.SMEM)] + [pl.BlockSpec(memory_space=pltpu.VMEM)] * 8,
        out_shape=(
            jax.ShapeDtypeStruct((length, 3 * width), jnp.bfloat16),
            jax.ShapeDtypeStruct((1, 3 * width), jnp.float32),
        ),
        scratch_shapes=[pltpu.VMEM((length, width), jnp.bfloat16)] + [pltpu.VMEM((length, width), jnp.float32)] * 2,
        compiler_params=pltpu.CompilerParams(vmem_limit_bytes=48 << 20),
        cost_estimate=pl.CostEstimate(
            flops=10 * length * length * width, bytes_accessed=30 * length * width,
            transcendentals=length * length * heads,
        ),
        name="attend_back",
    )(
        rank.reshape(1, 1), queries, keys, values, mixed_grad, logsum.T, tables,
        row_segments[:, None], row_segments[None, :],
    )


def adam_kernel(rate, turned, factor_ref, master_ref, moment_ref, square_ref, parts_ref, updated_ref, first_ref, second_ref):
    grad = jnp.sum(parts_ref[...].reshape((-1,) + parts_ref.shape[-2:]).astype(jnp.float32), axis=0)
    if turned:
        grad = grad.T
    updated_ref[0], first_ref[0], second_ref[0] = adam_step(
        master_ref[0], moment_ref[0], square_ref[0], grad, factor_ref[0, 0], rate, weight_decay
    )


def adam(master, moment, square, cuts, parts, place, factor, rate, turned=False):
    number, rows, width = master.shape
    rows //= cuts
    spec = pl.BlockSpec((1, rows, width), lambda i, j: (i, j, 0))
    block = (width, rows) if turned else (rows, width)
    parts_spec = pl.BlockSpec(parts.shape[:1] + (1,) * (parts.ndim - 3) + block, place)
    like = jax.ShapeDtypeStruct(master.shape, jnp.float32)
    return pl.pallas_call(
        functools.partial(adam_kernel, rate, turned),
        grid=(number, cuts),
        in_specs=[pl.BlockSpec(memory_space=pltpu.SMEM)] + [spec] * 3 + [parts_spec],
        out_specs=[spec] * 3,
        out_shape=[like] * 3,
        compiler_params=pltpu.CompilerParams(vmem_limit_bytes=60 << 20),
        cost_estimate=pl.CostEstimate(
            flops=20 * master.size, bytes_accessed=28 * master.size, transcendentals=0
        ),
        name="adam",
    )(factor.reshape(1, 1), master, moment, square, parts)


def feed_kernel(rows_ref, other_rows_ref, grad_rows_ref, other_grad_rows_ref, weight_ref, activated_ref, grad_ref,
                back_ref, other_back_ref, out_ref, other_out_ref, back_tile, out_tile):
    line, _, slab = weight_ref.shape
    half = activated_ref.shape[0]
    across = (((1,), (1,)), ((), ()))
    mine = pl.program_id(0) < pl.num_programs(0) // 2
    gate_up, activated_grad = 0.0, 0.0
    for z in range(line):
        columns = slice(z * slab, (z + 1) * slab)
        gate_up += lax.dot_general(
            weight_ref[z, : 2 * half, :],
            jnp.where(mine, rows_ref[:, columns], other_rows_ref[:, columns]),
            across,
            preferred_element_type=jnp.float32,
        )
        activated_grad += lax.dot_general(
            weight_ref[z, 2 * half :, :],
            jnp.where(mine, grad_rows_ref[:, columns], other_grad_rows_ref[:, columns]),
            across,
            preferred_element_type=jnp.float32,
        )
    gate, up = gate_up[:half], gate_up[half:]
    sigmoid_gate = jax.nn.sigmoid(gate)
    silu_gate = gate * sigmoid_gate
    activated = (silu_gate * up).astype(jnp.bfloat16)
    slope = sigmoid_gate * (1.0 + gate * (1.0 - sigmoid_gate))
    activated_ref[...] = activated
    grad_ref[:half, :] = (activated_grad * up * slope).astype(jnp.bfloat16)
    grad_ref[half:, :] = (activated_grad * silu_gate).astype(jnp.bfloat16)
    down = (((0,), (0,)), ((), ()))
    for z in range(line):
        columns = slice(z * slab, (z + 1) * slab)
        back_tile[:, columns] = lax.dot_general(
            grad_ref[...], weight_ref[z, : 2 * half, :], down, preferred_element_type=jnp.float32
        ).astype(jnp.bfloat16)
        out_tile[:, columns] = lax.dot_general(
            activated, weight_ref[z, 2 * half :, :], down, preferred_element_type=jnp.float32
        ).astype(jnp.bfloat16)

    @pl.when(mine)
    def _():
        back_ref[...] = back_tile[...]
        out_ref[...] = out_tile[...]

    @pl.when(jnp.logical_not(mine))
    def _():
        other_back_ref[...] = back_tile[...]
        other_out_ref[...] = out_tile[...]


def feed(sides, cotangent_sides, row, weights):
    length, width = sides[0].shape
    line, units, slab = weights.shape
    half = units // 3
    tile = min(512, length)
    steps = length // tile

    def first(i):
        return jnp.minimum(i, steps - 1)

    def second(i):
        return jnp.maximum(i - steps, 0)

    low = jnp.bfloat16
    two_sides = [pl.BlockSpec((tile, width), lambda i: (first(i), 0)), pl.BlockSpec((tile, width), lambda i: (second(i), 0))]
    return pl.pallas_call(
        feed_kernel,
        grid=(2 * steps,),
        in_specs=two_sides
        + [
            pl.BlockSpec((tile, width), lambda i: (row * steps + first(i), 0)),
            pl.BlockSpec((tile, width), lambda i: (row * steps + second(i), 0)),
            pl.BlockSpec(weights.shape, lambda i: (0, 0, 0)),
        ],
        out_specs=[
            pl.BlockSpec((half, tile), lambda i: (0, i)),
            pl.BlockSpec((2 * half, tile), lambda i: (0, i)),
        ]
        + two_sides * 2,
        out_shape=[
            jax.ShapeDtypeStruct((half, 2 * length), low),
            jax.ShapeDtypeStruct((2 * half, 2 * length), low),
        ]
        + [jax.ShapeDtypeStruct((length, width), low)] * 4,
        scratch_shapes=[pltpu.VMEM((tile, width), low)] * 2,
        compiler_params=pltpu.CompilerParams(vmem_limit_bytes=56 << 20),
        cost_estimate=pl.CostEstimate(
            flops=24 * length * width * half, bytes_accessed=20 * length * width, transcendentals=2 * length * half,
        ),
        name="feed",
    )(*sides, *cotangent_sides, weights)


def products_kernel(first_ref, second_ref, *refs):
    row_refs, more_refs, out_ref = refs[:4], refs[4:-1], refs[-1]
    height = first_ref.shape[0]
    size = row_refs[0].shape[0]
    total = 0.0
    for k, rows_ref in enumerate(row_refs):
        units_ref = (first_ref, second_ref)[k // 2]
        total += jnp.dot(
            units_ref[:, k % 2 * size : (k % 2 + 1) * size], rows_ref[...], preferred_element_type=jnp.float32
        )
    out_ref[0, :height] = total.astype(jnp.bfloat16)
    for more_ref in more_refs:
        out_ref[0, height:] = more_ref[0]


def products(units, row_blocks, count, *more):
    height, length = units[0].shape
    size = length // 2
    width = row_blocks[0][0].shape[1]
    slab = width // count
    total_height = height + sum(array.shape[1] for array in more)
    return pl.pallas_call(
        products_kernel,
        grid=(count,),
        in_specs=[pl.BlockSpec(units[0].shape, lambda i: (0, 0))] * 2
        + [pl.BlockSpec((size, slab), lambda i, row=row: (row, i)) for _, row in row_blocks]
        + [pl.BlockSpec((1,) + array.shape[1:], lambda i: (i, 0, 0)) for array in more],
        out_specs=pl.BlockSpec((1, total_height, slab), lambda i: (i, 0, 0)),
        out_shape=jax.ShapeDtypeStruct((count, total_height, slab), jnp.bfloat16),
        compiler_params=pltpu.CompilerParams(vmem_limit_bytes=56 << 20),
        cost_estimate=pl.CostEstimate(
            flops=4 * height * length * width, bytes_accessed=4 * length * width, transcendentals=0
        ),
        name="products",
    )(*units, *(array for array, _ in row_blocks), *more)


def heads_grad_kernel(normed_ref, raw_ref, attention_ref, mixed_ref, out_ref):
    down = (((0,), (0,)), ((), ()))
    cut = raw_ref.shape[1]
    for here, left_ref, right_ref in (
        (slice(0, cut), raw_ref, normed_ref),
        (slice(cut, out_ref.shape[0]), mixed_ref, attention_ref),
    ):
        out_ref[here, :] = lax.dot_general(
            left_ref[...], right_ref[...], down, preferred_element_type=jnp.float32
        ).astype(jnp.bfloat16)


def heads_grad(normed, raw_grad, attention, mixed):
    length, width = normed.shape
    columns = raw_grad.shape[1] + mixed.shape[1]
    tile = min(512, width)
    by_columns = pl.BlockSpec((length, tile), lambda i: (0, i))

    def whole(array):
        return pl.BlockSpec(array.shape, lambda i: (0, 0))

    return pl.pallas_call(
        heads_grad_kernel,
        grid=(width // tile,),
        in_specs=[by_columns, whole(raw_grad), by_columns, whole(mixed)],
        out_specs=pl.BlockSpec((columns, tile), lambda i: (0, i)),
        out_shape=jax.ShapeDtypeStruct((columns, width), jnp.bfloat16),
        compiler_params=pltpu.CompilerParams(vmem_limit_bytes=56 << 20),
        cost_estimate=pl.CostEstimate(
            flops=2 * length * width * columns, bytes_accessed=4 * length * width, transcendentals=0
        ),
        name="heads_grad",
    )(normed, raw_grad, attention, mixed)


def norm_back_kernel(values_ref, grad_ref, base_ref, gain_ref, out_ref, low_ref, gain_grad_ref, offset_grad_ref):
    values, grad = values_ref[...].astype(jnp.float32), grad_ref[...]
    center = values - jnp.mean(values, axis=-1, keepdims=True)
    scale = lax.rsqrt(jnp.mean(center * center, axis=-1, keepdims=True) + norm_eps)
    normal = center * scale
    inner = grad * gain_ref[...]
    inner_mean = jnp.mean(inner, axis=-1, keepdims=True)
    normal_mean = jnp.mean(inner * normal, axis=-1, keepdims=True)
    out = base_ref[...].astype(jnp.float32) + scale * (inner - inner_mean - normal * normal_mean)
    out_ref[...] = out
    low_ref[...] = out.astype(jnp.bfloat16)
    gain_grad_ref[...] = jnp.sum(grad * normal, axis=0, keepdims=True)
    offset_grad_ref[...] = jnp.sum(grad, axis=0, keepdims=True)


def norm_back(values, grad, base, gain):
    rows, width = values.shape
    vector = jax.ShapeDtypeStruct((1, width), jnp.float32)
    return pl.pallas_call(
        norm_back_kernel,
        out_shape=(
            jax.ShapeDtypeStruct((rows, width), jnp.float32),
            jax.ShapeDtypeStruct((rows, width), jnp.bfloat16),
            vector,
            vector,
        ),
        cost_estimate=pl.CostEstimate(flops=20 * rows * width, bytes_accessed=16 * rows * width, transcendentals=rows),
        name="norm_back",
    )(values, grad, base, gain.reshape(1, width))


def tie(value, *others):
    return lax.optimization_barrier((value, others))[0]


def turns(count, step):
    return [(i, (i + step) % count) for i in range(count)]


def hold(value, *others):
    def kernel(*refs):
        pass

    anywhere = pl.BlockSpec(memory_space=pl.ANY)
    return pl.pallas_call(
        kernel,
        out_shape=jax.ShapeDtypeStruct(value.shape, value.dtype),
        in_specs=[anywhere] * (1 + len(others)),
        out_specs=anywhere,
        input_output_aliases={0: 0},
        name="hold",
    )(value, *others)


def island(function, *operands):
    index = lax.axis_index("dp") * lax.axis_size("mp") + lax.axis_index("mp")
    shapes = jax.eval_shape(function, *operands)

    def never(*operands):
        return jax.tree.map(lambda shape: jnp.zeros(shape.shape, shape.dtype), shapes)

    return lax.cond(index >= 0, function, never, *operands)


def exchange(blocks, axis):
    return lax.all_to_all(blocks, axis, split_axis=0, concat_axis=0)


def sum_everywhere(values, axes):
    for axis, count, bits in axes:
        place = lax.rem(lax.axis_index(axis) // bits, count)
        arrived = [values] + [swap(values, bits * k, axis) for k in range(1, count)]
        total = 0.0
        for j in range(count):
            total = total + sum(jnp.where(place == j ^ k, arrived[k], 0.0) for k in range(count))
        values = total
    return values


def swap(value, bits, axis):
    return lax.ppermute(value, axis, [(i, i ^ bits) for i in range(lax.axis_size(axis))])


def gather_side(local, axis):
    count = lax.axis_size(axis)
    dim = local.ndim - 2
    if count != 8:
        pieces = [local] + [swap(local, 2 * k, axis) for k in range(1, count // 2)]
        return jnp.concatenate(pieces, axis=dim)
    rows = local.shape[dim] // 2
    near, far = swap(local, 2, axis), swap(local, 4, axis)
    corner_low = swap(lax.slice_in_dim(near, 0, rows, axis=dim), 4, axis)
    corner_high = swap(lax.slice_in_dim(far, rows, 2 * rows, axis=dim), 2, axis)
    return jnp.concatenate([local, near, far, corner_low, corner_high], axis=dim)


def gather_rows(local, axis):
    mine = gather_side(local, axis)
    return [mine, swap(mine, 1, axis)]


def pair_sum(mine, arrived, axis):
    pair = (mine.astype(jnp.float32) + arrived.astype(jnp.float32)).astype(jnp.bfloat16)
    return pair.reshape(pair.shape[:-2] + (lax.axis_size(axis) // 2, -1, pair.shape[-1]))


def halves_of(pair):
    half = pair.shape[-2] // 2
    return pair[..., :half, :], pair[..., half:, :]


def for_links(pair):
    low, high = halves_of(pair)
    near = jnp.stack([low[..., 1, :, :], low[..., 3, :, :]])
    return near, jnp.stack([high[..., 2, :, :], high[..., 3, :, :]])


def send_links(pair, axis):
    near, far = for_links(pair)
    return swap(near, 2, axis), swap(far, 4, axis)


def send_last(pair, near, far, axis):
    low, high = halves_of(pair)
    last_far = (low[..., 2, :, :].astype(jnp.float32) + near[1].astype(jnp.float32)).astype(jnp.bfloat16)
    last_near = (high[..., 1, :, :].astype(jnp.float32) + far[1].astype(jnp.float32)).astype(jnp.bfloat16)
    return swap(last_far, 4, axis), swap(last_near, 2, axis)


def total_of(pair, near, far, last_far, last_near):
    f32 = jnp.float32
    low, high = halves_of(pair)
    low = low[..., 0, :, :].astype(f32) + near[0].astype(f32) + last_far.astype(f32)
    high = high[..., 0, :, :].astype(f32) + far[0].astype(f32) + last_near.astype(f32)
    return jnp.concatenate([low, high], axis=-2)


def sum_rows(mine, others, axis):
    pair = pair_sum(mine, swap(others.astype(jnp.bfloat16), 1, axis), axis)
    if lax.axis_size(axis) != 8:
        total = pair[..., 0, :, :].astype(jnp.float32)
        for k in range(1, lax.axis_size(axis) // 2):
            total = total + swap(pair[..., k, :, :], 2 * k, axis).astype(jnp.float32)
        return total
    near, far = send_links(pair, axis)
    return total_of(pair, near, far, *send_last(pair, near, far, axis))


def per_device(
    inputs,
    segments,
    cotangent,
    triple_weight,
    output_weight,
    gate_weight,
    down_weight,
    vector_params,
    triple_moment,
    output_moment,
    gate_moment,
    down_moment,
    vector_moment,
    triple_square,
    output_square,
    gate_square,
    down_square,
    vector_square,
):
    bf16, f32 = jnp.bfloat16, jnp.float32
    line, count = lax.axis_size("dp"), lax.axis_size("mp")
    rank = lax.axis_index("mp")
    tokens, width = inputs.shape
    head_width = triple_weight.shape[2]
    slab = triple_weight.shape[1]
    half = down_weight.shape[0] // 2
    row_segments = segments[0]
    seq_length = row_segments.shape[0]
    side = seq_length // 2

    heads_low = jnp.concatenate(
        [triple_weight[p].astype(bf16).T for p in range(3)] + [output_weight.astype(bf16)], axis=0
    )
    heads_full = lax.all_gather(heads_low, "dp", axis=1, tiled=True)
    triple_full, output_full = heads_full[: 3 * head_width], heads_full[3 * head_width :]
    cotangent_swapped = swap(cotangent, 1, "dp")

    def first_rows(inputs, params, row_segments):
        normed = normalize(inputs.astype(f32), params[0], params[1]).astype(bf16)
        return jnp.concatenate(gather_rows(normed, "mp"), axis=0), rotary_lanes(row_segments, head_width)

    normed_one, tables = island(first_rows, inputs, vector_params, row_segments)

    gate_low = gate_weight.astype(bf16).swapaxes(1, 2).reshape(2, 2, half, slab)
    down_low = down_weight.astype(bf16).reshape(2, half, slab)
    feed_halves = [jnp.concatenate([gate_low[0, h], gate_low[1, h], down_low[h]], axis=0) for h in range(2)]
    cotangent_pair = hold(jnp.stack([cotangent_swapped, cotangent]), normed_one)

    def cotangent_side(pair):
        return gather_side(pair, "mp").reshape(-1, width)

    cotangent_mine = island(cotangent_side, cotangent_pair)
    cotangent_sides = [cotangent_mine, swap(cotangent_mine, 1, "mp")]
    feed_sent = hold(hold(jnp.stack(feed_halves * (line // 2)), cotangent_mine), heads_full)
    feed_weights = exchange(feed_sent, "dp")

    bias_rows = lax.dynamic_slice_in_dim(vector_params[4:7], rank * head_width, head_width, 1)
    across = (((1,), (1,)), ((), ()))
    down = (((0,), (0,)), ((), ()))
    mixed_rows, queries, keys, values, logsum = attend(
        rank, count, normed_one, heads_full, bias_rows.reshape(1, 3 * head_width), tables, row_segments, feed_sent
    )

    def second_rows(mixed_rows, output_full, inputs, params):
        parts = [
            jnp.dot(part, output_full, preferred_element_type=f32)
            for part in (mixed_rows[:side], mixed_rows[side:])
        ]
        hidden = inputs.astype(f32) + sum_rows(*parts, "mp")
        return hidden, normalize(hidden, params[2], params[3]).astype(bf16)

    hidden, normed_two = island(second_rows, mixed_rows, output_full, inputs, vector_params)
    normed_swapped = swap(normed_two, 1, "dp")
    rows_own = island(lambda normed: gather_rows(normed, "mp"), normed_two)

    own_results = feed(rows_own, cotangent_sides, 1, feed_weights)
    rows_other = island(lambda normed: gather_rows(normed, "mp"), hold(normed_swapped, own_results[0]))
    other_results = feed(rows_other, cotangent_sides, 0, feed_weights)
    activated, gate_up_grad = [(other_results[k], own_results[k]) for k in range(2)]
    normed_parts, feed_parts = [
        (other_results[k], own_results[k], other_results[k + 1], own_results[k + 1]) for k in (2, 4)
    ]

    def down_product(activated, cotangent_sides):
        return products(activated, [(cotangent_sides[k], row) for row in range(2) for k in range(2)], line)

    def gate_product(gate_up_grad, rows_other, rows_own):
        return products(gate_up_grad, [(array, 0) for array in (*rows_other, *rows_own)], line)

    if count == 8:
        def first_stage(parts, activated, cotangent_sides):
            arrived = swap(parts[2], 1, "mp")
            other_pair = pair_sum(parts[0], arrived, "mp")
            near, far = send_links(other_pair, "mp")
            own_pair = pair_sum(parts[1], swap(tie(parts[3], arrived), 1, "mp"), "mp")
            down_sent = down_product((hold(activated[0], other_pair), activated[1]), cotangent_sides)
            return other_pair, near, far, own_pair, down_sent

        other_pair, other_near, other_far, own_pair, down_sent = island(
            first_stage, normed_parts, activated, cotangent_sides
        )
        down_parts = exchange(down_sent, "dp")

        def second_stage(other_pair, other_near, other_far, own_pair, gate_up_grad, rows_other, rows_own, parts):
            last = send_last(other_pair, other_near, other_far, "mp")
            near, far = send_links(own_pair, "mp")
            normed_other = total_of(other_pair, other_near, other_far, *last).astype(bf16)
            normed_back = swap(normed_other, 1, "dp")
            units = (hold(gate_up_grad[0], normed_other), gate_up_grad[1])
            sent = gate_product(units, rows_other, rows_own)
            pairs = [pair_sum(parts[k], swap(tie(parts[k + 2], last), 1, "mp"), "mp") for k in range(2)]
            return normed_back, near, far, sent, pairs, for_links(pairs[0])

        normed_back, own_near, own_far, gate_sent, feed_pairs, other_sent = island(
            second_stage,
            hold(other_pair, down_sent),
            other_near,
            other_far,
            own_pair,
            gate_up_grad,
            rows_other,
            rows_own,
            feed_parts,
        )
        gate_sent = hold(gate_sent, down_parts)

        def attention_rows(normed_back, own_pair, own_near, own_far, hidden, cotangent, params):
            last = send_last(own_pair, own_near, own_far, "mp")
            grad = total_of(own_pair, own_near, own_far, *last) + normed_back.astype(f32)
            hidden_grad, hidden_grad_low, gain_grad, offset_grad = norm_back(hidden, grad, cotangent, params[2])
            sides = gather_rows(hidden_grad_low, "mp")
            return hidden_grad, gain_grad, offset_grad, jnp.concatenate(sides, axis=0)

        hidden_grad, gain_two_grad, offset_two_grad, attention_full = island(
            attention_rows,
            normed_back,
            hold(own_pair, gate_sent),
            own_near,
            own_far,
            hidden,
            cotangent,
            vector_params,
        )
    else:
        normed_back = swap(sum_rows(normed_parts[0], normed_parts[2], "mp").astype(bf16), 1, "dp")
        normed_two_grad = sum_rows(normed_parts[1], normed_parts[3], "mp") + normed_back.astype(f32)
        down_parts = exchange(down_product(activated, cotangent_sides), "dp")
        gate_sent = hold(gate_product(gate_up_grad, rows_other, rows_own), down_parts)
        hidden_grad, hidden_grad_low, gain_two_grad, offset_two_grad = norm_back(
            hidden, normed_two_grad, cotangent, vector_params[2]
        )
        attention_full = jnp.concatenate(gather_rows(hidden_grad_low, "mp"), axis=0)
    gate_parts = exchange(gate_sent, "dp")
    def attention_back(attention_full, output_full, queries, keys, values, logsum, tables, row_segments, other_sent):
        links = (swap(other_sent[0], 2, "mp"), swap(other_sent[1], 4, "mp")) if count == 8 else ()
        mixed_grad = lax.dot_general(attention_full, output_full, across, preferred_element_type=f32).astype(bf16)
        results = attend_back(rank, count, queries, keys, values, mixed_grad, logsum, tables, row_segments)
        return *results, links

    raw_grad, bias_grad, other_links = island(
        attention_back,
        attention_full,
        output_full,
        queries,
        keys,
        values,
        logsum,
        tables,
        row_segments,
        other_sent if count == 8 else (),
    )
    raw_grad = hold(raw_grad, gate_parts)
    heads_sent = heads_grad(normed_one, raw_grad, attention_full, mixed_rows)
    heads_total = lax.psum_scatter(heads_sent, "dp", scatter_dimension=1, tiled=True)
    stages = (("dp", line, 1), ("mp", count // 2, 2), ("mp", 2, 1))

    def last_sums(raw_grad, triple_full, feed, inputs, hidden, hidden_grad, params):
        parts = [
            jnp.dot(part, triple_full, preferred_element_type=f32)
            for part in (raw_grad[:side], raw_grad[side:])
        ]
        input_grad, _, gain_grad, offset_grad = norm_back(inputs, sum_rows(*parts, "mp"), hidden_grad, params[0])
        if count == 8:
            pairs, links = feed
            other_sum = total_of(pairs[0], *links, *send_last(pairs[0], *links, "mp"))
            links = send_links(pairs[1], "mp")
            own_sum = total_of(pairs[1], *links, *send_last(pairs[1], *links, "mp"))
        else:
            other_sum, own_sum = [sum_rows(feed[k], feed[k + 2], "mp") for k in range(2)]
        return input_grad, gain_grad, offset_grad, hidden + own_sum, other_sum.astype(bf16)

    input_grad, gain_one_grad, offset_one_grad, own_output, feed_other = island(
        last_sums,
        hold(raw_grad, heads_sent),
        triple_full,
        (feed_pairs, other_links) if count == 8 else feed_parts,
        inputs,
        hidden,
        hidden_grad,
        vector_params,
    )
    heads_total = hold(heads_total, input_grad)
    feed_back = swap(feed_other, 1, "dp")

    gate_grads = gate_parts.reshape(-1, 2, 2 * half, slab)
    down_grads = down_parts.reshape(-1, 2, half, slab)

    def squares_of(parts):
        return jnp.sum(jnp.square(jnp.sum(parts.astype(f32), axis=0)))

    local_squares = squares_of(gate_grads) + squares_of(down_grads) + squares_of(heads_total[None])
    bias_full = lax.dynamic_update_slice_in_dim(
        jnp.zeros((3, width), f32), bias_grad.reshape(3, head_width), rank * head_width, 1
    )
    squares_row = jnp.broadcast_to(local_squares, (1, width))
    vector_part = jnp.concatenate(
        [gain_one_grad, offset_one_grad, gain_two_grad, offset_two_grad, bias_full, squares_row], axis=0
    )
    summed = sum_everywhere(vector_part, stages)
    vector_total = summed[:7]
    square_total = summed[7, 0] + jnp.sum(vector_total * vector_total)
    grad_norm = jnp.sqrt(square_total)
    factor = jnp.minimum(1.0, clip_limit / (grad_norm + 1e-06))
    gate_results = adam(
        *(array.swapaxes(1, 2).reshape(4, half, slab) for array in (gate_weight, gate_moment, gate_square)),
        1,
        gate_grads,
        lambda i, j: (0, i % 2, i // 2, 0),
        factor,
        matrix_rate,
    )
    down_results = adam(
        *(array.reshape(2, half, slab) for array in (down_weight, down_moment, down_square)),
        1,
        down_grads,
        lambda i, j: (0, i, 0, 0),
        factor,
        matrix_rate,
    )
    triple_results = adam(
        triple_weight, triple_moment, triple_square, 1, heads_total[None], lambda i, j: (0, i, j), factor,
        matrix_rate, turned=True,
    )
    output_results = adam(
        *(array[None] for array in (output_weight, output_moment, output_square)),
        1,
        heads_total[None],
        lambda i, j: (0, 3, 0),
        factor,
        output_rate,
    )
    results = [
        triple_results,
        tuple(array[0] for array in output_results),
        tuple(array.reshape(2, 2 * half, slab).swapaxes(1, 2) for array in gate_results),
        tuple(array.reshape(2 * half, slab) for array in down_results),
        adam_step(vector_params, vector_moment, vector_square, vector_total, factor, vector_rate, 0.0),
    ]
    block_output = (own_output + hold(feed_back, gate_results[0]).astype(f32)).astype(bf16)
    return (
        (block_output, input_grad, grad_norm)
        + tuple(result[0] for result in results)
        + tuple(result[1] for result in results)
        + tuple(result[2] for result in results)
        + (vector_total[4],)
    )


def solution(mesh):
    in_specs = (
        P(("dp", "mp"), None),
        P("dp", None),
        P(("dp", "mp"), None),
        P(None, "dp", "mp"),
        P("mp", "dp"),
        P(None, "dp", "mp"),
        P("mp", "dp"),
        P(),
        P(None, "dp", "mp"),
        P("mp", "dp"),
        P(None, "dp", "mp"),
        P("mp", "dp"),
        P(),
        P(None, "dp", "mp"),
        P("mp", "dp"),
        P(None, "dp", "mp"),
        P("mp", "dp"),
        P(),
    )
    out_specs = (
        P(("dp", "mp"), None),
        P(("dp", "mp"), None),
        P(),
        P(None, "dp", "mp"),
        P("mp", "dp"),
        P(None, "dp", "mp"),
        P("mp", "dp"),
        P(),
        P(None, "dp", "mp"),
        P("mp", "dp"),
        P(None, "dp", "mp"),
        P("mp", "dp"),
        P(),
        P(None, "dp", "mp"),
        P("mp", "dp"),
        P(None, "dp", "mp"),
        P("mp", "dp"),
        P(),
        P(),
    )
    return jax.shard_map(
        per_device, mesh=mesh, in_specs=in_specs, out_specs=out_specs, check_vma=False
    )
```

```python
import functools

import jax
import jax.numpy as jnp
from jax import lax
from jax.experimental import pallas as pl
from jax.experimental.pallas import tpu as pltpu
from jax.sharding import PartitionSpec as P

HEAD_SIZE = 64
ROTARY = 16
STEP = 5


norm_eps = 1e-05
rotary_base = 10000.0
clip_limit = 1.0
first_decay = 0.9
second_decay = 0.95
adam_eps = 1e-08
matrix_rate = 0.03
output_rate = 0.2
vector_rate = 0.5
weight_decay = 0.1
masked_score = -1e30


def normalize(values, gain_row, offset_row):
    center = values - jnp.mean(values, axis=-1, keepdims=True)
    spread = jnp.mean(center * center, axis=-1, keepdims=True)
    return center * lax.rsqrt(spread + norm_eps) * gain_row + offset_row


def positions_of(row_segments):
    length = row_segments.shape[0]
    loop_counter = jnp.arange(length, dtype=jnp.int32)
    earlier = jnp.concatenate([jnp.full((1,), -1, jnp.int32), row_segments[:-1]])
    starts = jnp.where(row_segments != earlier, loop_counter, jnp.zeros_like(loop_counter))
    return loop_counter - lax.cummax(starts, axis=0)


def rotary_tables(positions, rotary):
    half_width = rotary // 2
    frequency = rotary_base ** (-2.0 * jnp.arange(half_width, dtype=jnp.float32) / rotary)
    angles = positions.astype(jnp.float32)[:, None] * frequency[None, :]
    return (jnp.cos(angles), jnp.sin(angles))


def adam_step(master, moment, square, grad, factor, rate, decay):
    clipped = grad * factor
    first_new = first_decay * moment + (1.0 - first_decay) * clipped
    second_new = second_decay * square + (1.0 - second_decay) * clipped * clipped
    first_hat = first_new / (1.0 - first_decay**STEP)
    second_hat = second_new / (1.0 - second_decay**STEP)
    updated = master - rate * (first_hat / (jnp.sqrt(second_hat) + adam_eps) + decay * master)
    return (updated, first_new, second_new)


def rotary_lanes(row_segments, width):
    cosine_table, sine_table = rotary_tables(positions_of(row_segments), ROTARY)
    half = ROTARY // 2
    lanes = jnp.arange(width) % HEAD_SIZE
    own = (lanes % half)[None, :] == jnp.arange(half)[:, None]
    turning = lanes < ROTARY
    plain = jnp.where(own & turning, 1.0, 0.0)
    ahead = jnp.where(own & (lanes < half), -1.0, 0.0)
    behind = jnp.where(own & turning & (lanes >= half), 1.0, 0.0)
    nothing = jnp.zeros_like(plain)
    rest = jnp.where(turning, 0.0, 1.0)[None, :]
    spread = jnp.concatenate(
        [
            jnp.concatenate([plain, nothing, nothing], axis=1),
            jnp.concatenate([nothing, ahead, behind], axis=1),
            jnp.concatenate([rest, jnp.zeros((1, 2 * width))], axis=1),
        ],
        axis=0,
    )
    factors = jnp.concatenate([cosine_table, sine_table, jnp.ones_like(cosine_table[:, :1])], axis=1)
    return jnp.dot(factors, spread, precision=lax.Precision.HIGHEST, preferred_element_type=jnp.float32)


def spot(rank, number, count, size):
    bits = jnp.bitwise_xor(rank, number)
    place = jnp.bitwise_and(bits, 1) * (count // 2) + jnp.right_shift(bits, 1)
    return pl.multiple_of(place * size, size)


def attend_kernel(rows, heads, scale, count, rank_ref, normed_ref, weight_ref, bias_ref, tables_ref, seg_col_ref, seg_row_ref,
                  before_ref, out_ref, q_ref, k_ref, v_ref, lse_ref, raw_ref):
    length, width = q_ref.shape
    size = length // count
    rank = rank_ref[0, 0]
    for start in range(0, length, rows):
        raw_ref[start : start + rows, :] = lax.dot_general(
            normed_ref[start : start + rows, :],
            weight_ref[...],
            (((1,), (1,)), ((), ())),
            preferred_element_type=jnp.float32,
        )
    for number in range(count):
        here = slice(number * size, (number + 1) * size)
        there = pl.ds(spot(rank, number, count, size), size)
        plain, ahead, behind = [tables_ref[here, k * width : (k + 1) * width] for k in range(3)]
        for part, low_ref in enumerate((q_ref, k_ref)):
            lanes = slice(part * width, (part + 1) * width)
            value = raw_ref[there, lanes] + bias_ref[:, lanes]
            turned = (
                value * plain
                + pltpu.roll(value, width - ROTARY // 2, 1) * ahead
                + pltpu.roll(value, ROTARY // 2, 1) * behind
            ).astype(jnp.bfloat16)
            low_ref[here, :] = turned * jnp.bfloat16(scale) if part == 0 else turned
        lanes = slice(2 * width, 3 * width)
        v_ref[here, :] = (raw_ref[there, lanes] + bias_ref[:, lanes]).astype(jnp.bfloat16)
    for start in range(0, length, rows):
        stop = start + rows
        allowed = (seg_col_ref[start:stop, :] == seg_row_ref[:, :stop]) & (
            lax.broadcasted_iota(jnp.int32, (rows, stop), 1)
            <= lax.broadcasted_iota(jnp.int32, (rows, stop), 0) + start
        )
        outs, logs = [], []
        for head in range(heads):
            lanes = slice(head * HEAD_SIZE, (head + 1) * HEAD_SIZE)
            scores = lax.dot_general(
                q_ref[start:stop, lanes], k_ref[:stop, lanes], (((1,), (1,)), ((), ())),
                preferred_element_type=jnp.float32,
            )
            masked = jnp.where(allowed, scores, masked_score)
            largest = jnp.max(masked, axis=-1, keepdims=True)
            powers = jnp.exp(masked - largest)
            totals = jnp.sum(powers, axis=-1, keepdims=True)
            soft_low = (powers * (1.0 / totals)).astype(jnp.bfloat16)
            outs.append(jnp.dot(soft_low, v_ref[:stop, lanes], preferred_element_type=jnp.float32))
            logs.append(largest + jnp.log(totals))
        mixed = jnp.concatenate(outs, axis=1).astype(jnp.bfloat16)
        for low in range(0, rows, size):
            out_ref[pl.ds(spot(rank, (start + low) // size, count, size), size), :] = mixed[low : low + size]
        lse_ref[start:stop, :] = jnp.concatenate(logs, axis=1)


def attend(rank, count, normed, weights, bias, tables, row_segments, before):
    length, features = normed.shape
    width = weights.shape[0] // 4
    heads = width // HEAD_SIZE
    rows = min(256, length)
    low = jax.ShapeDtypeStruct((length, width), jnp.bfloat16)

    def whole(shape):
        return pl.BlockSpec(shape, lambda i: (0,) * len(shape))

    return pl.pallas_call(
        functools.partial(attend_kernel, rows, heads, HEAD_SIZE ** (-0.5), count),
        grid=(1,),
        in_specs=[
            pl.BlockSpec(memory_space=pltpu.SMEM),
            whole((length, features)),
            whole((3 * width, features)),
            whole((1, 3 * width)),
        ]
        + [whole((length, 3 * width)), whole((length, 1)), whole((1, length)), pl.BlockSpec(memory_space=pl.ANY)],
        out_specs=[whole((length, width))] * 4 + [whole((length, heads))],
        scratch_shapes=[pltpu.VMEM((length, 3 * width), jnp.float32)],
        out_shape=(low, low, low, low, jax.ShapeDtypeStruct((length, heads), jnp.float32)),
        compiler_params=pltpu.CompilerParams(vmem_limit_bytes=60 << 20),
        cost_estimate=pl.CostEstimate(
            flops=4 * length * length * width + 6 * length * width * features, bytes_accessed=20 * length * width,
            transcendentals=length * length * heads,
        ),
        name="attend",
    )(rank.reshape(1, 1), normed, weights, bias, tables, row_segments[:, None], row_segments[None, :], before)


def attend_back_kernel(rows, heads, scale, count, rank_ref, q_ref, k_ref, v_ref, grad_ref, lse_ref, tables_ref,
                       seg_col_ref, seg_row_ref, raw_ref, bias_ref, g_ref, dk_ref, dv_ref):
    length, width = q_ref.shape
    size = length // count
    rank = rank_ref[0, 0]
    for number in range(count):
        there = pl.ds(spot(rank, number, count, size), size)
        g_ref[number * size : (number + 1) * size, :] = grad_ref[there, :]

    def put(start, stop, part, value):
        here = slice(start, stop)
        if part < 2:
            value = (
                value * tables_ref[here, :width]
                - pltpu.roll(value, width - ROTARY // 2, 1) * tables_ref[here, width : 2 * width]
                - pltpu.roll(value, ROTARY // 2, 1) * tables_ref[here, 2 * width :]
            )
        low = value.astype(jnp.bfloat16)
        lanes = slice(part * width, (part + 1) * width)
        for number in range(start // size, stop // size):
            there = pl.ds(spot(rank, number, count, size), size)
            raw_ref[there, lanes] = low[number * size - start : (number + 1) * size - start]
        bias_ref[:, lanes] += jnp.sum(low.astype(jnp.float32), axis=0, keepdims=True)

    bias_ref[...] = jnp.zeros_like(bias_ref)
    for start in reversed(range(0, length, rows)):
        stop = start + rows
        allowed = (seg_col_ref[:stop, :] == seg_row_ref[:, start:stop]) & (
            lax.broadcasted_iota(jnp.int32, (stop, rows), 0)
            <= lax.broadcasted_iota(jnp.int32, (stop, rows), 1) + start
        )
        query_grads, key_grads, value_grads = [], [], []
        for head in range(heads):
            lanes = slice(head * HEAD_SIZE, (head + 1) * HEAD_SIZE)
            q, g = q_ref[start:stop, lanes], g_ref[start:stop, lanes]
            k, v = k_ref[:stop, lanes], v_ref[:stop, lanes]
            across = (((1,), (1,)), ((), ()))
            scores = lax.dot_general(k, q, across, preferred_element_type=jnp.float32)
            soft = jnp.exp(
                jnp.where(allowed, scores - lse_ref[head:head + 1, start:stop], masked_score)
            )
            soft_grad = lax.dot_general(v, g, across, preferred_element_type=jnp.float32)
            inner = jnp.sum(soft * soft_grad, axis=0, keepdims=True)
            score_grad = (soft * (soft_grad - inner)).astype(jnp.bfloat16)
            soft_low = soft.astype(jnp.bfloat16)
            value_grads.append(jnp.dot(soft_low, g, preferred_element_type=jnp.float32))
            key_grads.append(jnp.dot(score_grad, q, preferred_element_type=jnp.float32))
            query_grads.append(lax.dot_general(
                score_grad, k, (((0,), (0,)), ((), ())), preferred_element_type=jnp.float32
            ))
        put(start, stop, 0, jnp.concatenate(query_grads, axis=1) * scale)
        key_grad = jnp.concatenate(key_grads, axis=1)
        value_grad = jnp.concatenate(value_grads, axis=1)
        if stop == length:
            dk_ref[...] = key_grad
            dv_ref[...] = value_grad
        else:
            dk_ref[:stop, :] += key_grad
            dv_ref[:stop, :] += value_grad
        put(start, stop, 1, dk_ref[start:stop, :])
        put(start, stop, 2, dv_ref[start:stop, :])


def attend_back(rank, count, queries, keys, values, mixed_grad, logsum, tables, row_segments):
    length, width = queries.shape
    heads = width // HEAD_SIZE
    rows = min(256, length)
    return pl.pallas_call(
        functools.partial(attend_back_kernel, rows, heads, HEAD_SIZE ** (-0.5), count),
        in_specs=[pl.BlockSpec(memory_space=pltpu.SMEM)] + [pl.BlockSpec(memory_space=pltpu.VMEM)] * 8,
        out_shape=(
            jax.ShapeDtypeStruct((length, 3 * width), jnp.bfloat16),
            jax.ShapeDtypeStruct((1, 3 * width), jnp.float32),
        ),
        scratch_shapes=[pltpu.VMEM((length, width), jnp.bfloat16)] + [pltpu.VMEM((length, width), jnp.float32)] * 2,
        compiler_params=pltpu.CompilerParams(vmem_limit_bytes=48 << 20),
        cost_estimate=pl.CostEstimate(
            flops=10 * length * length * width, bytes_accessed=30 * length * width,
            transcendentals=length * length * heads,
        ),
        name="attend_back",
    )(
        rank.reshape(1, 1), queries, keys, values, mixed_grad, logsum.T, tables,
        row_segments[:, None], row_segments[None, :],
    )


def adam_kernel(sections, factor_ref, *refs):
    in_refs, out_refs = refs[: 4 * len(sections)], refs[4 * len(sections) :]
    for k, (start, stop, rate, turned) in enumerate(sections):
        *state_refs, parts_ref = in_refs[4 * k : 4 * k + 4]
        results = out_refs[3 * k : 3 * k + 3]

        @pl.when((pl.program_id(0) >= start) & (pl.program_id(0) < stop))
        def _(state_refs=state_refs, parts_ref=parts_ref, results=results, rate=rate, turned=turned):
            grad = jnp.sum(parts_ref[...].reshape((-1,) + parts_ref.shape[-2:]).astype(jnp.float32), axis=0)
            if turned:
                grad = grad.T
            values = adam_step(*(ref[0] for ref in state_refs), grad, factor_ref[0, 0], rate, weight_decay)
            for result, value in zip(results, values):
                result[0] = value


def adam(factor, groups):
    sections, operands, in_specs, out_specs, out_shape = [], [], [], [], []
    start = 0
    for state, parts, place, rate, turned in groups:
        number, rows, width = state[0].shape

        def index(i, start=start, number=number):
            return jnp.clip(i - start, 0, number - 1)

        spec = pl.BlockSpec((1, rows, width), lambda i, index=index: (index(i), 0, 0))
        block = (width, rows) if turned else (rows, width)
        parts_spec = pl.BlockSpec(
            parts.shape[:1] + (1,) * (parts.ndim - 3) + block, lambda i, index=index, place=place: place(index(i))
        )
        sections.append((start, start + number, rate, turned))
        operands += [*state, parts]
        in_specs += [spec] * 3 + [parts_spec]
        out_specs += [spec] * 3
        out_shape += [jax.ShapeDtypeStruct(state[0].shape, jnp.float32)] * 3
        start += number
    size = sum(shape.size for shape in out_shape) // 3
    results = pl.pallas_call(
        functools.partial(adam_kernel, sections),
        grid=(start,),
        in_specs=[pl.BlockSpec(memory_space=pltpu.SMEM)] + in_specs,
        out_specs=out_specs,
        out_shape=out_shape,
        compiler_params=pltpu.CompilerParams(vmem_limit_bytes=60 << 20),
        cost_estimate=pl.CostEstimate(flops=20 * size, bytes_accessed=28 * size, transcendentals=0),
        name="adam",
    )(factor.reshape(1, 1), *operands)
    return [tuple(results[3 * k : 3 * k + 3]) for k in range(len(groups))]


def feed_kernel(rows_ref, other_rows_ref, grad_rows_ref, other_grad_rows_ref, weight_ref, activated_ref, grad_ref,
                back_ref, other_back_ref, out_ref, other_out_ref, back_tile, out_tile):
    line, _, slab = weight_ref.shape
    half = activated_ref.shape[0]
    across = (((1,), (1,)), ((), ()))
    mine = pl.program_id(0) < pl.num_programs(0) // 2
    gate_up, activated_grad = 0.0, 0.0
    for z in range(line):
        columns = slice(z * slab, (z + 1) * slab)
        gate_up += lax.dot_general(
            weight_ref[z, : 2 * half, :],
            jnp.where(mine, rows_ref[:, columns], other_rows_ref[:, columns]),
            across,
            preferred_element_type=jnp.float32,
        )
        activated_grad += lax.dot_general(
            weight_ref[z, 2 * half :, :],
            jnp.where(mine, grad_rows_ref[:, columns], other_grad_rows_ref[:, columns]),
            across,
            preferred_element_type=jnp.float32,
        )
    gate, up = gate_up[:half], gate_up[half:]
    sigmoid_gate = jax.nn.sigmoid(gate)
    silu_gate = gate * sigmoid_gate
    activated = (silu_gate * up).astype(jnp.bfloat16)
    slope = sigmoid_gate * (1.0 + gate * (1.0 - sigmoid_gate))
    activated_ref[...] = activated
    grad_ref[:half, :] = (activated_grad * up * slope).astype(jnp.bfloat16)
    grad_ref[half:, :] = (activated_grad * silu_gate).astype(jnp.bfloat16)
    down = (((0,), (0,)), ((), ()))
    for z in range(line):
        columns = slice(z * slab, (z + 1) * slab)
        back_tile[:, columns] = lax.dot_general(
            grad_ref[...], weight_ref[z, : 2 * half, :], down, preferred_element_type=jnp.float32
        ).astype(jnp.bfloat16)
        out_tile[:, columns] = lax.dot_general(
            activated, weight_ref[z, 2 * half :, :], down, preferred_element_type=jnp.float32
        ).astype(jnp.bfloat16)

    @pl.when(mine)
    def _():
        back_ref[...] = back_tile[...]
        out_ref[...] = out_tile[...]

    @pl.when(jnp.logical_not(mine))
    def _():
        other_back_ref[...] = back_tile[...]
        other_out_ref[...] = out_tile[...]


def feed(sides, cotangent_sides, row, weights):
    length, width = sides[0].shape
    line, units, slab = weights.shape
    half = units // 3
    tile = min(512, length)
    steps = length // tile

    def first(i):
        return jnp.minimum(i, steps - 1)

    def second(i):
        return jnp.maximum(i - steps, 0)

    low = jnp.bfloat16
    two_sides = [pl.BlockSpec((tile, width), lambda i: (first(i), 0)), pl.BlockSpec((tile, width), lambda i: (second(i), 0))]
    return pl.pallas_call(
        feed_kernel,
        grid=(2 * steps,),
        in_specs=two_sides
        + [
            pl.BlockSpec((tile, width), lambda i: (row * steps + first(i), 0)),
            pl.BlockSpec((tile, width), lambda i: (row * steps + second(i), 0)),
            pl.BlockSpec(weights.shape, lambda i: (0, 0, 0)),
        ],
        out_specs=[
            pl.BlockSpec((half, tile), lambda i: (0, i)),
            pl.BlockSpec((2 * half, tile), lambda i: (0, i)),
        ]
        + two_sides * 2,
        out_shape=[
            jax.ShapeDtypeStruct((half, 2 * length), low),
            jax.ShapeDtypeStruct((2 * half, 2 * length), low),
        ]
        + [jax.ShapeDtypeStruct((length, width), low)] * 4,
        scratch_shapes=[pltpu.VMEM((tile, width), low)] * 2,
        compiler_params=pltpu.CompilerParams(vmem_limit_bytes=56 << 20),
        cost_estimate=pl.CostEstimate(
            flops=24 * length * width * half, bytes_accessed=20 * length * width, transcendentals=2 * length * half,
        ),
        name="feed",
    )(*sides, *cotangent_sides, weights)


def products_kernel(first_ref, second_ref, *refs):
    row_refs, more_refs, out_ref = refs[:4], refs[4:-1], refs[-1]
    height = first_ref.shape[0]
    size = row_refs[0].shape[0]
    total = 0.0
    for k, rows_ref in enumerate(row_refs):
        units_ref = (first_ref, second_ref)[k // 2]
        total += jnp.dot(
            units_ref[:, k % 2 * size : (k % 2 + 1) * size], rows_ref[...], preferred_element_type=jnp.float32
        )
    out_ref[0, :height] = total.astype(jnp.bfloat16)
    for more_ref in more_refs:
        out_ref[0, height:] = more_ref[0]


def products(units, row_blocks, count, *more):
    height, length = units[0].shape
    size = length // 2
    width = row_blocks[0][0].shape[1]
    slab = width // count
    total_height = height + sum(array.shape[1] for array in more)
    return pl.pallas_call(
        products_kernel,
        grid=(count,),
        in_specs=[pl.BlockSpec(units[0].shape, lambda i: (0, 0))] * 2
        + [pl.BlockSpec((size, slab), lambda i, row=row: (row, i)) for _, row in row_blocks]
        + [pl.BlockSpec((1,) + array.shape[1:], lambda i: (i, 0, 0)) for array in more],
        out_specs=pl.BlockSpec((1, total_height, slab), lambda i: (i, 0, 0)),
        out_shape=jax.ShapeDtypeStruct((count, total_height, slab), jnp.bfloat16),
        compiler_params=pltpu.CompilerParams(vmem_limit_bytes=56 << 20),
        cost_estimate=pl.CostEstimate(
            flops=4 * height * length * width, bytes_accessed=4 * length * width, transcendentals=0
        ),
        name="products",
    )(*units, *(array for array, _ in row_blocks), *more)


def heads_grad_kernel(normed_ref, raw_ref, attention_ref, mixed_ref, out_ref):
    down = (((0,), (0,)), ((), ()))
    cut = raw_ref.shape[1]
    for here, left_ref, right_ref in (
        (slice(0, cut), raw_ref, normed_ref),
        (slice(cut, out_ref.shape[0]), mixed_ref, attention_ref),
    ):
        out_ref[here, :] = lax.dot_general(
            left_ref[...], right_ref[...], down, preferred_element_type=jnp.float32
        ).astype(jnp.bfloat16)


def heads_grad(normed, raw_grad, attention, mixed):
    length, width = normed.shape
    columns = raw_grad.shape[1] + mixed.shape[1]
    tile = min(512, width)
    by_columns = pl.BlockSpec((length, tile), lambda i: (0, i))

    def whole(array):
        return pl.BlockSpec(array.shape, lambda i: (0, 0))

    return pl.pallas_call(
        heads_grad_kernel,
        grid=(width // tile,),
        in_specs=[by_columns, whole(raw_grad), by_columns, whole(mixed)],
        out_specs=pl.BlockSpec((columns, tile), lambda i: (0, i)),
        out_shape=jax.ShapeDtypeStruct((columns, width), jnp.bfloat16),
        compiler_params=pltpu.CompilerParams(vmem_limit_bytes=56 << 20),
        cost_estimate=pl.CostEstimate(
            flops=2 * length * width * columns, bytes_accessed=4 * length * width, transcendentals=0
        ),
        name="heads_grad",
    )(normed, raw_grad, attention, mixed)


def total_from(pair_ref, near_ref, far_ref, last_far_ref, last_near_ref):
    half = near_ref.shape[1]
    f32 = jnp.float32
    low = pair_ref[0, :half].astype(f32) + near_ref[0].astype(f32) + last_far_ref[...].astype(f32)
    high = pair_ref[0, half:].astype(f32) + far_ref[0].astype(f32) + last_near_ref[...].astype(f32)
    return jnp.concatenate([low, high], axis=0)


def total_specs(pieces):
    first = [pl.BlockSpec((1,) + piece.shape[1:], lambda i: (0, 0, 0)) for piece in pieces[:3]]
    return first + [whole_block(piece) for piece in pieces[3:]]


def whole_block(array):
    return pl.BlockSpec(array.shape, lambda i: (0,) * array.ndim)


def norm_sum_kernel(base_ref, gain_ref, offset_ref, *refs):
    *piece_refs, hidden_ref, normed_ref = refs
    total = total_from(*piece_refs) if len(piece_refs) > 1 else piece_refs[0][...]
    hidden = base_ref[...].astype(jnp.float32) + total
    hidden_ref[...] = hidden
    normed_ref[...] = normalize(hidden, gain_ref[...], offset_ref[...]).astype(jnp.bfloat16)


def norm_sum(base, pieces, gain, offset):
    rows, width = base.shape
    operands = (base, gain.reshape(1, width), offset.reshape(1, width))
    shapes = (jax.ShapeDtypeStruct((rows, width), jnp.float32), jax.ShapeDtypeStruct((rows, width), jnp.bfloat16))
    return pl.pallas_call(
        norm_sum_kernel,
        grid=(1,),
        in_specs=[whole_block(array) for array in operands]
        + (total_specs(pieces) if len(pieces) > 1 else [whole_block(pieces[0])]),
        out_specs=[whole_block(shape) for shape in shapes],
        out_shape=shapes,
        cost_estimate=pl.CostEstimate(flops=12 * rows * width, bytes_accessed=14 * rows * width, transcendentals=rows),
        name="norm_sum",
    )(*operands, *pieces)


def norm_back_kernel(more, values_ref, base_ref, gain_ref, *refs):
    *piece_refs, out_ref, low_ref, gain_grad_ref, offset_grad_ref = refs
    values = values_ref[...].astype(jnp.float32)
    if more:
        *piece_refs, more_ref = piece_refs
    grad = total_from(*piece_refs) if len(piece_refs) > 1 else piece_refs[0][...]
    if more:
        grad = grad + more_ref[...].astype(jnp.float32)
    center = values - jnp.mean(values, axis=-1, keepdims=True)
    scale = lax.rsqrt(jnp.mean(center * center, axis=-1, keepdims=True) + norm_eps)
    normal = center * scale
    inner = grad * gain_ref[...]
    inner_mean = jnp.mean(inner, axis=-1, keepdims=True)
    normal_mean = jnp.mean(inner * normal, axis=-1, keepdims=True)
    out = base_ref[...].astype(jnp.float32) + scale * (inner - inner_mean - normal * normal_mean)
    out_ref[...] = out
    low_ref[...] = out.astype(jnp.bfloat16)
    gain_grad_ref[...] = jnp.sum(grad * normal, axis=0, keepdims=True)
    offset_grad_ref[...] = jnp.sum(grad, axis=0, keepdims=True)


def norm_back(values, pieces, base, gain, *more):
    rows, width = values.shape
    operands = (values, base, gain.reshape(1, width))
    vector = jax.ShapeDtypeStruct((1, width), jnp.float32)
    shapes = (
        jax.ShapeDtypeStruct((rows, width), jnp.float32),
        jax.ShapeDtypeStruct((rows, width), jnp.bfloat16),
        vector,
        vector,
    )
    return pl.pallas_call(
        functools.partial(norm_back_kernel, len(more)),
        grid=(1,),
        in_specs=[whole_block(array) for array in operands]
        + (total_specs(pieces) if len(pieces) > 1 else [whole_block(pieces[0])])
        + [whole_block(array) for array in more],
        out_specs=[whole_block(shape) for shape in shapes],
        out_shape=shapes,
        cost_estimate=pl.CostEstimate(flops=20 * rows * width, bytes_accessed=16 * rows * width, transcendentals=rows),
        name="norm_back",
    )(*operands, *pieces, *more)


def pair_kernel(mine_ref, arrived_ref, pair_ref, near_ref, far_ref):
    chips, rows, _ = pair_ref.shape
    half = rows // 2
    for chip in range(chips):
        here = slice(chip * rows, (chip + 1) * rows)
        total = (mine_ref[here, :].astype(jnp.float32) + arrived_ref[here, :].astype(jnp.float32)).astype(jnp.bfloat16)
        pair_ref[chip] = total
        if chip % 2:
            near_ref[chip // 2] = total[:half]
        if chip > 1:
            far_ref[chip - 2] = total[half:]


def pair_links(mine, arrived):
    length, width = mine.shape
    rows = length // 4
    low = jnp.bfloat16
    return pl.pallas_call(
        pair_kernel,
        out_shape=(
            jax.ShapeDtypeStruct((4, rows, width), low),
            jax.ShapeDtypeStruct((2, rows // 2, width), low),
            jax.ShapeDtypeStruct((2, rows // 2, width), low),
        ),
        cost_estimate=pl.CostEstimate(flops=length * width, bytes_accessed=8 * length * width, transcendentals=0),
        name="pair_links",
    )(mine, arrived)


def tie(value, *others):
    return lax.optimization_barrier((value, others))[0]


def turns(count, step):
    return [(i, (i + step) % count) for i in range(count)]


def hold(value, *others):
    def kernel(*refs):
        pass

    anywhere = pl.BlockSpec(memory_space=pl.ANY)
    return pl.pallas_call(
        kernel,
        out_shape=jax.ShapeDtypeStruct(value.shape, value.dtype),
        in_specs=[anywhere] * (1 + len(others)),
        out_specs=anywhere,
        input_output_aliases={0: 0},
        name="hold",
    )(value, *others)


def island(function, *operands):
    index = lax.axis_index("dp") * lax.axis_size("mp") + lax.axis_index("mp")
    shapes = jax.eval_shape(function, *operands)

    def never(*operands):
        return jax.tree.map(lambda shape: jnp.zeros(shape.shape, shape.dtype), shapes)

    return lax.cond(index >= 0, function, never, *operands)


def exchange(blocks, axis):
    return lax.all_to_all(blocks, axis, split_axis=0, concat_axis=0)


def sum_everywhere(values, axes):
    for axis, count, bits in axes:
        place = lax.rem(lax.axis_index(axis) // bits, count)
        arrived = [values] + [swap(values, bits * k, axis) for k in range(1, count)]
        total = 0.0
        for j in range(count):
            total = total + sum(jnp.where(place == j ^ k, arrived[k], 0.0) for k in range(count))
        values = total
    return values


def swap(value, bits, axis):
    return lax.ppermute(value, axis, [(i, i ^ bits) for i in range(lax.axis_size(axis))])


def gather_side(local, axis, beside=lambda: ()):
    count = lax.axis_size(axis)
    dim = local.ndim - 2
    if count != 8:
        pieces = [local] + [swap(local, 2 * k, axis) for k in range(1, count // 2)]
        return jnp.concatenate(pieces, axis=dim), beside()
    rows = local.shape[dim] // 2
    near, far = swap(local, 2, axis), swap(local, 4, axis)
    results = beside()
    if results:
        near, far = hold(near, results[0]), hold(far, results[0])
    corner_low = swap(lax.slice_in_dim(near, 0, rows, axis=dim), 4, axis)
    corner_high = swap(lax.slice_in_dim(far, rows, 2 * rows, axis=dim), 2, axis)
    return jnp.concatenate([local, near, far, corner_low, corner_high], axis=dim), results


def gather_rows(local, axis):
    mine, _ = gather_side(local, axis)
    return [mine, swap(mine, 1, axis)]


def pair_sum(mine, arrived, axis):
    pair = (mine.astype(jnp.float32) + arrived.astype(jnp.float32)).astype(jnp.bfloat16)
    return pair.reshape(pair.shape[:-2] + (lax.axis_size(axis) // 2, -1, pair.shape[-1]))


def halves_of(pair):
    half = pair.shape[-2] // 2
    return pair[..., :half, :], pair[..., half:, :]


def for_links(pair):
    low, high = halves_of(pair)
    near = jnp.stack([low[..., 1, :, :], low[..., 3, :, :]])
    return near, jnp.stack([high[..., 2, :, :], high[..., 3, :, :]])


def send_links(sent, axis):
    return swap(sent[0], 2, axis), swap(sent[1], 4, axis)


def send_last(pair, near, far, axis):
    low, high = halves_of(pair)
    last_far = (low[..., 2, :, :].astype(jnp.float32) + near[1].astype(jnp.float32)).astype(jnp.bfloat16)
    last_near = (high[..., 1, :, :].astype(jnp.float32) + far[1].astype(jnp.float32)).astype(jnp.bfloat16)
    return swap(last_far, 4, axis), swap(last_near, 2, axis)


def total_of(pair, near, far, last_far, last_near):
    f32 = jnp.float32
    low, high = halves_of(pair)
    low = low[..., 0, :, :].astype(f32) + near[0].astype(f32) + last_far.astype(f32)
    high = high[..., 0, :, :].astype(f32) + far[0].astype(f32) + last_near.astype(f32)
    return jnp.concatenate([low, high], axis=-2)


def sum_pieces(mine, others, axis):
    pair = pair_sum(mine, swap(others.astype(jnp.bfloat16), 1, axis), axis)
    if lax.axis_size(axis) != 8:
        total = pair[0].astype(jnp.float32)
        for k in range(1, lax.axis_size(axis) // 2):
            total = total + swap(pair[k], 2 * k, axis).astype(jnp.float32)
        return (total,)
    near, far = send_links(for_links(pair), axis)
    return (pair, near, far, *send_last(pair, near, far, axis))


def per_device(
    inputs,
    segments,
    cotangent,
    triple_weight,
    output_weight,
    gate_weight,
    down_weight,
    vector_params,
    triple_moment,
    output_moment,
    gate_moment,
    down_moment,
    vector_moment,
    triple_square,
    output_square,
    gate_square,
    down_square,
    vector_square,
):
    bf16, f32 = jnp.bfloat16, jnp.float32
    line, count = lax.axis_size("dp"), lax.axis_size("mp")
    rank = lax.axis_index("mp")
    tokens, width = inputs.shape
    head_width = triple_weight.shape[2]
    slab = triple_weight.shape[1]
    half = down_weight.shape[0] // 2
    row_segments = segments[0]
    seq_length = row_segments.shape[0]
    side = seq_length // 2

    heads_low = jnp.concatenate(
        [triple_weight[p].astype(bf16).T for p in range(3)] + [output_weight.astype(bf16)], axis=0
    )
    heads_full = lax.all_gather(heads_low, "dp", axis=1, tiled=True)
    triple_full, output_full = heads_full[: 3 * head_width], heads_full[3 * head_width :]
    cotangent_swapped = swap(cotangent, 1, "dp")

    def first_rows(inputs, params, row_segments):
        normed = normalize(inputs.astype(f32), params[0], params[1]).astype(bf16)
        return jnp.concatenate(gather_rows(normed, "mp"), axis=0), rotary_lanes(row_segments, head_width)

    normed_one, tables = island(first_rows, inputs, vector_params, row_segments)

    gate_low = gate_weight.astype(bf16).swapaxes(1, 2).reshape(2, 2, half, slab)
    down_low = down_weight.astype(bf16).reshape(2, half, slab)
    feed_halves = [jnp.concatenate([gate_low[0, h], gate_low[1, h], down_low[h]], axis=0) for h in range(2)]
    cotangent_pair = hold(jnp.stack([cotangent_swapped, cotangent]), normed_one)

    def cotangent_side(pair):
        return gather_side(pair, "mp")[0].reshape(-1, width)

    cotangent_mine = island(cotangent_side, cotangent_pair)
    cotangent_sides = [cotangent_mine, swap(cotangent_mine, 1, "mp")]
    feed_sent = hold(hold(jnp.stack(feed_halves * (line // 2)), cotangent_mine), heads_full)
    feed_weights = exchange(feed_sent, "dp")

    bias_rows = lax.dynamic_slice_in_dim(vector_params[4:7], rank * head_width, head_width, 1)
    across = (((1,), (1,)), ((), ()))
    down = (((0,), (0,)), ((), ()))
    mixed_rows, queries, keys, values, logsum = attend(
        rank, count, normed_one, heads_full, bias_rows.reshape(1, 3 * head_width), tables, row_segments, feed_sent
    )

    def second_rows(mixed_rows, output_full, inputs, params):
        parts = [
            jnp.dot(part, output_full, preferred_element_type=f32)
            for part in (mixed_rows[:side], mixed_rows[side:])
        ]
        return norm_sum(inputs, sum_pieces(*parts, "mp"), params[2], params[3])

    hidden, normed_two = island(second_rows, mixed_rows, output_full, inputs, vector_params)
    normed_swapped = swap(normed_two, 1, "dp")
    rows_own = island(lambda normed: gather_rows(normed, "mp"), normed_two)


    def other_rows(normed, rows_own, cotangent_sides, feed_weights):
        mine, results = gather_side(normed, "mp", lambda: feed(rows_own, cotangent_sides, 1, feed_weights))
        return [mine, swap(mine, 1, "mp")], results

    rows_other, own_results = island(other_rows, normed_swapped, rows_own, cotangent_sides, feed_weights)
    other_results = feed(rows_other, cotangent_sides, 0, feed_weights)
    activated, gate_up_grad = [(other_results[k], own_results[k]) for k in range(2)]
    normed_parts, feed_parts = [
        (other_results[k], own_results[k], other_results[k + 1], own_results[k + 1]) for k in (2, 4)
    ]

    def down_product(activated, cotangent_sides):
        return products(activated, [(cotangent_sides[k], row) for row in range(2) for k in range(2)], line)

    def gate_product(gate_up_grad, rows_other, rows_own):
        return products(gate_up_grad, [(array, 0) for array in (*rows_other, *rows_own)], line)

    if count == 8:
        def first_stage(parts, activated, cotangent_sides):
            arrived = swap(parts[2], 1, "mp")
            other_pair, *sent = pair_links(parts[0], arrived)
            near, far = send_links(sent, "mp")
            own_pair, *own_sent = pair_links(parts[1], swap(tie(parts[3], arrived), 1, "mp"))
            down_sent = down_product((hold(activated[0], other_pair), activated[1]), cotangent_sides)
            return other_pair, near, far, own_pair, own_sent, down_sent

        other_pair, other_near, other_far, own_pair, own_sent, down_sent = island(
            first_stage, normed_parts, activated, cotangent_sides
        )
        down_parts = exchange(down_sent, "dp")

        def second_stage(
            other_pair, other_near, other_far, own_pair, own_sent, gate_up_grad, rows_other, rows_own, parts
        ):
            last = send_last(other_pair, other_near, other_far, "mp")
            near, far = send_links(own_sent, "mp")
            normed_other = total_of(other_pair, other_near, other_far, *last).astype(bf16)
            normed_back = swap(normed_other, 1, "dp")
            units = (hold(gate_up_grad[0], normed_other), gate_up_grad[1])
            gate_sent = gate_product(units, rows_other, rows_own)
            near, far = hold(near, gate_sent), hold(far, gate_sent)
            own_last = send_last(own_pair, near, far, "mp")
            arrived = [swap(tie(parts[k + 2], last), 1, "mp") for k in range(2)]
            feed_pair = pair_links(hold(parts[0], near), arrived[0])
            return normed_back, (own_pair, near, far, *own_last), gate_sent, feed_pair, arrived[1]

        normed_back, own_pieces, gate_sent, feed_pair, feed_arrived = island(
            second_stage,
            hold(other_pair, down_sent),
            other_near,
            other_far,
            own_pair,
            own_sent,
            gate_up_grad,
            rows_other,
            rows_own,
            feed_parts,
        )
        gate_sent = hold(gate_sent, down_parts)

        def attention_rows(normed_back, pieces, hidden, cotangent, params):
            hidden_grad, hidden_grad_low, gain_grad, offset_grad = norm_back(
                hidden, pieces, cotangent, params[2], normed_back
            )
            sides = gather_rows(hidden_grad_low, "mp")
            return hidden_grad, gain_grad, offset_grad, jnp.concatenate(sides, axis=0)

        hidden_grad, gain_two_grad, offset_two_grad, attention_full = island(
            attention_rows, hold(normed_back, gate_sent), own_pieces, hidden, cotangent, vector_params
        )
    else:
        normed_back = swap(sum_pieces(normed_parts[0], normed_parts[2], "mp")[0].astype(bf16), 1, "dp")
        own_pieces = sum_pieces(normed_parts[1], normed_parts[3], "mp")
        down_parts = exchange(down_product(activated, cotangent_sides), "dp")
        gate_sent = hold(gate_product(gate_up_grad, rows_other, rows_own), down_parts)
        hidden_grad, hidden_grad_low, gain_two_grad, offset_two_grad = norm_back(
            hidden, own_pieces, cotangent, vector_params[2], normed_back
        )
        attention_full = jnp.concatenate(gather_rows(hidden_grad_low, "mp"), axis=0)
    gate_parts = exchange(gate_sent, "dp")
    def attention_back(attention_full, output_full, queries, keys, values, logsum, tables, row_segments, other_sent):
        links = send_links(other_sent, "mp") if count == 8 else ()
        mixed_grad = lax.dot_general(attention_full, output_full, across, preferred_element_type=f32).astype(bf16)
        results = attend_back(rank, count, queries, keys, values, mixed_grad, logsum, tables, row_segments)
        return *results, links

    raw_grad, bias_grad, other_links = island(
        attention_back,
        attention_full,
        output_full,
        queries,
        keys,
        values,
        logsum,
        tables,
        row_segments,
        feed_pair[1:] if count == 8 else (),
    )
    heads_sent = hold(heads_grad(normed_one, raw_grad, attention_full, mixed_rows), gate_parts)
    heads_total = lax.psum_scatter(heads_sent, "dp", scatter_dimension=1, tiled=True)
    stages = (("dp", line, 1), ("mp", count // 2, 2), ("mp", 2, 1))

    def last_sums(raw_grad, triple_full, feed, inputs, hidden, hidden_grad, params):
        parts = [
            jnp.dot(part, triple_full, preferred_element_type=f32)
            for part in (raw_grad[:side], raw_grad[side:])
        ]
        input_grad, _, gain_grad, offset_grad = norm_back(inputs, sum_pieces(*parts, "mp"), hidden_grad, params[0])
        if count == 8:
            other_pair, links, mine, arrived = feed
            own_pair, *sent = pair_links(mine, arrived)
            other_sum = total_of(other_pair, *links, *send_last(other_pair, *links, "mp"))
            links = send_links(sent, "mp")
            own_sum = total_of(own_pair, *links, *send_last(own_pair, *links, "mp"))
        else:
            other_sum, own_sum = [sum_pieces(feed[k], feed[k + 2], "mp")[0] for k in range(2)]
        return input_grad, gain_grad, offset_grad, hidden + own_sum, other_sum.astype(bf16)

    input_grad, gain_one_grad, offset_one_grad, own_output, feed_other = island(
        last_sums,
        hold(raw_grad, heads_sent),
        triple_full,
        (feed_pair[0], other_links, feed_parts[1], feed_arrived) if count == 8 else feed_parts,
        inputs,
        hidden,
        hidden_grad,
        vector_params,
    )
    heads_total = hold(heads_total, input_grad)
    feed_back = swap(feed_other, 1, "dp")

    gate_grads = gate_parts.reshape(-1, 2, 2 * half, slab)
    down_grads = down_parts.reshape(-1, 2, half, slab)

    def squares_of(parts):
        return jnp.sum(jnp.square(jnp.sum(parts.astype(f32), axis=0)))

    local_squares = squares_of(gate_grads) + squares_of(down_grads) + squares_of(heads_total[None])
    bias_full = lax.dynamic_update_slice_in_dim(
        jnp.zeros((3, width), f32), bias_grad.reshape(3, head_width), rank * head_width, 1
    )
    squares_row = jnp.broadcast_to(local_squares, (1, width))
    vector_part = jnp.concatenate(
        [gain_one_grad, offset_one_grad, gain_two_grad, offset_two_grad, bias_full, squares_row], axis=0
    )
    summed = sum_everywhere(vector_part, stages)
    vector_total = summed[:7]
    square_total = summed[7, 0] + jnp.sum(vector_total * vector_total)
    grad_norm = jnp.sqrt(square_total)
    factor = jnp.minimum(1.0, clip_limit / (grad_norm + 1e-06))
    gate_results, down_results, triple_results, output_results = adam(
        factor,
        [
            (
                [array.swapaxes(1, 2).reshape(4, half, slab) for array in (gate_weight, gate_moment, gate_square)],
                gate_grads,
                lambda i: (0, i % 2, i // 2, 0),
                matrix_rate,
                False,
            ),
            (
                [array.reshape(2, half, slab) for array in (down_weight, down_moment, down_square)],
                down_grads,
                lambda i: (0, i, 0, 0),
                matrix_rate,
                False,
            ),
            (
                [triple_weight, triple_moment, triple_square],
                heads_total[None],
                lambda i: (0, i, 0),
                matrix_rate,
                True,
            ),
            (
                [array[None] for array in (output_weight, output_moment, output_square)],
                heads_total[None],
                lambda i: (0, 3, 0),
                output_rate,
                False,
            ),
        ],
    )
    results = [
        triple_results,
        tuple(array[0] for array in output_results),
        tuple(array.reshape(2, 2 * half, slab).swapaxes(1, 2) for array in gate_results),
        tuple(array.reshape(2 * half, slab) for array in down_results),
        adam_step(vector_params, vector_moment, vector_square, vector_total, factor, vector_rate, 0.0),
    ]
    block_output = (own_output + hold(feed_back, gate_results[0]).astype(f32)).astype(bf16)
    return (
        (block_output, input_grad, grad_norm)
        + tuple(result[0] for result in results)
        + tuple(result[1] for result in results)
        + tuple(result[2] for result in results)
        + (vector_total[4],)
    )


def solution(mesh):
    in_specs = (
        P(("dp", "mp"), None),
        P("dp", None),
        P(("dp", "mp"), None),
        P(None, "dp", "mp"),
        P("mp", "dp"),
        P(None, "dp", "mp"),
        P("mp", "dp"),
        P(),
        P(None, "dp", "mp"),
        P("mp", "dp"),
        P(None, "dp", "mp"),
        P("mp", "dp"),
        P(),
        P(None, "dp", "mp"),
        P("mp", "dp"),
        P(None, "dp", "mp"),
        P("mp", "dp"),
        P(),
    )
    out_specs = (
        P(("dp", "mp"), None),
        P(("dp", "mp"), None),
        P(),
        P(None, "dp", "mp"),
        P("mp", "dp"),
        P(None, "dp", "mp"),
        P("mp", "dp"),
        P(),
        P(None, "dp", "mp"),
        P("mp", "dp"),
        P(None, "dp", "mp"),
        P("mp", "dp"),
        P(),
        P(None, "dp", "mp"),
        P("mp", "dp"),
        P(None, "dp", "mp"),
        P("mp", "dp"),
        P(),
        P(),
    )
    return jax.shard_map(
        per_device, mesh=mesh, in_specs=in_specs, out_specs=out_specs, check_vma=False
    )
```

```python
import functools

import jax
import jax.numpy as jnp
from jax import lax
from jax.experimental import pallas as pl
from jax.experimental.pallas import tpu as pltpu
from jax.sharding import PartitionSpec as P

HEAD_SIZE = 64
ROTARY = 16
STEP = 5


norm_eps = 1e-05
rotary_base = 10000.0
clip_limit = 1.0
first_decay = 0.9
second_decay = 0.95
adam_eps = 1e-08
matrix_rate = 0.03
output_rate = 0.2
vector_rate = 0.5
weight_decay = 0.1
masked_score = -1e30


def normalize(values, gain_row, offset_row):
    center = values - jnp.mean(values, axis=-1, keepdims=True)
    spread = jnp.mean(center * center, axis=-1, keepdims=True)
    return center * lax.rsqrt(spread + norm_eps) * gain_row + offset_row


def positions_of(row_segments):
    length = row_segments.shape[0]
    loop_counter = jnp.arange(length, dtype=jnp.int32)
    earlier = jnp.concatenate([jnp.full((1,), -1, jnp.int32), row_segments[:-1]])
    starts = jnp.where(row_segments != earlier, loop_counter, jnp.zeros_like(loop_counter))
    return loop_counter - lax.cummax(starts, axis=0)


def rotary_tables(positions, rotary):
    half_width = rotary // 2
    frequency = rotary_base ** (-2.0 * jnp.arange(half_width, dtype=jnp.float32) / rotary)
    angles = positions.astype(jnp.float32)[:, None] * frequency[None, :]
    return (jnp.cos(angles), jnp.sin(angles))


def adam_step(master, moment, square, grad, factor, rate, decay):
    clipped = grad * factor
    first_new = first_decay * moment + (1.0 - first_decay) * clipped
    second_new = second_decay * square + (1.0 - second_decay) * clipped * clipped
    first_hat = first_new / (1.0 - first_decay**STEP)
    second_hat = second_new / (1.0 - second_decay**STEP)
    updated = master - rate * (first_hat / (jnp.sqrt(second_hat) + adam_eps) + decay * master)
    return (updated, first_new, second_new)


def rotary_lanes(row_segments, width):
    cosine_table, sine_table = rotary_tables(positions_of(row_segments), ROTARY)
    half = ROTARY // 2
    lanes = jnp.arange(width) % HEAD_SIZE
    own = (lanes % half)[None, :] == jnp.arange(half)[:, None]
    turning = lanes < ROTARY
    plain = jnp.where(own & turning, 1.0, 0.0)
    ahead = jnp.where(own & (lanes < half), -1.0, 0.0)
    behind = jnp.where(own & turning & (lanes >= half), 1.0, 0.0)
    nothing = jnp.zeros_like(plain)
    rest = jnp.where(turning, 0.0, 1.0)[None, :]
    spread = jnp.concatenate(
        [
            jnp.concatenate([plain, nothing, nothing], axis=1),
            jnp.concatenate([nothing, ahead, behind], axis=1),
            jnp.concatenate([rest, jnp.zeros((1, 2 * width))], axis=1),
        ],
        axis=0,
    )
    factors = jnp.concatenate([cosine_table, sine_table, jnp.ones_like(cosine_table[:, :1])], axis=1)
    return jnp.dot(factors, spread, precision=lax.Precision.HIGHEST, preferred_element_type=jnp.float32)


def spot(rank, number, count, size):
    bits = jnp.bitwise_xor(rank, number)
    place = jnp.bitwise_and(bits, 1) * (count // 2) + jnp.right_shift(bits, 1)
    return pl.multiple_of(place * size, size)


def attend_kernel(rows, heads, scale, count, rank_ref, normed_ref, weight_ref, bias_ref, tables_ref, seg_col_ref, seg_row_ref,
                  before_ref, out_ref, q_ref, k_ref, v_ref, lse_ref, raw_ref):
    length, width = q_ref.shape
    size = length // count
    rank = rank_ref[0, 0]
    for start in range(0, length, rows):
        raw_ref[start : start + rows, :] = lax.dot_general(
            normed_ref[start : start + rows, :],
            weight_ref[...],
            (((1,), (1,)), ((), ())),
            preferred_element_type=jnp.float32,
        )
    for number in range(count):
        here = slice(number * size, (number + 1) * size)
        there = pl.ds(spot(rank, number, count, size), size)
        plain, ahead, behind = [tables_ref[here, k * width : (k + 1) * width] for k in range(3)]
        for part, low_ref in enumerate((q_ref, k_ref)):
            lanes = slice(part * width, (part + 1) * width)
            value = raw_ref[there, lanes] + bias_ref[:, lanes]
            turned = (
                value * plain
                + pltpu.roll(value, width - ROTARY // 2, 1) * ahead
                + pltpu.roll(value, ROTARY // 2, 1) * behind
            ).astype(jnp.bfloat16)
            low_ref[here, :] = turned * jnp.bfloat16(scale) if part == 0 else turned
        lanes = slice(2 * width, 3 * width)
        v_ref[here, :] = (raw_ref[there, lanes] + bias_ref[:, lanes]).astype(jnp.bfloat16)
    for start in range(0, length, rows):
        stop = start + rows
        allowed = (seg_col_ref[start:stop, :] == seg_row_ref[:, :stop]) & (
            lax.broadcasted_iota(jnp.int32, (rows, stop), 1)
            <= lax.broadcasted_iota(jnp.int32, (rows, stop), 0) + start
        )
        outs, logs = [], []
        for head in range(heads):
            lanes = slice(head * HEAD_SIZE, (head + 1) * HEAD_SIZE)
            scores = lax.dot_general(
                q_ref[start:stop, lanes], k_ref[:stop, lanes], (((1,), (1,)), ((), ())),
                preferred_element_type=jnp.float32,
            )
            masked = jnp.where(allowed, scores, masked_score)
            largest = jnp.max(masked, axis=-1, keepdims=True)
            powers = jnp.exp(masked - largest)
            totals = jnp.sum(powers, axis=-1, keepdims=True)
            soft_low = (powers * (1.0 / totals)).astype(jnp.bfloat16)
            outs.append(jnp.dot(soft_low, v_ref[:stop, lanes], preferred_element_type=jnp.float32))
            logs.append(largest + jnp.log(totals))
        mixed = jnp.concatenate(outs, axis=1).astype(jnp.bfloat16)
        for low in range(0, rows, size):
            out_ref[pl.ds(spot(rank, (start + low) // size, count, size), size), :] = mixed[low : low + size]
        lse_ref[start:stop, :] = jnp.concatenate(logs, axis=1)


def attend(rank, count, normed, weights, bias, tables, row_segments, before):
    length, features = normed.shape
    width = weights.shape[0] // 4
    heads = width // HEAD_SIZE
    rows = min(256, length)
    low = jax.ShapeDtypeStruct((length, width), jnp.bfloat16)

    def whole(shape):
        return pl.BlockSpec(shape, lambda i: (0,) * len(shape))

    return pl.pallas_call(
        functools.partial(attend_kernel, rows, heads, HEAD_SIZE ** (-0.5), count),
        grid=(1,),
        in_specs=[
            pl.BlockSpec(memory_space=pltpu.SMEM),
            whole((length, features)),
            whole((3 * width, features)),
            whole((1, 3 * width)),
        ]
        + [whole((length, 3 * width)), whole((length, 1)), whole((1, length)), pl.BlockSpec(memory_space=pl.ANY)],
        out_specs=[whole((length, width))] * 4 + [whole((length, heads))],
        scratch_shapes=[pltpu.VMEM((length, 3 * width), jnp.float32)],
        out_shape=(low, low, low, low, jax.ShapeDtypeStruct((length, heads), jnp.float32)),
        compiler_params=pltpu.CompilerParams(vmem_limit_bytes=60 << 20),
        cost_estimate=pl.CostEstimate(
            flops=4 * length * length * width + 6 * length * width * features, bytes_accessed=20 * length * width,
            transcendentals=length * length * heads,
        ),
        name="attend",
    )(rank.reshape(1, 1), normed, weights, bias, tables, row_segments[:, None], row_segments[None, :], before)


def attend_back_kernel(rows, heads, scale, count, rank_ref, q_ref, k_ref, v_ref, grad_ref, lse_ref, tables_ref,
                       seg_col_ref, seg_row_ref, raw_ref, bias_ref, g_ref, dk_ref, dv_ref):
    length, width = q_ref.shape
    size = length // count
    rank = rank_ref[0, 0]
    for number in range(count):
        there = pl.ds(spot(rank, number, count, size), size)
        g_ref[number * size : (number + 1) * size, :] = grad_ref[there, :]

    def put(start, stop, part, value):
        here = slice(start, stop)
        if part < 2:
            value = (
                value * tables_ref[here, :width]
                - pltpu.roll(value, width - ROTARY // 2, 1) * tables_ref[here, width : 2 * width]
                - pltpu.roll(value, ROTARY // 2, 1) * tables_ref[here, 2 * width :]
            )
        low = value.astype(jnp.bfloat16)
        lanes = slice(part * width, (part + 1) * width)
        for number in range(start // size, stop // size):
            there = pl.ds(spot(rank, number, count, size), size)
            raw_ref[there, lanes] = low[number * size - start : (number + 1) * size - start]
        bias_ref[:, lanes] += jnp.sum(low.astype(jnp.float32), axis=0, keepdims=True)

    bias_ref[...] = jnp.zeros_like(bias_ref)
    for start in reversed(range(0, length, rows)):
        stop = start + rows
        allowed = (seg_col_ref[:stop, :] == seg_row_ref[:, start:stop]) & (
            lax.broadcasted_iota(jnp.int32, (stop, rows), 0)
            <= lax.broadcasted_iota(jnp.int32, (stop, rows), 1) + start
        )
        query_grads, key_grads, value_grads = [], [], []
        for head in range(heads):
            lanes = slice(head * HEAD_SIZE, (head + 1) * HEAD_SIZE)
            q, g = q_ref[start:stop, lanes], g_ref[start:stop, lanes]
            k, v = k_ref[:stop, lanes], v_ref[:stop, lanes]
            across = (((1,), (1,)), ((), ()))
            scores = lax.dot_general(k, q, across, preferred_element_type=jnp.float32)
            soft = jnp.exp(
                jnp.where(allowed, scores - lse_ref[head:head + 1, start:stop], masked_score)
            )
            soft_grad = lax.dot_general(v, g, across, preferred_element_type=jnp.float32)
            inner = jnp.sum(soft * soft_grad, axis=0, keepdims=True)
            score_grad = (soft * (soft_grad - inner)).astype(jnp.bfloat16)
            soft_low = soft.astype(jnp.bfloat16)
            value_grads.append(jnp.dot(soft_low, g, preferred_element_type=jnp.float32))
            key_grads.append(jnp.dot(score_grad, q, preferred_element_type=jnp.float32))
            query_grads.append(lax.dot_general(
                score_grad, k, (((0,), (0,)), ((), ())), preferred_element_type=jnp.float32
            ))
        put(start, stop, 0, jnp.concatenate(query_grads, axis=1) * scale)
        key_grad = jnp.concatenate(key_grads, axis=1)
        value_grad = jnp.concatenate(value_grads, axis=1)
        if stop == length:
            dk_ref[...] = key_grad
            dv_ref[...] = value_grad
        else:
            dk_ref[:stop, :] += key_grad
            dv_ref[:stop, :] += value_grad
        put(start, stop, 1, dk_ref[start:stop, :])
        put(start, stop, 2, dv_ref[start:stop, :])


def attend_back(rank, count, queries, keys, values, mixed_grad, logsum, tables, row_segments):
    length, width = queries.shape
    heads = width // HEAD_SIZE
    rows = min(512, length)
    return pl.pallas_call(
        functools.partial(attend_back_kernel, rows, heads, HEAD_SIZE ** (-0.5), count),
        in_specs=[pl.BlockSpec(memory_space=pltpu.SMEM)] + [pl.BlockSpec(memory_space=pltpu.VMEM)] * 8,
        out_shape=(
            jax.ShapeDtypeStruct((length, 3 * width), jnp.bfloat16),
            jax.ShapeDtypeStruct((1, 3 * width), jnp.float32),
        ),
        scratch_shapes=[pltpu.VMEM((length, width), jnp.bfloat16)] + [pltpu.VMEM((length, width), jnp.float32)] * 2,
        compiler_params=pltpu.CompilerParams(vmem_limit_bytes=48 << 20),
        cost_estimate=pl.CostEstimate(
            flops=10 * length * length * width, bytes_accessed=30 * length * width,
            transcendentals=length * length * heads,
        ),
        name="attend_back",
    )(
        rank.reshape(1, 1), queries, keys, values, mixed_grad, logsum.T, tables,
        row_segments[:, None], row_segments[None, :],
    )


def adam_kernel(sections, factor_ref, *refs):
    in_refs, out_refs = refs[: 4 * len(sections)], refs[4 * len(sections) :]
    for k, (start, stop, rate, turned) in enumerate(sections):
        *state_refs, parts_ref = in_refs[4 * k : 4 * k + 4]
        results = out_refs[3 * k : 3 * k + 3]

        @pl.when((pl.program_id(0) >= start) & (pl.program_id(0) < stop))
        def _(state_refs=state_refs, parts_ref=parts_ref, results=results, rate=rate, turned=turned):
            grad = jnp.sum(parts_ref[...].reshape((-1,) + parts_ref.shape[-2:]).astype(jnp.float32), axis=0)
            if turned:
                grad = grad.T
            values = adam_step(*(ref[0] for ref in state_refs), grad, factor_ref[0, 0], rate, weight_decay)
            for result, value in zip(results, values):
                result[0] = value


def adam(factor, groups):
    sections, operands, in_specs, out_specs, out_shape = [], [], [], [], []
    start = 0
    for state, parts, place, rate, turned in groups:
        number, rows, width = state[0].shape

        def index(i, start=start, number=number):
            return jnp.clip(i - start, 0, number - 1)

        spec = pl.BlockSpec((1, rows, width), lambda i, index=index: (index(i), 0, 0))
        block = (width, rows) if turned else (rows, width)
        parts_spec = pl.BlockSpec(
            parts.shape[:1] + (1,) * (parts.ndim - 3) + block, lambda i, index=index, place=place: place(index(i))
        )
        sections.append((start, start + number, rate, turned))
        operands += [*state, parts]
        in_specs += [spec] * 3 + [parts_spec]
        out_specs += [spec] * 3
        out_shape += [jax.ShapeDtypeStruct(state[0].shape, jnp.float32)] * 3
        start += number
    size = sum(shape.size for shape in out_shape) // 3
    results = pl.pallas_call(
        functools.partial(adam_kernel, sections),
        grid=(start,),
        in_specs=[pl.BlockSpec(memory_space=pltpu.SMEM)] + in_specs,
        out_specs=out_specs,
        out_shape=out_shape,
        compiler_params=pltpu.CompilerParams(vmem_limit_bytes=60 << 20),
        cost_estimate=pl.CostEstimate(flops=20 * size, bytes_accessed=28 * size, transcendentals=0),
        name="adam",
    )(factor.reshape(1, 1), *operands)
    return [tuple(results[3 * k : 3 * k + 3]) for k in range(len(groups))]


def feed_kernel(rows_ref, other_rows_ref, grad_rows_ref, other_grad_rows_ref, weight_ref, activated_ref, grad_ref,
                back_ref, other_back_ref, out_ref, other_out_ref, back_tile, out_tile):
    line, _, slab = weight_ref.shape
    half = activated_ref.shape[0]
    across = (((1,), (1,)), ((), ()))
    mine = pl.program_id(0) < pl.num_programs(0) // 2
    gate_up, activated_grad = 0.0, 0.0
    for z in range(line):
        columns = slice(z * slab, (z + 1) * slab)
        gate_up += lax.dot_general(
            weight_ref[z, : 2 * half, :],
            jnp.where(mine, rows_ref[:, columns], other_rows_ref[:, columns]),
            across,
            preferred_element_type=jnp.float32,
        )
        activated_grad += lax.dot_general(
            weight_ref[z, 2 * half :, :],
            jnp.where(mine, grad_rows_ref[:, columns], other_grad_rows_ref[:, columns]),
            across,
            preferred_element_type=jnp.float32,
        )
    gate, up = gate_up[:half], gate_up[half:]
    sigmoid_gate = jax.nn.sigmoid(gate)
    silu_gate = gate * sigmoid_gate
    activated = (silu_gate * up).astype(jnp.bfloat16)
    slope = sigmoid_gate * (1.0 + gate * (1.0 - sigmoid_gate))
    activated_ref[...] = activated
    grad_ref[:half, :] = (activated_grad * up * slope).astype(jnp.bfloat16)
    grad_ref[half:, :] = (activated_grad * silu_gate).astype(jnp.bfloat16)
    down = (((0,), (0,)), ((), ()))
    for z in range(line):
        columns = slice(z * slab, (z + 1) * slab)
        back_tile[:, columns] = lax.dot_general(
            grad_ref[...], weight_ref[z, : 2 * half, :], down, preferred_element_type=jnp.float32
        ).astype(jnp.bfloat16)
        out_tile[:, columns] = lax.dot_general(
            activated, weight_ref[z, 2 * half :, :], down, preferred_element_type=jnp.float32
        ).astype(jnp.bfloat16)

    @pl.when(mine)
    def _():
        back_ref[...] = back_tile[...]
        out_ref[...] = out_tile[...]

    @pl.when(jnp.logical_not(mine))
    def _():
        other_back_ref[...] = back_tile[...]
        other_out_ref[...] = out_tile[...]


def feed(sides, cotangent_sides, row, weights):
    length, width = sides[0].shape
    line, units, slab = weights.shape
    half = units // 3
    tile = min(512, length)
    steps = length // tile

    def first(i):
        return jnp.minimum(i, steps - 1)

    def second(i):
        return jnp.maximum(i - steps, 0)

    low = jnp.bfloat16
    two_sides = [pl.BlockSpec((tile, width), lambda i: (first(i), 0)), pl.BlockSpec((tile, width), lambda i: (second(i), 0))]
    return pl.pallas_call(
        feed_kernel,
        grid=(2 * steps,),
        in_specs=two_sides
        + [
            pl.BlockSpec((tile, width), lambda i: (row * steps + first(i), 0)),
            pl.BlockSpec((tile, width), lambda i: (row * steps + second(i), 0)),
            pl.BlockSpec(weights.shape, lambda i: (0, 0, 0)),
        ],
        out_specs=[
            pl.BlockSpec((half, tile), lambda i: (0, i)),
            pl.BlockSpec((2 * half, tile), lambda i: (0, i)),
        ]
        + two_sides * 2,
        out_shape=[
            jax.ShapeDtypeStruct((half, 2 * length), low),
            jax.ShapeDtypeStruct((2 * half, 2 * length), low),
        ]
        + [jax.ShapeDtypeStruct((length, width), low)] * 4,
        scratch_shapes=[pltpu.VMEM((tile, width), low)] * 2,
        compiler_params=pltpu.CompilerParams(vmem_limit_bytes=56 << 20),
        cost_estimate=pl.CostEstimate(
            flops=24 * length * width * half, bytes_accessed=20 * length * width, transcendentals=2 * length * half,
        ),
        name="feed",
    )(*sides, *cotangent_sides, weights)


def products_kernel(first_ref, second_ref, *refs):
    row_refs, more_refs, out_ref = refs[:4], refs[4:-1], refs[-1]
    height = first_ref.shape[0]
    size = row_refs[0].shape[0]
    total = 0.0
    for k, rows_ref in enumerate(row_refs):
        units_ref = (first_ref, second_ref)[k // 2]
        total += jnp.dot(
            units_ref[:, k % 2 * size : (k % 2 + 1) * size], rows_ref[...], preferred_element_type=jnp.float32
        )
    out_ref[0, :height] = total.astype(jnp.bfloat16)
    for more_ref in more_refs:
        out_ref[0, height:] = more_ref[0]


def products(units, row_blocks, count, *more):
    height, length = units[0].shape
    size = length // 2
    width = row_blocks[0][0].shape[1]
    slab = width // count
    total_height = height + sum(array.shape[1] for array in more)
    return pl.pallas_call(
        products_kernel,
        grid=(count,),
        in_specs=[pl.BlockSpec(units[0].shape, lambda i: (0, 0))] * 2
        + [pl.BlockSpec((size, slab), lambda i, row=row: (row, i)) for _, row in row_blocks]
        + [pl.BlockSpec((1,) + array.shape[1:], lambda i: (i, 0, 0)) for array in more],
        out_specs=pl.BlockSpec((1, total_height, slab), lambda i: (i, 0, 0)),
        out_shape=jax.ShapeDtypeStruct((count, total_height, slab), jnp.bfloat16),
        compiler_params=pltpu.CompilerParams(vmem_limit_bytes=56 << 20),
        cost_estimate=pl.CostEstimate(
            flops=4 * height * length * width, bytes_accessed=4 * length * width, transcendentals=0
        ),
        name="products",
    )(*units, *(array for array, _ in row_blocks), *more)


def heads_grad_kernel(normed_ref, raw_ref, attention_ref, mixed_ref, out_ref):
    down = (((0,), (0,)), ((), ()))
    cut = raw_ref.shape[1]
    for here, left_ref, right_ref in (
        (slice(0, cut), raw_ref, normed_ref),
        (slice(cut, out_ref.shape[0]), mixed_ref, attention_ref),
    ):
        out_ref[here, :] = lax.dot_general(
            left_ref[...], right_ref[...], down, preferred_element_type=jnp.float32
        ).astype(jnp.bfloat16)


def heads_grad(normed, raw_grad, attention, mixed):
    length, width = normed.shape
    columns = raw_grad.shape[1] + mixed.shape[1]
    tile = min(512, width)
    by_columns = pl.BlockSpec((length, tile), lambda i: (0, i))

    def whole(array):
        return pl.BlockSpec(array.shape, lambda i: (0, 0))

    return pl.pallas_call(
        heads_grad_kernel,
        grid=(width // tile,),
        in_specs=[by_columns, whole(raw_grad), by_columns, whole(mixed)],
        out_specs=pl.BlockSpec((columns, tile), lambda i: (0, i)),
        out_shape=jax.ShapeDtypeStruct((columns, width), jnp.bfloat16),
        compiler_params=pltpu.CompilerParams(vmem_limit_bytes=56 << 20),
        cost_estimate=pl.CostEstimate(
            flops=2 * length * width * columns, bytes_accessed=4 * length * width, transcendentals=0
        ),
        name="heads_grad",
    )(normed, raw_grad, attention, mixed)


def total_from(pair_ref, near_ref, far_ref, last_far_ref, last_near_ref):
    half = near_ref.shape[1]
    f32 = jnp.float32
    low = pair_ref[0, :half].astype(f32) + near_ref[0].astype(f32) + last_far_ref[...].astype(f32)
    high = pair_ref[0, half:].astype(f32) + far_ref[0].astype(f32) + last_near_ref[...].astype(f32)
    return jnp.concatenate([low, high], axis=0)


def total_specs(pieces):
    first = [pl.BlockSpec((1,) + piece.shape[1:], lambda i: (0, 0, 0)) for piece in pieces[:3]]
    return first + [whole_block(piece) for piece in pieces[3:]]


def whole_block(array):
    return pl.BlockSpec(array.shape, lambda i: (0,) * array.ndim)


def norm_sum_kernel(base_ref, gain_ref, offset_ref, *refs):
    *piece_refs, hidden_ref, normed_ref = refs
    total = total_from(*piece_refs) if len(piece_refs) > 1 else piece_refs[0][...]
    hidden = base_ref[...].astype(jnp.float32) + total
    hidden_ref[...] = hidden
    normed_ref[...] = normalize(hidden, gain_ref[...], offset_ref[...]).astype(jnp.bfloat16)


def norm_sum(base, pieces, gain, offset):
    rows, width = base.shape
    operands = (base, gain.reshape(1, width), offset.reshape(1, width))
    shapes = (jax.ShapeDtypeStruct((rows, width), jnp.float32), jax.ShapeDtypeStruct((rows, width), jnp.bfloat16))
    return pl.pallas_call(
        norm_sum_kernel,
        grid=(1,),
        in_specs=[whole_block(array) for array in operands]
        + (total_specs(pieces) if len(pieces) > 1 else [whole_block(pieces[0])]),
        out_specs=[whole_block(shape) for shape in shapes],
        out_shape=shapes,
        cost_estimate=pl.CostEstimate(flops=12 * rows * width, bytes_accessed=14 * rows * width, transcendentals=rows),
        name="norm_sum",
    )(*operands, *pieces)


def norm_back_kernel(more, values_ref, base_ref, gain_ref, *refs):
    *piece_refs, out_ref, low_ref, gain_grad_ref, offset_grad_ref = refs
    values = values_ref[...].astype(jnp.float32)
    if more:
        *piece_refs, more_ref = piece_refs
    grad = total_from(*piece_refs) if len(piece_refs) > 1 else piece_refs[0][...]
    if more:
        grad = grad + more_ref[...].astype(jnp.float32)
    center = values - jnp.mean(values, axis=-1, keepdims=True)
    scale = lax.rsqrt(jnp.mean(center * center, axis=-1, keepdims=True) + norm_eps)
    normal = center * scale
    inner = grad * gain_ref[...]
    inner_mean = jnp.mean(inner, axis=-1, keepdims=True)
    normal_mean = jnp.mean(inner * normal, axis=-1, keepdims=True)
    out = base_ref[...].astype(jnp.float32) + scale * (inner - inner_mean - normal * normal_mean)
    out_ref[...] = out
    low_ref[...] = out.astype(jnp.bfloat16)
    gain_grad_ref[...] = jnp.sum(grad * normal, axis=0, keepdims=True)
    offset_grad_ref[...] = jnp.sum(grad, axis=0, keepdims=True)


def norm_back(values, pieces, base, gain, *more):
    rows, width = values.shape
    operands = (values, base, gain.reshape(1, width))
    vector = jax.ShapeDtypeStruct((1, width), jnp.float32)
    shapes = (
        jax.ShapeDtypeStruct((rows, width), jnp.float32),
        jax.ShapeDtypeStruct((rows, width), jnp.bfloat16),
        vector,
        vector,
    )
    return pl.pallas_call(
        functools.partial(norm_back_kernel, len(more)),
        grid=(1,),
        in_specs=[whole_block(array) for array in operands]
        + (total_specs(pieces) if len(pieces) > 1 else [whole_block(pieces[0])])
        + [whole_block(array) for array in more],
        out_specs=[whole_block(shape) for shape in shapes],
        out_shape=shapes,
        cost_estimate=pl.CostEstimate(flops=20 * rows * width, bytes_accessed=16 * rows * width, transcendentals=rows),
        name="norm_back",
    )(*operands, *pieces, *more)


def pair_kernel(mine_ref, arrived_ref, pair_ref, near_ref, far_ref):
    chips, rows, _ = pair_ref.shape
    half = rows // 2
    for chip in range(chips):
        here = slice(chip * rows, (chip + 1) * rows)
        total = (mine_ref[here, :].astype(jnp.float32) + arrived_ref[here, :].astype(jnp.float32)).astype(jnp.bfloat16)
        pair_ref[chip] = total
        if chip % 2:
            near_ref[chip // 2] = total[:half]
        if chip > 1:
            far_ref[chip - 2] = total[half:]


def pair_links(mine, arrived):
    length, width = mine.shape
    rows = length // 4
    low = jnp.bfloat16
    return pl.pallas_call(
        pair_kernel,
        out_shape=(
            jax.ShapeDtypeStruct((4, rows, width), low),
            jax.ShapeDtypeStruct((2, rows // 2, width), low),
            jax.ShapeDtypeStruct((2, rows // 2, width), low),
        ),
        cost_estimate=pl.CostEstimate(flops=length * width, bytes_accessed=8 * length * width, transcendentals=0),
        name="pair_links",
    )(mine, arrived)


def tie(value, *others):
    return lax.optimization_barrier((value, others))[0]


def turns(count, step):
    return [(i, (i + step) % count) for i in range(count)]


def hold(value, *others):
    def kernel(*refs):
        pass

    anywhere = pl.BlockSpec(memory_space=pl.ANY)
    return pl.pallas_call(
        kernel,
        out_shape=jax.ShapeDtypeStruct(value.shape, value.dtype),
        in_specs=[anywhere] * (1 + len(others)),
        out_specs=anywhere,
        input_output_aliases={0: 0},
        name="hold",
    )(value, *others)


def island(function, *operands):
    index = lax.axis_index("dp") * lax.axis_size("mp") + lax.axis_index("mp")
    shapes = jax.eval_shape(function, *operands)

    def never(*operands):
        return jax.tree.map(lambda shape: jnp.zeros(shape.shape, shape.dtype), shapes)

    return lax.cond(index >= 0, function, never, *operands)


def exchange(blocks, axis):
    return lax.all_to_all(blocks, axis, split_axis=0, concat_axis=0)


def sum_everywhere(values, axes):
    for axis, count, bits in axes:
        place = lax.rem(lax.axis_index(axis) // bits, count)
        arrived = [values] + [swap(values, bits * k, axis) for k in range(1, count)]
        total = 0.0
        for j in range(count):
            total = total + sum(jnp.where(place == j ^ k, arrived[k], 0.0) for k in range(count))
        values = total
    return values


def swap(value, bits, axis):
    return lax.ppermute(value, axis, [(i, i ^ bits) for i in range(lax.axis_size(axis))])


def gather_side(local, axis, beside=lambda: ()):
    count = lax.axis_size(axis)
    dim = local.ndim - 2
    if count != 8:
        pieces = [local] + [swap(local, 2 * k, axis) for k in range(1, count // 2)]
        return jnp.concatenate(pieces, axis=dim), beside()
    rows = local.shape[dim] // 2
    near, far = swap(local, 2, axis), swap(local, 4, axis)
    results = beside()
    if results:
        near, far = hold(near, results[0]), hold(far, results[0])
    corner_low = swap(lax.slice_in_dim(near, 0, rows, axis=dim), 4, axis)
    corner_high = swap(lax.slice_in_dim(far, rows, 2 * rows, axis=dim), 2, axis)
    return jnp.concatenate([local, near, far, corner_low, corner_high], axis=dim), results


def gather_rows(local, axis):
    mine, _ = gather_side(local, axis)
    return [mine, swap(mine, 1, axis)]


def pair_sum(mine, arrived, axis):
    pair = (mine.astype(jnp.float32) + arrived.astype(jnp.float32)).astype(jnp.bfloat16)
    return pair.reshape(pair.shape[:-2] + (lax.axis_size(axis) // 2, -1, pair.shape[-1]))


def halves_of(pair):
    half = pair.shape[-2] // 2
    return pair[..., :half, :], pair[..., half:, :]


def for_links(pair):
    low, high = halves_of(pair)
    near = jnp.stack([low[..., 1, :, :], low[..., 3, :, :]])
    return near, jnp.stack([high[..., 2, :, :], high[..., 3, :, :]])


def send_links(sent, axis):
    return swap(sent[0], 2, axis), swap(sent[1], 4, axis)


def send_last(pair, near, far, axis):
    low, high = halves_of(pair)
    last_far = (low[..., 2, :, :].astype(jnp.float32) + near[1].astype(jnp.float32)).astype(jnp.bfloat16)
    last_near = (high[..., 1, :, :].astype(jnp.float32) + far[1].astype(jnp.float32)).astype(jnp.bfloat16)
    return swap(last_far, 4, axis), swap(last_near, 2, axis)


def total_of(pair, near, far, last_far, last_near):
    f32 = jnp.float32
    low, high = halves_of(pair)
    low = low[..., 0, :, :].astype(f32) + near[0].astype(f32) + last_far.astype(f32)
    high = high[..., 0, :, :].astype(f32) + far[0].astype(f32) + last_near.astype(f32)
    return jnp.concatenate([low, high], axis=-2)


def sum_pieces(mine, others, axis):
    pair = pair_sum(mine, swap(others.astype(jnp.bfloat16), 1, axis), axis)
    if lax.axis_size(axis) != 8:
        total = pair[0].astype(jnp.float32)
        for k in range(1, lax.axis_size(axis) // 2):
            total = total + swap(pair[k], 2 * k, axis).astype(jnp.float32)
        return (total,)
    near, far = send_links(for_links(pair), axis)
    return (pair, near, far, *send_last(pair, near, far, axis))


def per_device(
    inputs,
    segments,
    cotangent,
    triple_weight,
    output_weight,
    gate_weight,
    down_weight,
    vector_params,
    triple_moment,
    output_moment,
    gate_moment,
    down_moment,
    vector_moment,
    triple_square,
    output_square,
    gate_square,
    down_square,
    vector_square,
):
    bf16, f32 = jnp.bfloat16, jnp.float32
    line, count = lax.axis_size("dp"), lax.axis_size("mp")
    rank = lax.axis_index("mp")
    tokens, width = inputs.shape
    head_width = triple_weight.shape[2]
    slab = triple_weight.shape[1]
    half = down_weight.shape[0] // 2
    row_segments = segments[0]
    seq_length = row_segments.shape[0]
    side = seq_length // 2

    heads_low = jnp.concatenate(
        [triple_weight[p].astype(bf16).T for p in range(3)] + [output_weight.astype(bf16)], axis=0
    )
    heads_full = lax.all_gather(heads_low, "dp", axis=1, tiled=True)
    triple_full, output_full = heads_full[: 3 * head_width], heads_full[3 * head_width :]
    cotangent_swapped = swap(cotangent, 1, "dp")

    def first_rows(inputs, params, row_segments):
        normed = normalize(inputs.astype(f32), params[0], params[1]).astype(bf16)
        return jnp.concatenate(gather_rows(normed, "mp"), axis=0), rotary_lanes(row_segments, head_width)

    normed_one, tables = island(first_rows, inputs, vector_params, row_segments)

    def cotangent_side(cotangent_swapped, cotangent, gate_weight, down_weight):
        gate_low = gate_weight.astype(bf16).swapaxes(1, 2).reshape(2, 2, half, slab)
        down_low = down_weight.astype(bf16).reshape(2, half, slab)
        halves = [jnp.concatenate([gate_low[0, h], gate_low[1, h], down_low[h]], axis=0) for h in range(2)]
        side, _ = gather_side(jnp.stack([cotangent_swapped, cotangent]), "mp")
        return side.reshape(-1, width), jnp.stack(halves * (line // 2))

    cotangent_mine, feed_sent = island(
        cotangent_side, hold(cotangent_swapped, normed_one), cotangent, gate_weight, down_weight
    )
    feed_weights = exchange(feed_sent, "dp")
    cotangent_sides = [cotangent_mine, swap(cotangent_mine, 1, "mp")]

    bias_rows = lax.dynamic_slice_in_dim(vector_params[4:7], rank * head_width, head_width, 1)
    across = (((1,), (1,)), ((), ()))
    down = (((0,), (0,)), ((), ()))
    mixed_rows, queries, keys, values, logsum = attend(
        rank, count, normed_one, heads_full, bias_rows.reshape(1, 3 * head_width), tables, row_segments, feed_sent
    )

    def second_rows(mixed_rows, output_full, inputs, params):
        parts = [
            jnp.dot(part, output_full, preferred_element_type=f32)
            for part in (mixed_rows[:side], mixed_rows[side:])
        ]
        return norm_sum(inputs, sum_pieces(*parts, "mp"), params[2], params[3])

    hidden, normed_two = island(second_rows, mixed_rows, output_full, inputs, vector_params)
    normed_swapped = swap(normed_two, 1, "dp")
    rows_own = island(lambda normed: gather_rows(normed, "mp"), normed_two)


    def other_rows(normed, rows_own, cotangent_sides, feed_weights):
        mine, results = gather_side(normed, "mp", lambda: feed(rows_own, cotangent_sides, 1, feed_weights))
        return [mine, swap(mine, 1, "mp")], results

    rows_other, own_results = island(other_rows, normed_swapped, rows_own, cotangent_sides, feed_weights)
    other_results = feed(rows_other, cotangent_sides, 0, feed_weights)
    activated, gate_up_grad = [(other_results[k], own_results[k]) for k in range(2)]
    normed_parts, feed_parts = [
        (other_results[k], own_results[k], other_results[k + 1], own_results[k + 1]) for k in (2, 4)
    ]

    def down_product(activated, cotangent_sides):
        return products(activated, [(cotangent_sides[k], row) for row in range(2) for k in range(2)], line)

    def gate_product(gate_up_grad, rows_other, rows_own):
        return products(gate_up_grad, [(array, 0) for array in (*rows_other, *rows_own)], line)

    def mixed_back(sides, output_full):
        parts = [lax.dot_general(part, output_full, across, preferred_element_type=f32).astype(bf16) for part in sides]
        return jnp.concatenate(parts, axis=0)

    if count == 8:
        def first_stage(parts, activated, cotangent_sides):
            arrived = swap(parts[2], 1, "mp")
            other_pair = pair_sum(parts[0], arrived, "mp")
            near, far = send_links(for_links(other_pair), "mp")
            own_pair = pair_sum(parts[1], swap(tie(parts[3], arrived), 1, "mp"), "mp")
            own_sent = for_links(own_pair)
            down_sent = down_product((hold(activated[0], other_pair), activated[1]), cotangent_sides)
            return other_pair, near, far, own_pair, own_sent, down_sent

        other_pair, other_near, other_far, own_pair, own_sent, down_sent = island(
            first_stage, normed_parts, activated, cotangent_sides
        )
        down_parts = exchange(down_sent, "dp")

        def second_stage(
            other_pair, other_near, other_far, own_pair, own_sent, gate_up_grad, rows_other, rows_own, parts
        ):
            last = send_last(other_pair, other_near, other_far, "mp")
            near, far = send_links(own_sent, "mp")
            normed_other = total_of(other_pair, other_near, other_far, *last).astype(bf16)
            normed_back = swap(normed_other, 1, "dp")
            units = (hold(gate_up_grad[0], normed_other), gate_up_grad[1])
            gate_sent = gate_product(units, rows_other, rows_own)
            near, far = hold(near, gate_sent), hold(far, gate_sent)
            own_last = send_last(own_pair, near, far, "mp")
            arrived = [swap(tie(parts[k + 2], last), 1, "mp") for k in range(2)]
            feed_pair = pair_links(hold(parts[0], near), arrived[0])
            return normed_back, (own_pair, near, far, *own_last), gate_sent, feed_pair, arrived[1]

        normed_back, own_pieces, gate_sent, feed_pair, feed_arrived = island(
            second_stage,
            hold(other_pair, down_sent),
            other_near,
            other_far,
            own_pair,
            own_sent,
            gate_up_grad,
            rows_other,
            rows_own,
            feed_parts,
        )
        gate_sent = hold(gate_sent, down_parts)

        def attention_rows(normed_back, pieces, hidden, cotangent, params, output_full):
            hidden_grad, hidden_grad_low, gain_grad, offset_grad = norm_back(
                hidden, pieces, cotangent, params[2], normed_back
            )
            sides = gather_rows(hidden_grad_low, "mp")
            return hidden_grad, gain_grad, offset_grad, jnp.concatenate(sides, axis=0), mixed_back(sides, output_full)

        hidden_grad, gain_two_grad, offset_two_grad, attention_full, mixed_grad = island(
            attention_rows, hold(normed_back, gate_sent), own_pieces, hidden, cotangent, vector_params, output_full
        )
    else:
        normed_back = swap(sum_pieces(normed_parts[0], normed_parts[2], "mp")[0].astype(bf16), 1, "dp")
        own_pieces = sum_pieces(normed_parts[1], normed_parts[3], "mp")
        down_parts = exchange(down_product(activated, cotangent_sides), "dp")
        gate_sent = hold(gate_product(gate_up_grad, rows_other, rows_own), down_parts)
        hidden_grad, hidden_grad_low, gain_two_grad, offset_two_grad = norm_back(
            hidden, own_pieces, cotangent, vector_params[2], normed_back
        )
        attention_sides = gather_rows(hidden_grad_low, "mp")
        attention_full, mixed_grad = jnp.concatenate(attention_sides, axis=0), mixed_back(attention_sides, output_full)
    gate_parts = exchange(gate_sent, "dp")
    def attention_back(mixed_grad, queries, keys, values, logsum, tables, row_segments, other_sent):
        links = send_links(other_sent, "mp") if count == 8 else ()
        results = attend_back(rank, count, queries, keys, values, mixed_grad, logsum, tables, row_segments)
        return *results, links

    raw_grad, bias_grad, other_links = island(
        attention_back,
        mixed_grad,
        queries,
        keys,
        values,
        logsum,
        tables,
        row_segments,
        feed_pair[1:] if count == 8 else (),
    )
    heads_sent = hold(heads_grad(normed_one, raw_grad, attention_full, mixed_rows), gate_parts)
    heads_total = lax.psum_scatter(heads_sent, "dp", scatter_dimension=1, tiled=True)
    stages = (("dp", line, 1), ("mp", count // 2, 2), ("mp", 2, 1))

    def last_sums(raw_grad, triple_full, feed, inputs, hidden, hidden_grad, params):
        parts = [
            jnp.dot(part, triple_full, preferred_element_type=f32)
            for part in (raw_grad[:side], raw_grad[side:])
        ]
        input_grad, _, gain_grad, offset_grad = norm_back(inputs, sum_pieces(*parts, "mp"), hidden_grad, params[0])
        if count == 8:
            other_pair, links, mine, arrived = feed
            own_pair, *sent = pair_links(mine, arrived)
            other_sum = total_of(other_pair, *links, *send_last(other_pair, *links, "mp"))
            links = send_links(sent, "mp")
            own_sum = total_of(own_pair, *links, *send_last(own_pair, *links, "mp"))
        else:
            other_sum, own_sum = [sum_pieces(feed[k], feed[k + 2], "mp")[0] for k in range(2)]
        return input_grad, gain_grad, offset_grad, hidden + own_sum, other_sum.astype(bf16)

    input_grad, gain_one_grad, offset_one_grad, own_output, feed_other = island(
        last_sums,
        hold(raw_grad, heads_sent),
        triple_full,
        (feed_pair[0], other_links, feed_parts[1], feed_arrived) if count == 8 else feed_parts,
        inputs,
        hidden,
        hidden_grad,
        vector_params,
    )
    heads_total = hold(heads_total, input_grad)
    feed_back = swap(feed_other, 1, "dp")

    gate_grads = gate_parts.reshape(-1, 2, 2 * half, slab)
    down_grads = down_parts.reshape(-1, 2, half, slab)

    def squares_of(parts):
        return jnp.sum(jnp.square(jnp.sum(parts.astype(f32), axis=0)))

    local_squares = squares_of(gate_grads) + squares_of(down_grads) + squares_of(heads_total[None])
    bias_full = lax.dynamic_update_slice_in_dim(
        jnp.zeros((3, width), f32), bias_grad.reshape(3, head_width), rank * head_width, 1
    )
    squares_row = jnp.broadcast_to(local_squares, (1, width))
    vector_part = jnp.concatenate(
        [gain_one_grad, offset_one_grad, gain_two_grad, offset_two_grad, bias_full, squares_row], axis=0
    )
    summed = sum_everywhere(vector_part, stages)
    vector_total = summed[:7]
    square_total = summed[7, 0] + jnp.sum(vector_total * vector_total)
    grad_norm = jnp.sqrt(square_total)
    factor = jnp.minimum(1.0, clip_limit / (grad_norm + 1e-06))
    gate_results, down_results, triple_results, output_results = adam(
        factor,
        [
            (
                [array.swapaxes(1, 2).reshape(4, half, slab) for array in (gate_weight, gate_moment, gate_square)],
                gate_grads,
                lambda i: (0, i % 2, i // 2, 0),
                matrix_rate,
                False,
            ),
            (
                [array.reshape(2, half, slab) for array in (down_weight, down_moment, down_square)],
                down_grads,
                lambda i: (0, i, 0, 0),
                matrix_rate,
                False,
            ),
            (
                [triple_weight, triple_moment, triple_square],
                heads_total[None],
                lambda i: (0, i, 0),
                matrix_rate,
                True,
            ),
            (
                [array[None] for array in (output_weight, output_moment, output_square)],
                heads_total[None],
                lambda i: (0, 3, 0),
                output_rate,
                False,
            ),
        ],
    )
    results = [
        triple_results,
        tuple(array[0] for array in output_results),
        tuple(array.reshape(2, 2 * half, slab).swapaxes(1, 2) for array in gate_results),
        tuple(array.reshape(2 * half, slab) for array in down_results),
        adam_step(vector_params, vector_moment, vector_square, vector_total, factor, vector_rate, 0.0),
    ]
    block_output = (own_output + hold(feed_back, gate_results[0]).astype(f32)).astype(bf16)
    return (
        (block_output, input_grad, grad_norm)
        + tuple(result[0] for result in results)
        + tuple(result[1] for result in results)
        + tuple(result[2] for result in results)
        + (vector_total[4],)
    )


def solution(mesh):
    in_specs = (
        P(("dp", "mp"), None),
        P("dp", None),
        P(("dp", "mp"), None),
        P(None, "dp", "mp"),
        P("mp", "dp"),
        P(None, "dp", "mp"),
        P("mp", "dp"),
        P(),
        P(None, "dp", "mp"),
        P("mp", "dp"),
        P(None, "dp", "mp"),
        P("mp", "dp"),
        P(),
        P(None, "dp", "mp"),
        P("mp", "dp"),
        P(None, "dp", "mp"),
        P("mp", "dp"),
        P(),
    )
    out_specs = (
        P(("dp", "mp"), None),
        P(("dp", "mp"), None),
        P(),
        P(None, "dp", "mp"),
        P("mp", "dp"),
        P(None, "dp", "mp"),
        P("mp", "dp"),
        P(),
        P(None, "dp", "mp"),
        P("mp", "dp"),
        P(None, "dp", "mp"),
        P("mp", "dp"),
        P(),
        P(None, "dp", "mp"),
        P("mp", "dp"),
        P(None, "dp", "mp"),
        P("mp", "dp"),
        P(),
        P(),
    )
    return jax.shard_map(
        per_device, mesh=mesh, in_specs=in_specs, out_specs=out_specs, check_vma=False
    )
```
